32 devices in a mesh: seq: 16 (over z, y, core), head: 2 (over x).
Axes of the slice: x: 2, y: 2, z: 4, core: 2. Of those that a mesh axis runs over, the one named last changes fastest.
Arguments:
- inputs: bfloat16 [2, 2048, 1024], P(None, 'seq'), may hold values from -6 to 6
- encoded: bfloat16 [2, 6144, 1024], P(None, 'seq'), may hold values from -6 to 6
- tgt_bounds: int32 [2, 3], replicated, may hold values from 1 to 2048, as said below
- src_bounds: int32 [2, 3], replicated, may hold values from 1 to 6144, as said below
- self_query: bfloat16 [1024, 1024], P(None, 'head'), may hold values from -0.1875 to 0.1875
- self_key: bfloat16 [1024, 1024], P(None, 'head'), may hold values from -0.1875 to 0.1875
- self_value: bfloat16 [1024, 1024], P(None, 'head'), may hold values from -0.1875 to 0.1875
- self_out: bfloat16 [1024, 1024], P('head'), may hold values from -1.5 to 1.5
- cross_query: bfloat16 [1024, 1024], P(None, 'head'), may hold values from -0.1875 to 0.1875
- cross_key: bfloat16 [1024, 1024], P(None, 'head'), may hold values from -0.1875 to 0.1875
- cross_value: bfloat16 [1024, 1024], P(None, 'head'), may hold values from -0.1875 to 0.1875
- cross_out: bfloat16 [1024, 1024], P('head'), may hold values from -2.5 to 2.5
- ffn_in: bfloat16 [1024, 4096], P(None, 'head'), may hold values from -0.1875 to 0.1875
- ffn_out: bfloat16 [4096, 1024], P('head'), may hold values from -0.09375 to 0.09375
- adapter_down: bfloat16 [1024, 512], P(None, 'head'), may hold values from -0.1875 to 0.1875
- adapter_up: bfloat16 [512, 1024], P('head'), may hold values from -0.0625 to 0.0625
- norm1_gain: float32 [1024], replicated, may hold values from 0.25 to 1.75
- norm1_bias: float32 [1024], replicated, may hold values from -3 to 3
- norm2_gain: float32 [1024], replicated, may hold values from 0.25 to 1.75
- norm2_bias: float32 [1024], replicated, may hold values from -3 to 3
- norm3_gain: float32 [1024], replicated, may hold values from 0.25 to 1.75
- norm3_bias: float32 [1024], replicated, may hold values from -3 to 3
- cotangent: bfloat16 [2, 2048, 1024], P(None, 'seq'), may hold values from -6 to 6
Outputs:
- output: float32 [2, 2048, 1024], P(None, 'seq')
- grad_inputs: float32 [2, 2048, 1024], P(None, 'seq')
- grad_encoded: float32 [2, 6144, 1024], P(None, 'seq')
- grad_self_query: float32 [1024, 1024], P('seq', 'head')
- grad_self_key: float32 [1024, 1024], P('seq', 'head')
- grad_self_value: float32 [1024, 1024], P('seq', 'head')
- grad_self_out: float32 [1024, 1024], P('head', 'seq')
- grad_cross_query: float32 [1024, 1024], P('seq', 'head')
- grad_cross_key: float32 [1024, 1024], P('seq', 'head')
- grad_cross_value: float32 [1024, 1024], P('seq', 'head')
- grad_cross_out: float32 [1024, 1024], P('head', 'seq')
- grad_adapter_down: float32 [1024, 512], P(None, 'head')
- grad_adapter_up: float32 [512, 1024], P('head')
- grad_norm1_gain: float32 [1024], replicated
- grad_norm1_bias: float32 [1024], replicated
- grad_norm2_gain: float32 [1024], replicated
- grad_norm2_bias: float32 [1024], replicated
- grad_norm3_gain: float32 [1024], replicated
- grad_norm3_bias: float32 [1024], replicated
The draws below stay inside these ranges and needn't reach their ends.
Inputs may be any that keep to these rules, and one draw needn't show every extreme that they name: `tgt_bounds`: each row is non-decreasing. In one packed sequence, chosen anew with each draw and the same one as in src_bounds, the first entry lies within the first 128 positions, the second within the last 128, and every further entry equals 2048, so that the sequence holds three documents; in every other sequence entry k (counted from 1) lies within 128 of 4 * k * 128. `src_bounds`: each row is non-decreasing. In the packed sequence chosen for tgt_bounds, the first entry lies within the first 384 positions, the second within the last 384, and every further entry equals 6144; in every other sequence entry k (counted from 1) lies within 384 of 4 * k * 384.
All inputs are finite; a program needn't handle non-finite values.
Results may differ from the reference program's by a relative error of at most 0.04.
Values may be sent and summed in bfloat16 or wider, within the bound.
No kernel may reach another device: no remote copies, remote signals or barrier semaphores. Data moves between devices by JAX's collectives and lax.ppermute only.
A program may use at most 320 MiB of HBM per device.

```python
import jax
import jax.numpy as jnp
from jax import lax

D = 1024
HEADS = 16
HEAD_DIM = 64
FF = 4096
AD = 512
PACKS = 2
TOK_DEV = 128
SRC_DEV = 384
TGT_LEN = 2048
SRC_LEN = 6144
STARTS = 3


def long_pack(key):
    return jax.random.randint(jax.random.fold_in(key, 5), (), 0, PACKS)


def pack_starts(key, chosen_pack, per_device, length):
    steps = jnp.arange(1, STARTS + 1, dtype=jnp.int32)
    jitter = jax.random.randint(jax.random.fold_in(key, 1), (PACKS, STARTS), -per_device, per_device + 1)
    regular = steps[None, :] * (4 * per_device) + jitter
    first = jax.random.randint(jax.random.fold_in(key, 2), (PACKS, 1), 1, per_device)
    last = jax.random.randint(jax.random.fold_in(key, 3), (PACKS, 1), length - per_device + 1, length)
    filler = jnp.full((PACKS, STARTS - 2), length, dtype=jnp.int32)
    spanning = jnp.concatenate([first, last, filler], axis=1)
    picked = (jnp.arange(PACKS, dtype=jnp.int32) == chosen_pack)[:, None]
    return jnp.where(picked, spanning, regular).astype(jnp.int32)


def draw_tgt_bounds(key, part):
    chosen_pack = long_pack(key)
    key = jax.random.fold_in(key, 11)
    return pack_starts(key, chosen_pack, TOK_DEV, TGT_LEN)


def draw_src_bounds(key, part):
    chosen_pack = long_pack(key)
    key = jax.random.fold_in(key, 12)
    return pack_starts(key, chosen_pack, SRC_DEV, SRC_LEN)


def block_levels(own_key, extent, split, least, high):
    def one(axis_at, parts):
        heights = jax.random.uniform(jax.random.fold_in(jax.random.fold_in(own_key, 6), axis_at), (parts,), jnp.float32, least / len(split), high / len(split))
        return jnp.repeat(jnp.exp(heights), extent[axis_at] // parts).reshape((-1,) + (1,) * (len(extent) - axis_at - 1))

    level = one(*split[0])
    for cut in split[1:]:
        level = level * one(*cut)
    return level


def normal_values(own_key, extent, scale, bound, shards=(), kind=jnp.bfloat16):
    drawn = scale * jax.random.normal(own_key, extent, jnp.float32)
    if shards:
        drawn = drawn * block_levels(own_key, extent, shards, -0.22, 0.18)
    return jnp.clip(drawn, -bound, bound).astype(kind)


def setup_inputs(seed: int = 0) -> dict:
    keys = jax.random.split(jax.random.key(seed), 24)
    return {
        "inputs": normal_values(keys[0], (PACKS, TGT_LEN, D), 1.0, 6.0, ((1, 16),)),
        "encoded": normal_values(keys[1], (PACKS, SRC_LEN, D), 1.0, 6.0, ((1, 16),)),
        "tgt_bounds": draw_tgt_bounds(jax.random.fold_in(keys[23], 71), 0),
        "src_bounds": draw_src_bounds(jax.random.fold_in(keys[23], 71), 0),
        "self_query": normal_values(keys[4], (D, D), D ** -0.5, 0.1875, ((1, 2),)),
        "self_key": normal_values(keys[5], (D, D), D ** -0.5, 0.1875, ((1, 2),)),
        "self_value": normal_values(keys[6], (D, D), D ** -0.5, 0.1875, ((1, 2),)),
        "self_out": normal_values(keys[7], (D, D), (max(4, 32 * D // TGT_LEN)) ** -0.5, 1.5, ((0, 2),)),
        "cross_query": normal_values(keys[8], (D, D), D ** -0.5, 0.1875, ((1, 2),)),
        "cross_key": normal_values(keys[9], (D, D), D ** -0.5, 0.1875, ((1, 2),)),
        "cross_value": normal_values(keys[10], (D, D), D ** -0.5, 0.1875, ((1, 2),)),
        "cross_out": normal_values(keys[11], (D, D), (max(4, 32 * D // SRC_LEN)) ** -0.5, 2.5, ((0, 2),)),
        "ffn_in": normal_values(keys[12], (D, FF), D ** -0.5, 0.1875, ((1, 2),)),
        "ffn_out": normal_values(keys[13], (FF, D), FF ** -0.5, 0.09375, ((0, 2),)),
        "adapter_down": normal_values(keys[14], (D, AD), D ** -0.5, 0.1875, ((1, 2),)),
        "adapter_up": normal_values(keys[15], (AD, D), (16 * AD) ** -0.5, 0.0625, ((0, 2),)),
        "norm1_gain": jnp.clip(1.0 + 0.15 * jax.random.normal(keys[16], (D,), jnp.float32), 0.25, 1.75),
        "norm1_bias": normal_values(keys[17], (D,), 0.5, 3.0, (), jnp.float32),
        "norm2_gain": jnp.clip(1.0 + 0.15 * jax.random.normal(keys[18], (D,), jnp.float32), 0.25, 1.75),
        "norm2_bias": normal_values(keys[19], (D,), 0.5, 3.0, (), jnp.float32),
        "norm3_gain": jnp.clip(1.0 + 0.15 * jax.random.normal(keys[20], (D,), jnp.float32), 0.25, 1.75),
        "norm3_bias": normal_values(keys[21], (D,), 0.5, 3.0, (), jnp.float32),
        "cotangent": normal_values(keys[22], (PACKS, TGT_LEN, D), 1.0, 6.0, ((1, 16),)),
    }


@jax.custom_vjp
def low(v):
    return lax.optimization_barrier(v.astype(jnp.bfloat16)).astype(jnp.float32)

@jax.custom_vjp
def low_back(v):
    return v

def low_keep(v):
    return (low(v), None)

def low_pass(kept, grad):
    return (grad,)

def back_keep(v):
    return (v, None)

def back_low(kept, grad):
    return (low(grad),)
low.defvjp(low_keep, low_pass)
low_back.defvjp(back_keep, back_low)

def matrix_product(left, right):
    return jnp.dot(left, right, precision=lax.Precision.HIGHEST, preferred_element_type=jnp.float32)

def norm_rows(values, norm_gain, norm_bias):
    average = lax.optimization_barrier(jnp.mean(values, axis=-1, keepdims=True))
    centred = values - average
    spread = lax.optimization_barrier(jnp.mean(centred * centred, axis=-1, keepdims=True))
    return centred * lax.rsqrt(spread + 1e-05) * norm_gain + norm_bias

def doc_ids(row_count, bounds):
    places = jnp.arange(row_count, dtype=jnp.int32)
    return lax.optimization_barrier(jnp.sum((places[None, :, None] >= bounds[:, None, :]).astype(jnp.int32), axis=2))

def attend(queries, key_rows, value_rows, query_docs, key_docs, causal):
    row_count = queries.shape[0]
    block_rows = min(512, row_count)
    blocks = row_count // block_rows
    scaling = HEAD_DIM ** (-0.5)
    key_places = jnp.arange(key_rows.shape[0], dtype=jnp.int32)
    key_heads = key_rows.reshape(key_rows.shape[0], HEADS, HEAD_DIM)
    value_heads = value_rows.reshape(value_rows.shape[0], HEADS, HEAD_DIM)
    query_blocks = queries.reshape(blocks, block_rows, HEADS, HEAD_DIM)
    place_blocks = jnp.arange(row_count, dtype=jnp.int32).reshape(blocks, block_rows)
    doc_blocks = query_docs.reshape(blocks, block_rows)

    def one_block(pieces):
        query_block, place_block, doc_block = pieces
        raw_scores = jnp.einsum('qhd,khd->hqk', query_block, key_heads, precision=lax.Precision.HIGHEST) * scaling
        scores = low_back(raw_scores)
        allowed = doc_block[:, None] == key_docs[None, :]
        if causal:
            allowed = jnp.logical_and(allowed, place_block[:, None] >= key_places[None, :])
        scores = jnp.where(allowed[None], scores, -1e+30)
        highest = lax.optimization_barrier(jnp.max(scores, axis=-1, keepdims=True))
        weights = jnp.exp(scores - highest)
        probabilities = weights / lax.optimization_barrier(jnp.sum(weights, axis=-1, keepdims=True))
        return jnp.einsum('hqk,khd->qhd', low(probabilities), value_heads, precision=lax.Precision.HIGHEST)
    blocks_out = lax.map(jax.checkpoint(one_block), (query_blocks, place_blocks, doc_blocks))
    return blocks_out.reshape(row_count, HEADS * HEAD_DIM)

def reference(inputs, encoded, tgt_bounds, src_bounds, self_query, self_key, self_value, self_out, cross_query, cross_key, cross_value, cross_out, ffn_in, ffn_out, adapter_down, adapter_up, norm1_gain, norm1_bias, norm2_gain, norm2_bias, norm3_gain, norm3_bias, cotangent):
    target_docs = doc_ids(TGT_LEN, tgt_bounds)
    source_docs = doc_ids(SRC_LEN, src_bounds)
    weight_in = ffn_in.astype(jnp.float32)
    weight_out = ffn_out.astype(jnp.float32)

    def attend_all(queries, key_rows, value_rows, key_docs, causal):
        return jnp.stack([attend(queries[index], key_rows[index], value_rows[index], target_docs[index], key_docs[index], causal) for index in range(PACKS)])

    def forward_pass(token_input, source_input, self_query_weight, self_key_weight, self_value_weight, self_output_weight, cross_query_weight, cross_key_weight, cross_value_weight, cross_output_weight, down_weight, up_weight, first_norm_gain, first_norm_bias, second_norm_gain, second_norm_bias, third_norm_gain, third_norm_bias):
        query_one = low_back(low(matrix_product(token_input, self_query_weight)))
        key_one = low_back(low(matrix_product(token_input, self_key_weight)))
        value_one = low_back(low(matrix_product(token_input, self_value_weight)))
        attended_one = attend_all(query_one, key_one, value_one, target_docs, True)
        out_one = low_back(matrix_product(low_back(low(attended_one)), self_output_weight))
        normed_one = norm_rows(token_input + out_one, first_norm_gain, first_norm_bias)
        normed_one_low = low(normed_one)
        query_two = low_back(low(matrix_product(normed_one_low, cross_query_weight)))
        key_two = low_back(low(matrix_product(source_input, cross_key_weight)))
        value_two = low_back(low(matrix_product(source_input, cross_value_weight)))
        attended_two = attend_all(query_two, key_two, value_two, source_docs, False)
        out_two = low_back(matrix_product(low_back(low(attended_two)), cross_output_weight))
        normed_two = norm_rows(normed_one + out_two, second_norm_gain, second_norm_bias)
        normed_two_low = low(normed_two)
        hidden = low_back(matrix_product(normed_two_low, weight_in))
        activated = low(jax.nn.gelu(hidden))
        narrow = low_back(matrix_product(normed_two_low, down_weight))
        narrow_act = low(jax.nn.gelu(narrow))
        branch = low_back(matrix_product(activated, weight_out) + 4.0 * matrix_product(narrow_act, up_weight))
        return norm_rows(normed_two + branch, third_norm_gain, third_norm_bias)
    primals = tuple((entry.astype(jnp.float32) for entry in (inputs, encoded, self_query, self_key, self_value, self_out, cross_query, cross_key, cross_value, cross_out, adapter_down, adapter_up, norm1_gain, norm1_bias, norm2_gain, norm2_bias, norm3_gain, norm3_bias)))
    result, pullback = jax.vjp(forward_pass, *primals)
    gradients = pullback(cotangent.astype(jnp.float32))
    return (result, gradients[0], gradients[1], gradients[2], gradients[3], gradients[4], gradients[5], gradients[6], gradients[7], gradients[8], gradients[9], gradients[10], gradients[11], gradients[12], gradients[13], gradients[14], gradients[15], gradients[16], gradients[17])
```

```python
import functools

import jax
import jax.numpy as jnp
from jax import lax
from jax.experimental import pallas as pl
from jax.experimental.pallas import tpu as pltpu
from jax.sharding import PartitionSpec as P

HEAD_DIM = 64
PAIR = 2 * HEAD_DIM
STATS = 16
LOWEST = -1e29
EXCLUDED = -1e30
F32 = jnp.float32
BF16 = jnp.bfloat16


def matrix_product(left, right):
    return jnp.dot(left, right, preferred_element_type=F32)


def contract(left, right, left_dim, right_dim):
    return lax.dot_general(
        left, right, (((left_dim,), (right_dim,)), ((), ())), preferred_element_type=F32
    )


def times_transposed(left, right):
    return contract(left, right, 1, 1)


def transposed_times(left, right):
    return contract(left, right, 0, 0)


def norm_rows(values, norm_gain, norm_bias):
    average = jnp.mean(values, axis=-1, keepdims=True)
    centred = values - average
    spread = jnp.mean(centred * centred, axis=-1, keepdims=True)
    return centred * lax.rsqrt(spread + 1e-05) * norm_gain + norm_bias


class Shape:
    def __init__(self, chips, groups, packs, rows, source_rows, starts, causal):
        self.chips, self.groups, self.packs, self.rows = chips, groups, packs, rows
        self.source_rows, self.starts, self.causal = source_rows, starts, causal
        self.step = groups
        while self.step > 1 and self.step * source_rows > 768:
            self.step //= 2
        self.steps = groups // self.step
        self.tile = 2 * rows
        self.length = 2 * chips * rows
        self.source_length = 2 * chips * source_rows


def position_range(shape, places, pack, target_bounds, source_bounds):
    starts = shape.starts
    low = jnp.zeros_like(places)
    high = jnp.zeros_like(places) + source_bounds[pack * starts]
    for entry in range(starts):
        later = places >= target_bounds[pack * starts + entry]
        low = jnp.where(later, source_bounds[pack * starts + entry], low)
        if entry + 1 < starts:
            following = source_bounds[pack * starts + entry + 1]
        else:
            following = jnp.int32(shape.source_length)
        high = jnp.where(later, following, high)
    if shape.causal:
        high = places + 1
    return low, high


def lane_places(shape, chip, core):
    lanes = lax.broadcasted_iota(jnp.int32, (1, shape.tile), 1)
    own = (2 * chip + core) * shape.rows + lanes
    other = (2 * chip + 1 - core) * shape.rows + lanes - shape.rows
    return jnp.where(lanes < shape.rows, own, other)


def step_conditions(shape, chip, pack, first_group, place, target_bounds, source_bounds):
    base, core = place[0], place[1]
    head = chip * (2 * shape.rows)
    tail = head + 2 * shape.rows - 1
    low_first, high_first = position_range(shape, head, pack, target_bounds, source_bounds)
    low_last, high_last = position_range(shape, tail, pack, target_bounds, source_bounds)
    begin = (base + 2 * first_group + core) * shape.source_rows
    end = begin + (2 * shape.step - 1) * shape.source_rows
    some = jnp.logical_and(low_first < end, high_last > begin)
    whole = jnp.logical_and(low_last <= begin, high_first >= end)
    return begin, some, whole


def source_places(shape, begin):
    size = shape.step * shape.source_rows
    rows = lax.broadcasted_iota(jnp.int32, (size, shape.tile), 0)
    places = begin + rows
    for group in range(1, shape.step):
        places = places + jnp.where(rows >= group * shape.source_rows, shape.source_rows, 0)
    return places


def both(own_ref, other_ref, chip, first, last, pack, rows):
    lanes = slice(pack * rows, (pack + 1) * rows)
    return jnp.concatenate(
        [own_ref[chip, first:last, lanes], other_ref[chip, first:last, lanes]], axis=1
    )


def one_head(pair_rows, head):
    feature = lax.broadcasted_iota(jnp.int32, pair_rows.shape, 0)
    mine = (feature >= HEAD_DIM) if head else (feature < HEAD_DIM)
    return jnp.where(mine, pair_rows, jnp.zeros_like(pair_rows))


def split_low(value):
    high = value.astype(BF16).astype(F32)
    return high, value - high


def split_parts(value):
    high = lax.reduce_precision(value, 8, 7)
    return high, value - high


def stat_rows(rows, width):
    index = lax.broadcasted_iota(jnp.int32, (STATS, width), 0)
    total = jnp.zeros((STATS, width), F32)
    for number, row in enumerate(rows):
        total = jnp.where(index == number, row, total)
    return total.astype(BF16)


def forward_kernel(
    shape, target_bounds, source_bounds, place, own_q, other_q, keys_values, own_out, other_out,
    value_t, maxima, sums, total,
):
    step_rows = shape.step * shape.source_rows
    for group in range(shape.groups):
        for pack in range(shape.packs):
            part = slice(pack * shape.source_rows, (pack + 1) * shape.source_rows)
            value_t[pack, :, group * shape.source_rows : (group + 1) * shape.source_rows] = (
                keys_values[group, 1, part, :].T
            )

    for pack in range(shape.packs):
        part = slice(pack * shape.source_rows, (pack + 1) * shape.source_rows)

        def per_chip(chip, unused, pack=pack, part=part):
            query = both(own_q, other_q, chip, 0, PAIR, pack, shape.rows)
            low, high = position_range(
                shape, lane_places(shape, chip, place[1]), pack, target_bounds, source_bounds
            )
            maxima[...] = jnp.full_like(maxima, LOWEST)
            sums[...] = jnp.zeros_like(sums)
            total[...] = jnp.zeros_like(total)
            for step in range(shape.steps):
                groups = slice(step * shape.step, (step + 1) * shape.step)
                begin, some, whole = step_conditions(
                    shape, chip, pack, step * shape.step, place, target_bounds, source_bounds
                )

                def fold(masked, step=step, groups=groups, begin=begin):
                    key_rows = keys_values[groups, 0, part, :].reshape(step_rows, PAIR)
                    if masked:
                        places = source_places(shape, begin)
                        allowed = jnp.logical_and(places >= low, places < high)
                    for head in range(2):
                        features = slice(head * HEAD_DIM, (head + 1) * HEAD_DIM)
                        scores = matrix_product(key_rows, one_head(query, head))
                        if masked:
                            scores = jnp.where(allowed, scores, EXCLUDED)
                        before = maxima[head : head + 1, :]
                        now = jnp.maximum(before, jnp.max(scores, axis=0, keepdims=True))
                        weights = jnp.exp(scores - now)
                        fading = jnp.exp(before - now)
                        maxima[head : head + 1, :] = now
                        sums[head : head + 1, :] = sums[head : head + 1, :] * fading + jnp.sum(
                            weights, axis=0, keepdims=True
                        )
                        values = value_t[pack, features, step * step_rows : (step + 1) * step_rows]
                        total[features, :] = total[features, :] * fading + matrix_product(
                            values, weights.astype(BF16)
                        )

                pl.when(jnp.logical_and(some, whole))(functools.partial(fold, False))
                pl.when(jnp.logical_and(some, jnp.logical_not(whole)))(
                    functools.partial(fold, True)
                )
            statistics = []
            for head in range(2):
                features = slice(head * HEAD_DIM, (head + 1) * HEAD_DIM)
                divisor = jnp.maximum(sums[head : head + 1, :], 1e-37)
                filled = sums[head : head + 1, :] > 0.0
                logs = jnp.where(filled, maxima[head : head + 1, :] + jnp.log(divisor), LOWEST)
                statistics.extend(split_low(logs))
                result = (total[features, :] / divisor).astype(BF16)
                for ref, offset in ((own_out, 0), (other_out, shape.rows)):
                    ref[chip, features, pack * shape.rows : (pack + 1) * shape.rows] = result[
                        :, offset : offset + shape.rows
                    ]
            statistics = stat_rows(statistics, shape.tile)
            for ref, offset in ((own_out, 0), (other_out, shape.rows)):
                ref[chip, PAIR : PAIR + STATS, pack * shape.rows : (pack + 1) * shape.rows] = (
                    statistics[:, offset : offset + shape.rows]
                )
            return 0

        lax.fori_loop(0, shape.chips, per_chip, 0)


def backward_kernel(
    shape, target_bounds, source_bounds, place, own_q, other_q, own_g, other_g, keys_values,
    own_dq, other_dq, key_grads, key_t, grad_key, grad_value, grad_query,
):
    step_rows = shape.step * shape.source_rows
    grad_key[...] = jnp.zeros_like(grad_key)
    grad_value[...] = jnp.zeros_like(grad_value)
    for group in range(shape.groups):
        for pack in range(shape.packs):
            part = slice(pack * shape.source_rows, (pack + 1) * shape.source_rows)
            key_t[pack, :, group * shape.source_rows : (group + 1) * shape.source_rows] = (
                keys_values[group, 0, part, :].T
            )

    for pack in range(shape.packs):
        part = slice(pack * shape.source_rows, (pack + 1) * shape.source_rows)

        def per_chip(chip, unused, pack=pack, part=part):
            query = both(own_q, other_q, chip, 0, PAIR, pack, shape.rows)
            grads = both(own_g, other_g, chip, 0, PAIR, pack, shape.rows)
            statistics = both(own_g, other_g, chip, PAIR, PAIR + STATS, pack, shape.rows).astype(F32)
            low, high = position_range(
                shape, lane_places(shape, chip, place[1]), pack, target_bounds, source_bounds
            )
            grad_query[...] = jnp.zeros_like(grad_query)
            for step in range(shape.steps):
                groups = slice(step * shape.step, (step + 1) * shape.step)
                begin, some, whole = step_conditions(
                    shape, chip, pack, step * shape.step, place, target_bounds, source_bounds
                )

                def fold(masked, step=step, groups=groups, begin=begin):
                    key_rows = keys_values[groups, 0, part, :].reshape(step_rows, PAIR)
                    value_rows = keys_values[groups, 1, part, :].reshape(step_rows, PAIR)
                    if masked:
                        places = source_places(shape, begin)
                        allowed = jnp.logical_and(places >= low, places < high)
                    probs, diffs, queries, gradients = [], [], [], []
                    lanes = slice(step * step_rows, (step + 1) * step_rows)
                    for head in range(2):
                        features = slice(head * HEAD_DIM, (head + 1) * HEAD_DIM)
                        head_query, head_grad = one_head(query, head), one_head(grads, head)
                        logs = statistics[2 * head : 2 * head + 1] + statistics[2 * head + 1 : 2 * head + 2]
                        delta = statistics[2 * head + 4 : 2 * head + 5] + statistics[2 * head + 5 : 2 * head + 6]
                        scores = matrix_product(key_rows, head_query)
                        if masked:
                            scores = jnp.where(allowed, scores, EXCLUDED)
                        weights = jnp.exp(scores - logs)
                        change = matrix_product(value_rows, head_grad)
                        diff = (weights * (change - delta)).astype(BF16)
                        grad_query[features, :] += matrix_product(key_t[pack, features, lanes], diff)
                        probs.append(weights.astype(BF16))
                        diffs.append(diff)
                        queries.append(head_query)
                        gradients.append(head_grad)
                    grad_key[pack, lanes, :] += times_transposed(
                        jnp.concatenate(diffs, axis=1), jnp.concatenate(queries, axis=1)
                    )
                    grad_value[pack, lanes, :] += times_transposed(
                        jnp.concatenate(probs, axis=1), jnp.concatenate(gradients, axis=1)
                    )

                pl.when(jnp.logical_and(some, whole))(functools.partial(fold, False))
                pl.when(jnp.logical_and(some, jnp.logical_not(whole)))(
                    functools.partial(fold, True)
                )
            result = (grad_query[...] * HEAD_DIM**-0.5).astype(BF16)
            for ref, offset in ((own_dq, 0), (other_dq, shape.rows)):
                ref[chip, :, pack * shape.rows : (pack + 1) * shape.rows] = result[
                    :, offset : offset + shape.rows
                ]
            return 0

        lax.fori_loop(0, shape.chips, per_chip, 0)

    for group in range(shape.groups):
        for pack in range(shape.packs):
            part = slice(pack * shape.source_rows, (pack + 1) * shape.source_rows)
            lanes = slice(group * shape.source_rows, (group + 1) * shape.source_rows)
            key_grads[group, 0, part, :] = grad_key[pack, lanes, :].astype(BF16)
            key_grads[group, 1, part, :] = grad_value[pack, lanes, :].astype(BF16)


def smem():
    return pl.BlockSpec(memory_space=pltpu.SMEM)


def vmem():
    return pl.BlockSpec(memory_space=pltpu.VMEM)


PARAMS = dict(vmem_limit_bytes=48 * 1024 * 1024)


def attention_forward(shape, bounds, place, own_q, other_q, keys_values):
    width = shape.packs * shape.rows
    pairs = shape.packs * shape.length * shape.groups * shape.source_rows
    message = jax.ShapeDtypeStruct((shape.chips, PAIR + STATS, width), BF16)
    return pl.pallas_call(
        functools.partial(forward_kernel, shape),
        out_shape=(message, message),
        in_specs=[smem()] * 3 + [vmem()] * 3,
        out_specs=(vmem(), vmem()),
        scratch_shapes=[
            pltpu.VMEM((shape.packs, PAIR, shape.groups * shape.source_rows), BF16),
            pltpu.VMEM((8, shape.tile), F32),
            pltpu.VMEM((8, shape.tile), F32),
            pltpu.VMEM((PAIR, shape.tile), F32),
        ],
        compiler_params=pltpu.CompilerParams(**PARAMS),
        cost_estimate=pl.CostEstimate(
            flops=8 * pairs * HEAD_DIM, bytes_accessed=6 * 1024 * 1024, transcendentals=2 * pairs
        ),
    )(bounds[0], bounds[1], place, own_q, other_q, keys_values)


def attention_backward(shape, bounds, place, own_q, other_q, own_g, other_g, keys_values):
    width = shape.packs * shape.rows
    pairs = shape.packs * shape.length * shape.groups * shape.source_rows
    source = shape.groups * shape.source_rows
    message = jax.ShapeDtypeStruct((shape.chips, PAIR, width), BF16)
    return pl.pallas_call(
        functools.partial(backward_kernel, shape),
        out_shape=(message, message, jax.ShapeDtypeStruct(keys_values.shape, BF16)),
        in_specs=[smem()] * 3 + [vmem()] * 5,
        out_specs=(vmem(), vmem(), vmem()),
        scratch_shapes=[
            pltpu.VMEM((shape.packs, PAIR, source), BF16),
            pltpu.VMEM((shape.packs, source, PAIR), F32),
            pltpu.VMEM((shape.packs, source, PAIR), F32),
            pltpu.VMEM((PAIR, shape.tile), F32),
        ],
        compiler_params=pltpu.CompilerParams(**PARAMS),
        cost_estimate=pl.CostEstimate(
            flops=20 * pairs * HEAD_DIM, bytes_accessed=8 * 1024 * 1024, transcendentals=2 * pairs
        ),
    )(bounds[0], bounds[1], place, own_q, other_q, own_g, other_g, keys_values)


def on_device(
    seq_size,
    head_size,
    inputs,
    encoded,
    tgt_bounds,
    src_bounds,
    self_query,
    self_key,
    self_value,
    self_out,
    cross_query,
    cross_key,
    cross_value,
    cross_out,
    ffn_in,
    ffn_out,
    adapter_down,
    adapter_up,
    norm1_gain,
    norm1_bias,
    norm2_gain,
    norm2_bias,
    norm3_gain,
    norm3_bias,
    cotangent,
):
    pack_count, row_count, model_width = inputs.shape
    source_rows = encoded.shape[1]
    local_width = self_query.shape[1]
    pairs_here = local_width // PAIR
    chips = seq_size // 2
    copies = chips // pairs_here
    rows = pack_count * row_count
    starts = tgt_bounds.shape[1]
    position = lax.axis_index("seq")
    core = position % 2
    base = position // (2 * pairs_here) * (2 * pairs_here)
    place = jnp.stack([base, core]).astype(jnp.int32)
    self_bounds = (tgt_bounds.reshape(-1), tgt_bounds.reshape(-1))
    cross_bounds = (tgt_bounds.reshape(-1), src_bounds.reshape(-1))
    self_shape = Shape(chips, pairs_here, pack_count, row_count, row_count, starts, True)
    cross_shape = Shape(chips, pairs_here, pack_count, row_count, source_rows, starts, False)
    flat_inputs = inputs.reshape(rows, model_width)
    flat_encoded = encoded.reshape(pack_count * source_rows, model_width)

    all_chips = [[2 * chip + side for chip in range(chips)] for side in range(2)]
    near_chips = [
        [2 * (copy * pairs_here + pair) + side for pair in range(pairs_here)]
        for copy in range(copies)
        for side in range(2)
    ]

    def swap_core(value):
        return lax.ppermute(value, "seq", [(i, i ^ 1) for i in range(seq_size)])

    def to_all(value):
        return lax.all_to_all(value, "seq", 0, 0, axis_index_groups=all_chips, tiled=True)

    def to_near(value):
        if pairs_here == 1:
            return value
        return lax.all_to_all(value, "seq", 0, 0, axis_index_groups=near_chips, tiled=True)

    def head_sum(value):
        if head_size == 2:
            low = lax.reduce_precision(value, 8, 7)
            return low + lax.ppermute(low.astype(BF16), "head", [(0, 1), (1, 0)]).astype(F32)
        return lax.psum(value, "head")

    def spread_queries(features):
        message = features.reshape(pairs_here, -1, rows)
        own = to_all(jnp.tile(message, (copies, 1, 1)))
        return own, swap_core(own)

    def pair_rows(keys, values):
        def cut(value):
            return value.reshape(-1, pairs_here, PAIR).transpose(1, 0, 2)

        return jnp.stack([cut(keys), cut(values)], axis=1)

    def join_rows(message):
        return message.transpose(1, 2, 0, 3).reshape(2, -1, local_width)

    def logs_of(message):
        stats = message[:, PAIR : PAIR + 4, :].astype(F32)
        return stats[:, 0::2] + stats[:, 1::2]

    def weighted(parts, logs):
        highest = jnp.max(logs, axis=0)
        weights = jnp.exp(logs - highest)
        denominator = jnp.sum(weights, axis=0)
        shares = weights / denominator
        split = parts.reshape(parts.shape[:-2] + (2, HEAD_DIM, rows)).astype(F32)
        merged = jnp.sum(split * shares[:, :, :, None, :], axis=0)
        return merged, highest + jnp.log(denominator)

    def collect(own_part, other_part):
        met = swap_core(other_part)
        parts = jnp.stack([own_part, met])
        logs = jnp.stack([logs_of(own_part), logs_of(met)])
        merged, total = weighted(parts[:, :, :PAIR], logs)
        high, low = split_parts(total)
        statistics = jnp.stack([high, low], axis=2).reshape(chips, 4, rows)
        statistics = jnp.pad(statistics, ((0, 0), (0, STATS - 4), (0, 0)))
        message = jnp.concatenate(
            [merged.reshape(chips, PAIR, rows).astype(BF16), statistics.astype(BF16)], axis=1
        )
        back = to_all(message)
        logs = logs_of(back).reshape(copies, pairs_here, 2, rows)
        features = back[:, :PAIR].reshape(copies, pairs_here, PAIR, rows)
        merged, total = weighted(features, logs)
        return merged, total

    def spread_grads(grad_features, merged, total):
        split = grad_features.reshape(pairs_here, 2, HEAD_DIM, rows).astype(F32)
        delta = jnp.sum(split * merged, axis=2)
        statistics = jnp.concatenate(
            [
                jnp.stack(split_parts(total), axis=2).reshape(pairs_here, 4, rows),
                jnp.stack(split_parts(delta), axis=2).reshape(pairs_here, 4, rows),
                jnp.zeros((pairs_here, STATS - 8, rows), F32),
            ],
            axis=1,
        ).astype(BF16)
        message = jnp.concatenate([grad_features.reshape(pairs_here, PAIR, rows), statistics], axis=1)
        return spread_queries(message)

    def collect_query_grads(own_part, other_part):
        total = (own_part.astype(F32) + swap_core(other_part).astype(F32)).astype(BF16)
        back = to_all(total).reshape(copies, local_width, rows)
        return jnp.sum(back.astype(F32), axis=0).astype(BF16)

    scaling = HEAD_DIM**-0.5
    query_self = (contract(self_query, flat_inputs, 0, 1) * scaling).astype(BF16)
    key_self = matrix_product(flat_inputs, self_key).astype(BF16)
    value_self = matrix_product(flat_inputs, self_value).astype(BF16)
    self_q = spread_queries(query_self)
    self_kv = to_near(pair_rows(key_self, value_self))
    own_part, other_part = attention_forward(self_shape, self_bounds, place, *self_q, self_kv)
    attended_self, log_self = collect(own_part, other_part)
    mixed_self = attended_self.reshape(local_width, rows).astype(BF16)
    out_self = head_sum(transposed_times(mixed_self, self_out))
    normed_one, norm_one_back = jax.vjp(
        norm_rows, flat_inputs.astype(F32) + out_self, norm1_gain, norm1_bias
    )
    normed_one_low = normed_one.astype(BF16)
    query_cross = (contract(cross_query, normed_one_low, 0, 1) * scaling).astype(BF16)
    key_cross = matrix_product(flat_encoded, cross_key).astype(BF16)
    value_cross = matrix_product(flat_encoded, cross_value).astype(BF16)
    cross_kv = to_near(pair_rows(key_cross, value_cross))
    cross_q = spread_queries(query_cross)
    own_part, other_part = attention_forward(cross_shape, cross_bounds, place, *cross_q, cross_kv)
    attended_cross, log_cross = collect(own_part, other_part)
    mixed_cross = attended_cross.reshape(local_width, rows).astype(BF16)
    out_cross = head_sum(transposed_times(mixed_cross, cross_out))
    normed_two, norm_two_back = jax.vjp(norm_rows, normed_one + out_cross, norm2_gain, norm2_bias)
    normed_two_low = normed_two.astype(BF16)
    hidden = matrix_product(normed_two_low, ffn_in)
    activated, gelu_hidden_back = jax.vjp(jax.nn.gelu, hidden)
    activated_low = activated.astype(BF16)
    narrow = matrix_product(normed_two_low, adapter_down)
    narrow_act, gelu_narrow_back = jax.vjp(jax.nn.gelu, narrow)
    narrow_low = narrow_act.astype(BF16)
    branch_part = matrix_product(activated_low, ffn_out) + 4.0 * matrix_product(
        narrow_low, adapter_up
    )
    branch = head_sum(branch_part)
    normed_three, norm_three_back = jax.vjp(norm_rows, normed_two + branch, norm3_gain, norm3_bias)
    grad_third, grad_gain_three, grad_bias_three = norm_three_back(
        cotangent.reshape(rows, model_width).astype(F32)
    )
    grad_branch = grad_third.astype(BF16)
    grad_hidden = gelu_hidden_back(times_transposed(grad_branch, ffn_out))[0].astype(BF16)
    grad_narrow = gelu_narrow_back(4.0 * times_transposed(grad_branch, adapter_up))[0].astype(BF16)
    grad_adapter_up = 4.0 * transposed_times(narrow_low, grad_branch)
    grad_adapter_down_t = transposed_times(grad_narrow, normed_two_low)
    grad_two_part = times_transposed(grad_hidden, ffn_in) + times_transposed(
        grad_narrow, adapter_down
    )
    adapters = lax.psum(
        jnp.concatenate([grad_adapter_up, grad_adapter_down_t], axis=0).astype(BF16), "seq"
    ).astype(F32)
    grad_two = grad_third + head_sum(grad_two_part)
    grad_second, grad_gain_two, grad_bias_two = norm_two_back(grad_two)
    grad_second_low = grad_second.astype(BF16)
    grad_cross_out_t = contract(grad_second_low, mixed_cross, 0, 1)
    grad_mixed_cross = times_transposed(cross_out, grad_second_low).astype(BF16)
    cross_g = spread_grads(grad_mixed_cross, attended_cross, log_cross)
    own_part, other_part, cross_dkv = attention_backward(
        cross_shape, cross_bounds, place, *cross_q, *cross_g, cross_kv
    )
    grad_query_cross = collect_query_grads(own_part, other_part)
    grad_key_cross, grad_value_cross = join_rows(to_near(cross_dkv))
    grad_one_sum = head_sum(transposed_times(grad_query_cross, contract_t(cross_query)))
    grad_source = head_sum(
        times_transposed(grad_key_cross, cross_key) + times_transposed(grad_value_cross, cross_value)
    )
    grad_cross_query = contract(normed_one_low, grad_query_cross, 0, 1)
    grad_cross_key = transposed_times(flat_encoded, grad_key_cross)
    grad_cross_value = transposed_times(flat_encoded, grad_value_cross)
    grad_first, grad_gain_one, grad_bias_one = norm_one_back(grad_second + grad_one_sum)
    grad_first_low = grad_first.astype(BF16)
    grad_self_out_t = contract(grad_first_low, mixed_self, 0, 1)
    grad_mixed_self = times_transposed(self_out, grad_first_low).astype(BF16)
    self_g = spread_grads(grad_mixed_self, attended_self, log_self)
    own_part, other_part, self_dkv = attention_backward(
        self_shape, self_bounds, place, *self_q, *self_g, self_kv
    )
    grad_query_self = collect_query_grads(own_part, other_part)
    grad_key_self, grad_value_self = join_rows(to_near(self_dkv))
    grad_in_part = (
        transposed_times(grad_query_self, contract_t(self_query))
        + times_transposed(grad_key_self, self_key)
        + times_transposed(grad_value_self, self_value)
    )
    grad_inputs = grad_first + head_sum(grad_in_part)
    grad_self_query = contract(flat_inputs, grad_query_self, 0, 1)
    grad_self_key = transposed_times(flat_inputs, grad_key_self)
    grad_self_value = transposed_times(flat_inputs, grad_value_self)

    def scatter(parts):
        joined = jnp.concatenate([part.astype(BF16) for part in parts], axis=1)
        scattered = lax.psum_scatter(joined, "seq", scatter_dimension=0, tiled=True).astype(F32)
        return jnp.split(scattered, len(parts), axis=1)

    cross_out_t, cross_query_g, cross_key_g, cross_value_g = scatter(
        [grad_cross_out_t, grad_cross_query, grad_cross_key, grad_cross_value]
    )
    self_out_t, self_query_g, self_key_g, self_value_g = scatter(
        [grad_self_out_t, grad_self_query, grad_self_key, grad_self_value]
    )
    small = lax.psum(
        jnp.stack(
            [
                grad_gain_one,
                grad_bias_one,
                grad_gain_two,
                grad_bias_two,
                grad_gain_three,
                grad_bias_three,
            ]
        ),
        "seq",
    )
    half = adapter_up.shape[0]
    return (
        normed_three.reshape(pack_count, row_count, model_width),
        grad_inputs.reshape(pack_count, row_count, model_width),
        grad_source.reshape(pack_count, source_rows, model_width),
        self_query_g,
        self_key_g,
        self_value_g,
        self_out_t.T,
        cross_query_g,
        cross_key_g,
        cross_value_g,
        cross_out_t.T,
        adapters[half:].T,
        adapters[:half],
        small[0],
        small[1],
        small[2],
        small[3],
        small[4],
        small[5],
    )


def contract_t(weight):
    return weight.T


def solution(mesh):
    placed = (
        P(None, "seq", None),
        P(None, "seq", None),
        P(),
        P(),
        P(None, "head"),
        P(None, "head"),
        P(None, "head"),
        P("head", None),
        P(None, "head"),
        P(None, "head"),
        P(None, "head"),
        P("head", None),
        P(None, "head"),
        P("head", None),
        P(None, "head"),
        P("head", None),
        P(),
        P(),
        P(),
        P(),
        P(),
        P(),
        P(None, "seq", None),
    )
    return jax.shard_map(
        functools.partial(on_device, mesh.shape["seq"], mesh.shape["head"]),
        mesh=mesh,
        in_specs=placed,
        out_specs=(
            P(None, "seq", None),
            P(None, "seq", None),
            P(None, "seq", None),
            P("seq", "head"),
            P("seq", "head"),
            P("seq", "head"),
            P("head", "seq"),
            P("seq", "head"),
            P("seq", "head"),
            P("seq", "head"),
            P("head", "seq"),
            P(None, "head"),
            P("head", None),
            P(),
            P(),
            P(),
            P(),
            P(),
            P(),
        ),
        check_vma=False,
    )
```

```python
import functools

import jax
import jax.numpy as jnp
from jax import lax
from jax.experimental import pallas as pl
from jax.experimental.pallas import tpu as pltpu
from jax.sharding import PartitionSpec as P

HEAD_DIM = 64
PAIR = 2 * HEAD_DIM
STATS = 16
LOWEST = -1e29
EXCLUDED = -1e30
F32 = jnp.float32
BF16 = jnp.bfloat16


def matrix_product(left, right):
    return jnp.dot(left, right, preferred_element_type=F32)


def contract(left, right, left_dim, right_dim):
    return lax.dot_general(
        left, right, (((left_dim,), (right_dim,)), ((), ())), preferred_element_type=F32
    )


def times_transposed(left, right):
    return contract(left, right, 1, 1)


def transposed_times(left, right):
    return contract(left, right, 0, 0)


def norm_parts(values, norm_gain, norm_bias):
    average = jnp.mean(values, axis=-1, keepdims=True)
    centred = values - average
    scale = lax.rsqrt(jnp.mean(centred * centred, axis=-1, keepdims=True) + 1e-05)
    unit = centred * scale
    return unit * norm_gain + norm_bias, (unit, scale, norm_gain)


def norm_back(kept, grad):
    unit, scale, norm_gain = kept
    scaled = grad * norm_gain
    first = jnp.mean(scaled, axis=-1, keepdims=True)
    second = jnp.mean(scaled * unit, axis=-1, keepdims=True)
    return (scaled - first - unit * second) * scale, jnp.sum(grad * unit, axis=0), jnp.sum(grad, axis=0)


class Shape:
    def __init__(self, chips, groups, packs, rows, source_rows, starts, causal):
        self.chips, self.groups, self.packs, self.rows = chips, groups, packs, rows
        self.source_rows, self.starts, self.causal = source_rows, starts, causal
        self.step = groups
        while self.step > 1 and self.step * source_rows > 768:
            self.step //= 2
        self.steps = groups // self.step
        self.tile = 2 * rows
        self.length = 2 * chips * rows
        self.source_length = 2 * chips * source_rows


def position_range(shape, places, pack, target_bounds, source_bounds):
    starts = shape.starts
    low = jnp.zeros_like(places)
    high = jnp.zeros_like(places) + source_bounds[pack * starts]
    for entry in range(starts):
        later = places >= target_bounds[pack * starts + entry]
        low = jnp.where(later, source_bounds[pack * starts + entry], low)
        if entry + 1 < starts:
            following = source_bounds[pack * starts + entry + 1]
        else:
            following = jnp.int32(shape.source_length)
        high = jnp.where(later, following, high)
    if shape.causal:
        high = places + 1
    return low, high


def lane_places(shape, chip, core):
    lanes = lax.broadcasted_iota(jnp.int32, (1, shape.tile), 1)
    own = (2 * chip + core) * shape.rows + lanes
    other = (2 * chip + 1 - core) * shape.rows + lanes - shape.rows
    return jnp.where(lanes < shape.rows, own, other)


def step_conditions(shape, chip, pack, first_group, place, target_bounds, source_bounds):
    base, core = place[0], place[1]
    head = chip * (2 * shape.rows)
    tail = head + 2 * shape.rows - 1
    low_first, high_first = position_range(shape, head, pack, target_bounds, source_bounds)
    low_last, high_last = position_range(shape, tail, pack, target_bounds, source_bounds)
    begin = (base + 2 * first_group + core) * shape.source_rows
    end = begin + (2 * shape.step - 1) * shape.source_rows
    some = jnp.logical_and(low_first < end, high_last > begin)
    whole = jnp.logical_and(low_last <= begin, high_first >= end)
    return begin, some, whole


def source_places(shape, begin):
    size = shape.step * shape.source_rows
    rows = lax.broadcasted_iota(jnp.int32, (size, shape.tile), 0)
    places = begin + rows
    for group in range(1, shape.step):
        places = places + jnp.where(rows >= group * shape.source_rows, shape.source_rows, 0)
    return places


def both(own_ref, other_ref, chip, first, last, pack, rows):
    lanes = slice(pack * rows, (pack + 1) * rows)
    return jnp.concatenate(
        [own_ref[chip, first:last, lanes], other_ref[chip, first:last, lanes]], axis=1
    )


def one_head(pair_rows, head):
    feature = lax.broadcasted_iota(jnp.int32, pair_rows.shape, 0)
    mine = (feature >= HEAD_DIM) if head else (feature < HEAD_DIM)
    return jnp.where(mine, pair_rows, jnp.zeros_like(pair_rows))


def split_low(value):
    high = value.astype(BF16).astype(F32)
    return high, value - high


def split_parts(value):
    high = lax.reduce_precision(value, 8, 7)
    return high, value - high


def stat_rows(rows, width):
    index = lax.broadcasted_iota(jnp.int32, (STATS, width), 0)
    total = jnp.zeros((STATS, width), F32)
    for number, row in enumerate(rows):
        total = jnp.where(index == number, row, total)
    return total.astype(BF16)


def forward_kernel(
    shape, target_bounds, source_bounds, place, own_q, other_q, keys_values, own_out, other_out,
    value_t, maxima, sums, total,
):
    step_rows = shape.step * shape.source_rows
    for group in range(shape.groups):
        for pack in range(shape.packs):
            part = slice(pack * shape.source_rows, (pack + 1) * shape.source_rows)
            value_t[pack, :, group * shape.source_rows : (group + 1) * shape.source_rows] = (
                keys_values[group, 1, part, :].T
            )

    for pack in range(shape.packs):
        part = slice(pack * shape.source_rows, (pack + 1) * shape.source_rows)

        def per_chip(chip, unused, pack=pack, part=part):
            query = both(own_q, other_q, chip, 0, PAIR, pack, shape.rows)
            low, high = position_range(
                shape, lane_places(shape, chip, place[1]), pack, target_bounds, source_bounds
            )
            maxima[...] = jnp.full_like(maxima, LOWEST)
            sums[...] = jnp.zeros_like(sums)
            total[...] = jnp.zeros_like(total)
            for step in range(shape.steps):
                groups = slice(step * shape.step, (step + 1) * shape.step)
                begin, some, whole = step_conditions(
                    shape, chip, pack, step * shape.step, place, target_bounds, source_bounds
                )

                def fold(masked, step=step, groups=groups, begin=begin):
                    key_rows = keys_values[groups, 0, part, :].reshape(step_rows, PAIR)
                    if masked:
                        places = source_places(shape, begin)
                        allowed = jnp.logical_and(places >= low, places < high)
                    for head in range(2):
                        features = slice(head * HEAD_DIM, (head + 1) * HEAD_DIM)
                        scores = matrix_product(key_rows, one_head(query, head))
                        if masked:
                            scores = jnp.where(allowed, scores, EXCLUDED)
                        before = maxima[head : head + 1, :]
                        now = jnp.maximum(before, jnp.max(scores, axis=0, keepdims=True))
                        weights = jnp.exp(scores - now)
                        fading = jnp.exp(before - now)
                        maxima[head : head + 1, :] = now
                        sums[head : head + 1, :] = sums[head : head + 1, :] * fading + jnp.sum(
                            weights, axis=0, keepdims=True
                        )
                        values = value_t[pack, features, step * step_rows : (step + 1) * step_rows]
                        total[features, :] = total[features, :] * fading + matrix_product(
                            values, weights.astype(BF16)
                        )

                pl.when(jnp.logical_and(some, whole))(functools.partial(fold, False))
                pl.when(jnp.logical_and(some, jnp.logical_not(whole)))(
                    functools.partial(fold, True)
                )
            statistics = []
            for head in range(2):
                features = slice(head * HEAD_DIM, (head + 1) * HEAD_DIM)
                divisor = jnp.maximum(sums[head : head + 1, :], 1e-37)
                filled = sums[head : head + 1, :] > 0.0
                logs = jnp.where(filled, maxima[head : head + 1, :] + jnp.log(divisor), LOWEST)
                statistics.extend(split_low(logs))
                result = (total[features, :] / divisor).astype(BF16)
                for ref, offset in ((own_out, 0), (other_out, shape.rows)):
                    ref[chip, features, pack * shape.rows : (pack + 1) * shape.rows] = result[
                        :, offset : offset + shape.rows
                    ]
            statistics = stat_rows(statistics, shape.tile)
            for ref, offset in ((own_out, 0), (other_out, shape.rows)):
                ref[chip, PAIR : PAIR + STATS, pack * shape.rows : (pack + 1) * shape.rows] = (
                    statistics[:, offset : offset + shape.rows]
                )
            return 0

        lax.fori_loop(0, shape.chips, per_chip, 0)


def backward_kernel(
    shape, target_bounds, source_bounds, place, own_q, other_q, own_g, other_g, keys_values,
    own_dq, other_dq, key_grads, key_t, grad_key, grad_value, grad_query,
):
    step_rows = shape.step * shape.source_rows
    grad_key[...] = jnp.zeros_like(grad_key)
    grad_value[...] = jnp.zeros_like(grad_value)
    for group in range(shape.groups):
        for pack in range(shape.packs):
            part = slice(pack * shape.source_rows, (pack + 1) * shape.source_rows)
            key_t[pack, :, group * shape.source_rows : (group + 1) * shape.source_rows] = (
                keys_values[group, 0, part, :].T
            )

    for pack in range(shape.packs):
        part = slice(pack * shape.source_rows, (pack + 1) * shape.source_rows)

        def per_chip(chip, unused, pack=pack, part=part):
            query = both(own_q, other_q, chip, 0, PAIR, pack, shape.rows)
            grads = both(own_g, other_g, chip, 0, PAIR, pack, shape.rows)
            statistics = both(own_g, other_g, chip, PAIR, PAIR + STATS, pack, shape.rows).astype(F32)
            low, high = position_range(
                shape, lane_places(shape, chip, place[1]), pack, target_bounds, source_bounds
            )
            grad_query[...] = jnp.zeros_like(grad_query)
            for step in range(shape.steps):
                groups = slice(step * shape.step, (step + 1) * shape.step)
                begin, some, whole = step_conditions(
                    shape, chip, pack, step * shape.step, place, target_bounds, source_bounds
                )

                def fold(masked, step=step, groups=groups, begin=begin):
                    key_rows = keys_values[groups, 0, part, :].reshape(step_rows, PAIR)
                    value_rows = keys_values[groups, 1, part, :].reshape(step_rows, PAIR)
                    if masked:
                        places = source_places(shape, begin)
                        allowed = jnp.logical_and(places >= low, places < high)
                    probs, diffs, queries, gradients = [], [], [], []
                    lanes = slice(step * step_rows, (step + 1) * step_rows)
                    for head in range(2):
                        features = slice(head * HEAD_DIM, (head + 1) * HEAD_DIM)
                        head_query, head_grad = one_head(query, head), one_head(grads, head)
                        logs = statistics[2 * head : 2 * head + 1] + statistics[2 * head + 1 : 2 * head + 2]
                        delta = statistics[2 * head + 4 : 2 * head + 5] + statistics[2 * head + 5 : 2 * head + 6]
                        scores = matrix_product(key_rows, head_query)
                        if masked:
                            scores = jnp.where(allowed, scores, EXCLUDED)
                        weights = jnp.exp(scores - logs)
                        change = matrix_product(value_rows, head_grad)
                        diff = (weights * (change - delta)).astype(BF16)
                        grad_query[features, :] += matrix_product(key_t[pack, features, lanes], diff)
                        probs.append(weights.astype(BF16))
                        diffs.append(diff)
                        queries.append(head_query)
                        gradients.append(head_grad)
                    grad_key[pack, lanes, :] += times_transposed(
                        jnp.concatenate(diffs, axis=1), jnp.concatenate(queries, axis=1)
                    )
                    grad_value[pack, lanes, :] += times_transposed(
                        jnp.concatenate(probs, axis=1), jnp.concatenate(gradients, axis=1)
                    )

                pl.when(jnp.logical_and(some, whole))(functools.partial(fold, False))
                pl.when(jnp.logical_and(some, jnp.logical_not(whole)))(
                    functools.partial(fold, True)
                )
            result = (grad_query[...] * HEAD_DIM**-0.5).astype(BF16)
            for ref, offset in ((own_dq, 0), (other_dq, shape.rows)):
                ref[chip, :, pack * shape.rows : (pack + 1) * shape.rows] = result[
                    :, offset : offset + shape.rows
                ]
            return 0

        lax.fori_loop(0, shape.chips, per_chip, 0)

    for group in range(shape.groups):
        for pack in range(shape.packs):
            part = slice(pack * shape.source_rows, (pack + 1) * shape.source_rows)
            lanes = slice(group * shape.source_rows, (group + 1) * shape.source_rows)
            key_grads[group, 0, part, :] = grad_key[pack, lanes, :].astype(BF16)
            key_grads[group, 1, part, :] = grad_value[pack, lanes, :].astype(BF16)


def smem():
    return pl.BlockSpec(memory_space=pltpu.SMEM)


def vmem():
    return pl.BlockSpec(memory_space=pltpu.VMEM)


PARAMS = dict(vmem_limit_bytes=48 * 1024 * 1024)


def attention_forward(shape, bounds, place, own_q, other_q, keys_values):
    width = shape.packs * shape.rows
    pairs = shape.packs * shape.length * shape.groups * shape.source_rows
    message = jax.ShapeDtypeStruct((shape.chips, PAIR + STATS, width), BF16)
    return pl.pallas_call(
        functools.partial(forward_kernel, shape),
        out_shape=(message, message),
        in_specs=[smem()] * 3 + [vmem()] * 3,
        out_specs=(vmem(), vmem()),
        scratch_shapes=[
            pltpu.VMEM((shape.packs, PAIR, shape.groups * shape.source_rows), BF16),
            pltpu.VMEM((8, shape.tile), F32),
            pltpu.VMEM((8, shape.tile), F32),
            pltpu.VMEM((PAIR, shape.tile), F32),
        ],
        compiler_params=pltpu.CompilerParams(**PARAMS),
        cost_estimate=pl.CostEstimate(
            flops=8 * pairs * HEAD_DIM, bytes_accessed=6 * 1024 * 1024, transcendentals=2 * pairs
        ),
    )(bounds[0], bounds[1], place, own_q, other_q, keys_values)


def attention_backward(shape, bounds, place, own_q, other_q, own_g, other_g, keys_values):
    width = shape.packs * shape.rows
    pairs = shape.packs * shape.length * shape.groups * shape.source_rows
    source = shape.groups * shape.source_rows
    message = jax.ShapeDtypeStruct((shape.chips, PAIR, width), BF16)
    return pl.pallas_call(
        functools.partial(backward_kernel, shape),
        out_shape=(message, message, jax.ShapeDtypeStruct(keys_values.shape, BF16)),
        in_specs=[smem()] * 3 + [vmem()] * 5,
        out_specs=(vmem(), vmem(), vmem()),
        scratch_shapes=[
            pltpu.VMEM((shape.packs, PAIR, source), BF16),
            pltpu.VMEM((shape.packs, source, PAIR), F32),
            pltpu.VMEM((shape.packs, source, PAIR), F32),
            pltpu.VMEM((PAIR, shape.tile), F32),
        ],
        compiler_params=pltpu.CompilerParams(**PARAMS),
        cost_estimate=pl.CostEstimate(
            flops=20 * pairs * HEAD_DIM, bytes_accessed=8 * 1024 * 1024, transcendentals=2 * pairs
        ),
    )(bounds[0], bounds[1], place, own_q, other_q, own_g, other_g, keys_values)


class RowShape:
    def __init__(self, chips, rows, starts):
        self.chips, self.rows, self.starts = chips, rows, starts
        self.source_length, self.causal = 2 * chips * rows, True
        self.span = 2 if chips % 2 == 0 else 1
        self.tiles = chips // self.span
        self.tile = self.span * rows
        self.step = 2 * self.span * rows


def own_places(shape, tile, core):
    lanes = lax.broadcasted_iota(jnp.int32, (1, shape.tile), 1)
    places = 2 * tile * shape.span * shape.rows + core * shape.rows + lanes
    for block in range(1, shape.span):
        places = places + jnp.where(lanes >= block * shape.rows, shape.rows, 0)
    return places


def chip_places(shape, step, core):
    rows = lax.broadcasted_iota(jnp.int32, (shape.step, shape.tile), 0)
    places = step * shape.step + rows
    for block in range(2 * shape.span):
        here = jnp.logical_and(rows >= block * shape.rows, rows < (block + 1) * shape.rows)
        shift = shape.rows * core if block % 2 == 0 else -shape.rows * core
        places = places + jnp.where(here, shift, 0)
    return places


def row_conditions(shape, tile, step, pack, bounds):
    head = tile * shape.step
    tail = head + shape.step - 1
    begin = step * shape.step
    end = begin + shape.step
    low_first, _ = position_range(shape, head, pack, bounds, bounds)
    low_last, _ = position_range(shape, tail, pack, bounds, bounds)
    some = low_first < end
    whole = jnp.logical_and(low_last <= begin, end <= head + 1)
    return some, whole


def fill_rows(shape, own_kv, other_kv, which, target, transposed):
    for chip in range(shape.chips):
        for side, ref in enumerate((own_kv, other_kv)):
            first = (2 * chip + side) * shape.rows
            block = ref[chip, which]
            if transposed:
                target[:, first : first + shape.rows] = block.T
            else:
                target[first : first + shape.rows, :] = block


def tile_lanes(ref, tile, span):
    return jnp.concatenate([ref[tile * span + block] for block in range(span)], axis=1)


def row_forward_kernel(
    shape, bounds, place, queries, own_kv, other_kv, out, logs, key_all, value_t, maxima, sums, total
):
    pack, core = place[0], place[1]
    fill_rows(shape, own_kv, other_kv, 0, key_all, False)
    fill_rows(shape, own_kv, other_kv, 1, value_t, True)

    def per_tile(tile, unused):
        query = tile_lanes(queries, tile, shape.span)
        low, high = position_range(shape, own_places(shape, tile, core), pack, bounds, bounds)
        maxima[...] = jnp.full_like(maxima, LOWEST)
        sums[...] = jnp.zeros_like(sums)
        total[...] = jnp.zeros_like(total)

        def per_step(step, unused):
            some, whole = row_conditions(shape, tile, step, pack, bounds)
            first = pl.multiple_of(step * shape.step, shape.step)

            def fold(masked):
                key_rows = key_all[pl.ds(first, shape.step), :]
                if masked:
                    places = chip_places(shape, step, core)
                    allowed = jnp.logical_and(places >= low, places < high)
                for head in range(2):
                    features = slice(head * HEAD_DIM, (head + 1) * HEAD_DIM)
                    scores = matrix_product(key_rows, one_head(query, head))
                    if masked:
                        scores = jnp.where(allowed, scores, EXCLUDED)
                    before = maxima[head : head + 1, :]
                    now = jnp.maximum(before, jnp.max(scores, axis=0, keepdims=True))
                    weights = jnp.exp(scores - now)
                    fading = jnp.exp(before - now)
                    maxima[head : head + 1, :] = now
                    sums[head : head + 1, :] = sums[head : head + 1, :] * fading + jnp.sum(
                        weights, axis=0, keepdims=True
                    )
                    values = value_t[features, pl.ds(first, shape.step)]
                    total[features, :] = total[features, :] * fading + matrix_product(
                        values, weights.astype(BF16)
                    )

            pl.when(jnp.logical_and(some, whole))(functools.partial(fold, False))
            pl.when(jnp.logical_and(some, jnp.logical_not(whole)))(functools.partial(fold, True))
            return 0

        lax.fori_loop(0, tile + 1, per_step, 0)
        for head in range(2):
            features = slice(head * HEAD_DIM, (head + 1) * HEAD_DIM)
            divisor = sums[head : head + 1, :]
            result = (total[features, :] / divisor).astype(BF16)
            found = maxima[head : head + 1, :] + jnp.log(divisor)
            for block in range(shape.span):
                lanes = slice(block * shape.rows, (block + 1) * shape.rows)
                out[tile * shape.span + block, features, :] = result[:, lanes]
                logs[tile * shape.span + block, head : head + 1, :] = found[:, lanes]
        return 0

    lax.fori_loop(0, shape.tiles, per_tile, 0)


def row_backward_kernel(
    shape, bounds, place, queries, outputs, logs, grads, own_kv, other_kv,
    query_grads, own_dkv, other_dkv, key_all, value_all, key_t, grad_key, grad_value, grad_query,
):
    pack, core = place[0], place[1]
    fill_rows(shape, own_kv, other_kv, 0, key_all, False)
    fill_rows(shape, own_kv, other_kv, 1, value_all, False)
    fill_rows(shape, own_kv, other_kv, 0, key_t, True)
    grad_key[...] = jnp.zeros_like(grad_key)
    grad_value[...] = jnp.zeros_like(grad_value)

    def per_tile(tile, unused):
        query = tile_lanes(queries, tile, shape.span)
        grad = tile_lanes(grads, tile, shape.span)
        product = grad.astype(F32) * tile_lanes(outputs, tile, shape.span).astype(F32)
        log_rows = tile_lanes(logs, tile, shape.span)
        low, high = position_range(shape, own_places(shape, tile, core), pack, bounds, bounds)
        heads = []
        for head in range(2):
            features = slice(head * HEAD_DIM, (head + 1) * HEAD_DIM)
            delta = jnp.sum(product[features], axis=0, keepdims=True)
            heads.append((one_head(query, head), one_head(grad, head), log_rows[head : head + 1], delta))
        grad_query[...] = jnp.zeros_like(grad_query)

        def per_step(step, unused):
            some, whole = row_conditions(shape, tile, step, pack, bounds)
            first = pl.multiple_of(step * shape.step, shape.step)

            def fold(masked):
                part = pl.ds(first, shape.step)
                key_rows, value_rows = key_all[part, :], value_all[part, :]
                if masked:
                    places = chip_places(shape, step, core)
                    allowed = jnp.logical_and(places >= low, places < high)
                probs, diffs = [], []
                for head in range(2):
                    head_query, head_grad, log_row, delta = heads[head]
                    features = slice(head * HEAD_DIM, (head + 1) * HEAD_DIM)
                    scores = matrix_product(key_rows, head_query)
                    if masked:
                        scores = jnp.where(allowed, scores, EXCLUDED)
                    weights = jnp.exp(scores - log_row)
                    change = matrix_product(value_rows, head_grad)
                    diff = (weights * (change - delta)).astype(BF16)
                    grad_query[features, :] += matrix_product(key_t[features, part], diff)
                    probs.append(weights.astype(BF16))
                    diffs.append(diff)
                grad_key[part, :] += times_transposed(
                    jnp.concatenate(diffs, axis=1),
                    jnp.concatenate([heads[0][0], heads[1][0]], axis=1),
                )
                grad_value[part, :] += times_transposed(
                    jnp.concatenate(probs, axis=1),
                    jnp.concatenate([heads[0][1], heads[1][1]], axis=1),
                )

            pl.when(jnp.logical_and(some, whole))(functools.partial(fold, False))
            pl.when(jnp.logical_and(some, jnp.logical_not(whole)))(functools.partial(fold, True))
            return 0

        lax.fori_loop(0, tile + 1, per_step, 0)
        result = (grad_query[...] * HEAD_DIM**-0.5).astype(BF16)
        for block in range(shape.span):
            query_grads[tile * shape.span + block] = result[
                :, block * shape.rows : (block + 1) * shape.rows
            ]
        return 0

    lax.fori_loop(0, shape.tiles, per_tile, 0)
    for chip in range(shape.chips):
        for side, ref in enumerate((own_dkv, other_dkv)):
            first = (2 * chip + side) * shape.rows
            ref[chip, 0] = grad_key[first : first + shape.rows, :].astype(BF16)
            ref[chip, 1] = grad_value[first : first + shape.rows, :].astype(BF16)


def row_forward(shape, bounds, place, queries, own_kv, other_kv):
    length = shape.source_length
    return pl.pallas_call(
        functools.partial(row_forward_kernel, shape),
        out_shape=(
            jax.ShapeDtypeStruct(queries.shape, BF16),
            jax.ShapeDtypeStruct((shape.chips, 2, shape.rows), F32),
        ),
        in_specs=[smem()] * 2 + [vmem()] * 3,
        out_specs=(vmem(), vmem()),
        scratch_shapes=[
            pltpu.VMEM((length, PAIR), BF16),
            pltpu.VMEM((PAIR, length), BF16),
            pltpu.VMEM((8, shape.tile), F32),
            pltpu.VMEM((8, shape.tile), F32),
            pltpu.VMEM((PAIR, shape.tile), F32),
        ],
        compiler_params=pltpu.CompilerParams(**PARAMS),
        cost_estimate=pl.CostEstimate(
            flops=6 * length * length * HEAD_DIM,
            bytes_accessed=4 * 1024 * 1024,
            transcendentals=length * length,
        ),
    )(bounds, place, queries, own_kv, other_kv)


def row_backward(shape, bounds, place, queries, outputs, logs, grads, own_kv, other_kv):
    length = shape.source_length
    return pl.pallas_call(
        functools.partial(row_backward_kernel, shape),
        out_shape=(
            jax.ShapeDtypeStruct(queries.shape, BF16),
            jax.ShapeDtypeStruct(own_kv.shape, BF16),
            jax.ShapeDtypeStruct(own_kv.shape, BF16),
        ),
        in_specs=[smem()] * 2 + [vmem()] * 6,
        out_specs=(vmem(), vmem(), vmem()),
        scratch_shapes=[
            pltpu.VMEM((length, PAIR), BF16),
            pltpu.VMEM((length, PAIR), BF16),
            pltpu.VMEM((PAIR, length), BF16),
            pltpu.VMEM((length, PAIR), F32),
            pltpu.VMEM((length, PAIR), F32),
            pltpu.VMEM((PAIR, shape.tile), F32),
        ],
        compiler_params=pltpu.CompilerParams(**PARAMS),
        cost_estimate=pl.CostEstimate(
            flops=12 * length * length * HEAD_DIM,
            bytes_accessed=6 * 1024 * 1024,
            transcendentals=length * length,
        ),
    )(bounds, place, queries, outputs, logs, grads, own_kv, other_kv)


def blocks(array):
    return pl.BlockSpec(array.shape, lambda step, zeros=(0,) * array.ndim: zeros)


def call(kernel, out_shape, args, grid=None, in_specs=None, out_specs=None, scratch=(), flops=0):
    if in_specs is None:
        in_specs = [vmem()] * len(args)
    if out_specs is None:
        out_specs = jax.tree.map(lambda _: vmem(), out_shape)
    extra = {} if grid is None else {"grid": grid}
    return pl.pallas_call(
        kernel,
        out_shape=out_shape,
        in_specs=in_specs,
        out_specs=out_specs,
        scratch_shapes=list(scratch),
        compiler_params=pltpu.CompilerParams(**PARAMS),
        cost_estimate=pl.CostEstimate(flops=flops, bytes_accessed=8 << 20, transcendentals=0),
        **extra,
    )(*args)


def project_self(x, wq, wk, wv, packs):
    rows, width = x.shape[0], wq.shape[1]
    pairs, each = width // PAIR, rows // packs

    def kernel(x_ref, wq_ref, wk_ref, wv_ref, out):
        value = x_ref[...]
        query = (matrix_product(value, wq_ref[...]) * HEAD_DIM**-0.5).astype(BF16)
        for pack in range(packs):
            for pair in range(pairs):
                part = query[pack * each : (pack + 1) * each, pair * PAIR : (pair + 1) * PAIR]
                out[pack * pairs + pair, 0] = part.T
        for number, ref in ((1, wk_ref), (2, wv_ref)):
            result = matrix_product(value, ref[...]).astype(BF16)
            for pack in range(packs):
                for pair in range(pairs):
                    out[pack * pairs + pair, number] = result[
                        pack * each : (pack + 1) * each, pair * PAIR : (pair + 1) * PAIR
                    ]

    return call(
        kernel,
        jax.ShapeDtypeStruct((packs * pairs, 3, each, PAIR), BF16),
        (x, wq, wk, wv),
        flops=6 * rows * x.shape[1] * width,
    )


def project_sources(x, wk, wv):
    rows, depth = x.shape
    pairs = wk.shape[1] // PAIR
    size = rows // 3 if rows % 48 == 0 else rows

    def kernel(x_ref, wk_ref, wv_ref, out):
        for number, ref in enumerate((wk_ref, wv_ref)):
            result = matrix_product(x_ref[...], ref[...]).astype(BF16)
            for pair in range(pairs):
                out[pair, number] = result[:, pair * PAIR : (pair + 1) * PAIR]

    return call(
        kernel,
        jax.ShapeDtypeStruct((pairs, 2, rows, PAIR), BF16),
        (x, wk, wv),
        grid=(rows // size,),
        in_specs=[pl.BlockSpec((size, depth), lambda i: (i, 0)), blocks(wk), blocks(wv)],
        out_specs=pl.BlockSpec((pairs, 2, size, PAIR), lambda i: (0, 0, i, 0)),
        flops=4 * rows * depth * wk.shape[1],
    )


def source_grads(grads, wk, wv):
    pairs, _, rows, _ = grads.shape
    size = rows // 3 if rows % 48 == 0 else rows
    depth = wk.shape[0]

    def kernel(grads_ref, wk_ref, wv_ref, out):
        keys = jnp.concatenate([grads_ref[pair, 0] for pair in range(pairs)], axis=1)
        values = jnp.concatenate([grads_ref[pair, 1] for pair in range(pairs)], axis=1)
        total = times_transposed(keys, wk_ref[...]) + times_transposed(values, wv_ref[...])
        out[...] = total.astype(BF16)

    return call(
        kernel,
        jax.ShapeDtypeStruct((rows, depth), BF16),
        (grads, wk, wv),
        grid=(rows // size,),
        in_specs=[
            pl.BlockSpec((pairs, 2, size, PAIR), lambda i: (0, 0, i, 0)),
            blocks(wk),
            blocks(wv),
        ],
        out_specs=pl.BlockSpec((size, depth), lambda i: (i, 0)),
        flops=4 * rows * depth * wk.shape[1],
    )


def input_grads(back, wq, wk, wv, packs):
    pairs = back.shape[0] // packs
    each = back.shape[3]
    depth = wq.shape[0]

    def kernel(back_ref, wq_ref, wk_ref, wv_ref, out):
        for pack in range(packs):
            first = pack * pairs
            parts = [
                jnp.concatenate([back_ref[first + pair, 0].T for pair in range(pairs)], axis=1),
                jnp.concatenate([back_ref[first + pair, 1] for pair in range(pairs)], axis=1),
                jnp.concatenate([back_ref[first + pair, 2] for pair in range(pairs)], axis=1),
            ]
            total = times_transposed(parts[0], wq_ref[...])
            total += times_transposed(parts[1], wk_ref[...])
            total += times_transposed(parts[2], wv_ref[...])
            out[pack * each : (pack + 1) * each, :] = total.astype(BF16)

    return call(
        kernel,
        jax.ShapeDtypeStruct((packs * each, depth), BF16),
        (back, wq, wk, wv),
        flops=6 * packs * each * depth * wq.shape[1],
    )


def self_weight_grads(x, back, packs):
    pairs = back.shape[0] // packs
    rows, depth = x.shape
    width = pairs * PAIR

    def kernel(x_ref, back_ref, out):
        value = x_ref[...].T
        each = rows // packs
        for number in range(3):
            for pair in range(pairs):
                column = number * width + pair * PAIR
                if number == 0:
                    other = jnp.concatenate(
                        [back_ref[pack * pairs + pair, 0] for pack in range(packs)], axis=1
                    )
                    result = times_transposed(value, other)
                else:
                    other = jnp.concatenate(
                        [back_ref[pack * pairs + pair, number] for pack in range(packs)], axis=0
                    )
                    result = matrix_product(value, other)
                out[:, column : column + PAIR] = result.astype(BF16)

    return call(
        kernel,
        jax.ShapeDtypeStruct((depth, 3 * width), BF16),
        (x, back),
        flops=2 * rows * depth * 3 * width,
    )


def middle_weight_grads(
    second, mixed_cross, first, mixed_self, one, query_grads, source, source_dkv,
    third, narrow, two, narrow_grads,
):
    depth = second.shape[1]
    width = mixed_cross.shape[0]
    pairs = width // PAIR

    def kernel(
        second_ref, cross_ref, first_ref, self_ref, one_ref, query_ref, source_ref, dkv_ref,
        third_ref, narrow_ref, two_ref, dnarrow_ref, out,
    ):
        step = pl.program_id(0)

        def rows_by_features(left, right):
            out[...] = times_transposed(left[...].T, right[...]).astype(BF16)

        pl.when(step == 0)(lambda: rows_by_features(second_ref, cross_ref))
        pl.when(step == 1)(lambda: rows_by_features(first_ref, self_ref))
        pl.when(step == 2)(lambda: rows_by_features(one_ref, query_ref))

        def sources(number):
            right = jnp.concatenate([dkv_ref[pair, number] for pair in range(pairs)], axis=1)
            out[...] = matrix_product(source_ref[...].T, right).astype(BF16)

        pl.when(step == 3)(lambda: sources(0))
        pl.when(step == 4)(lambda: sources(1))

        def adapters():
            half = narrow_ref.shape[1]
            up = 4.0 * matrix_product(third_ref[...].T, narrow_ref[...])
            out[:, :half] = up.astype(BF16)
            out[:, half:] = matrix_product(two_ref[...].T, dnarrow_ref[...]).astype(BF16)

        pl.when(step == 5)(adapters)

    args = (
        second, mixed_cross, first, mixed_self, one, query_grads, source, source_dkv,
        third, narrow, two, narrow_grads,
    )
    return call(
        kernel,
        jax.ShapeDtypeStruct((depth, 6 * width), BF16),
        args,
        grid=(6,),
        in_specs=[blocks(value) for value in args],
        out_specs=pl.BlockSpec((depth, width), lambda i: (0, i)),
        flops=2 * depth * width * 2560,
    )


def cross_message(second, weight, attended, logs):
    rows = second.shape[0]
    pairs = weight.shape[0] // PAIR

    def kernel(second_ref, weight_ref, attended_ref, logs_ref, out):
        for pair in range(pairs):
            grads = times_transposed(weight_ref[pair * PAIR : (pair + 1) * PAIR, :], second_ref[...])
            low = grads.astype(BF16)
            out[pair, :PAIR, :] = low
            low = low.astype(F32)
            first, later = [], []
            for side in range(2):
                head = 2 * pair + side
                product = low[side * HEAD_DIM : (side + 1) * HEAD_DIM] * attended_ref[head]
                first.extend(split_low(logs_ref[head : head + 1, :]))
                later.extend(split_low(jnp.sum(product, axis=0, keepdims=True)))
            out[pair, PAIR : PAIR + STATS, :] = stat_rows(first + later, rows)

    return call(
        kernel,
        jax.ShapeDtypeStruct((pairs, PAIR + STATS, rows), BF16),
        (second, weight, attended, logs),
        flops=2 * rows * weight.shape[0] * weight.shape[1],
    )


def on_device(
    seq_size,
    head_size,
    inputs,
    encoded,
    tgt_bounds,
    src_bounds,
    self_query,
    self_key,
    self_value,
    self_out,
    cross_query,
    cross_key,
    cross_value,
    cross_out,
    ffn_in,
    ffn_out,
    adapter_down,
    adapter_up,
    norm1_gain,
    norm1_bias,
    norm2_gain,
    norm2_bias,
    norm3_gain,
    norm3_bias,
    cotangent,
):
    pack_count, row_count, model_width = inputs.shape
    source_rows = encoded.shape[1]
    local_width = self_query.shape[1]
    pairs_here = local_width // PAIR
    chips = seq_size // 2
    copies = chips // pairs_here
    rows = pack_count * row_count
    starts = tgt_bounds.shape[1]
    position = lax.axis_index("seq")
    core = position % 2
    base = position // (2 * pairs_here) * (2 * pairs_here)
    place = jnp.stack([base, core]).astype(jnp.int32)
    by_pack = pairs_here * pack_count == chips and head_size == 2
    row_place = jnp.stack([position // (2 * pairs_here), core]).astype(jnp.int32)
    row_shape = RowShape(chips, row_count, starts)
    self_bounds = (tgt_bounds.reshape(-1), tgt_bounds.reshape(-1))
    cross_bounds = (tgt_bounds.reshape(-1), src_bounds.reshape(-1))
    self_shape = Shape(chips, pairs_here, pack_count, row_count, row_count, starts, True)
    cross_shape = Shape(chips, pairs_here, pack_count, row_count, source_rows, starts, False)
    flat_inputs = inputs.reshape(rows, model_width)
    flat_encoded = encoded.reshape(pack_count * source_rows, model_width)

    all_chips = [[2 * chip + side for chip in range(chips)] for side in range(2)]
    near_chips = [
        [2 * (copy * pairs_here + pair) + side for pair in range(pairs_here)]
        for copy in range(copies)
        for side in range(2)
    ]

    def swap_core(value):
        return lax.ppermute(value, "seq", [(i, i ^ 1) for i in range(seq_size)])

    def to_all(value):
        return lax.all_to_all(value, "seq", 0, 0, axis_index_groups=all_chips, tiled=True)

    def to_near(value):
        if pairs_here == 1:
            return value
        return lax.all_to_all(value, "seq", 0, 0, axis_index_groups=near_chips, tiled=True)

    def head_sum(value):
        if head_size == 2:
            low = lax.reduce_precision(value, 8, 7)
            return low + lax.ppermute(low.astype(BF16), "head", [(0, 1), (1, 0)]).astype(F32)
        return lax.psum(value, "head")

    def head_sum_low(low):
        if head_size == 2:
            met = lax.ppermute(low, "head", [(0, 1), (1, 0)])
            return low.astype(F32) + met.astype(F32)
        return lax.psum(low.astype(F32), "head")

    def spread_queries(features):
        message = features.reshape(pairs_here, -1, rows)
        own = to_all(jnp.tile(message, (copies, 1, 1)))
        return own, swap_core(own)

    def pair_rows(keys, values):
        def cut(value):
            return value.reshape(-1, pairs_here, PAIR).transpose(1, 0, 2)

        return jnp.stack([cut(keys), cut(values)], axis=1)

    def join_rows(message):
        return message.transpose(1, 2, 0, 3).reshape(2, -1, local_width)

    def logs_of(message):
        stats = message[:, PAIR : PAIR + 4, :].astype(F32)
        return stats[:, 0::2] + stats[:, 1::2]

    def weighted(parts, logs):
        highest = jnp.max(logs, axis=0)
        weights = jnp.exp(logs - highest)
        denominator = jnp.sum(weights, axis=0)
        shares = weights / denominator
        split = parts.reshape(parts.shape[:-2] + (2, HEAD_DIM, rows)).astype(F32)
        merged = jnp.sum(split * shares[:, :, :, None, :], axis=0)
        return merged, highest + jnp.log(denominator)

    def collect(own_part, other_part):
        met = swap_core(other_part)
        parts = jnp.stack([own_part, met])
        logs = jnp.stack([logs_of(own_part), logs_of(met)])
        merged, total = weighted(parts[:, :, :PAIR], logs)
        high, low = split_parts(total)
        statistics = jnp.stack([high, low], axis=2).reshape(chips, 4, rows)
        statistics = jnp.pad(statistics, ((0, 0), (0, STATS - 4), (0, 0)))
        message = jnp.concatenate(
            [merged.reshape(chips, PAIR, rows).astype(BF16), statistics.astype(BF16)], axis=1
        )
        back = to_all(message)
        logs = logs_of(back).reshape(copies, pairs_here, 2, rows)
        features = back[:, :PAIR].reshape(copies, pairs_here, PAIR, rows)
        merged, total = weighted(features, logs)
        return merged, total

    def spread_grads(grad_features, merged, total):
        split = grad_features.reshape(pairs_here, 2, HEAD_DIM, rows).astype(F32)
        delta = jnp.sum(split * merged, axis=2)
        statistics = jnp.concatenate(
            [
                jnp.stack(split_parts(total), axis=2).reshape(pairs_here, 4, rows),
                jnp.stack(split_parts(delta), axis=2).reshape(pairs_here, 4, rows),
                jnp.zeros((pairs_here, STATS - 8, rows), F32),
            ],
            axis=1,
        ).astype(BF16)
        message = jnp.concatenate([grad_features.reshape(pairs_here, PAIR, rows), statistics], axis=1)
        return spread_queries(message)

    def collect_query_grads(own_part, other_part):
        total = (own_part.astype(F32) + swap_core(other_part).astype(F32)).astype(BF16)
        back = to_all(total).reshape(copies, local_width, rows)
        return jnp.sum(back.astype(F32), axis=0).astype(BF16)

    scaling = HEAD_DIM**-0.5
    cross_kv = to_near(project_sources(flat_encoded, cross_key, cross_value))
    if by_pack:
        message = project_self(flat_inputs, self_query, self_key, self_value, pack_count)
        met = to_all(message)
        self_q, self_kv = met[:, 0], met[:, 1:]
        self_kv_other = swap_core(self_kv)
        self_heads, self_logs = row_forward(
            row_shape, self_bounds[0], row_place, self_q, self_kv, self_kv_other
        )
        self_heads, cross_kv = lax.optimization_barrier((self_heads, cross_kv))
        back = to_all(self_heads).reshape(pack_count, pairs_here, PAIR, row_count)
        mixed_self = back.transpose(1, 2, 0, 3).reshape(local_width, rows)
    else:
        query_self = (contract(self_query, flat_inputs, 0, 1) * scaling).astype(BF16)
        key_self = matrix_product(flat_inputs, self_key).astype(BF16)
        value_self = matrix_product(flat_inputs, self_value).astype(BF16)
        self_q = spread_queries(query_self)
        self_kv = to_near(pair_rows(key_self, value_self))
        own_part, other_part = attention_forward(self_shape, self_bounds, place, *self_q, self_kv)
        attended_self, log_self = collect(own_part, other_part)
        mixed_self = attended_self.reshape(local_width, rows).astype(BF16)
    out_self = head_sum(transposed_times(mixed_self, self_out))
    normed_one, norm_one_back = norm_parts(flat_inputs.astype(F32) + out_self, norm1_gain, norm1_bias)
    normed_one_low = normed_one.astype(BF16)
    query_cross = (contract(cross_query, normed_one_low, 0, 1) * scaling).astype(BF16)
    cross_q = spread_queries(query_cross)
    own_part, other_part = attention_forward(cross_shape, cross_bounds, place, *cross_q, cross_kv)
    attended_cross, log_cross = collect(own_part, other_part)
    mixed_cross = attended_cross.reshape(local_width, rows).astype(BF16)
    out_cross = head_sum(transposed_times(mixed_cross, cross_out))
    normed_two, norm_two_back = norm_parts(normed_one + out_cross, norm2_gain, norm2_bias)
    normed_two_low = normed_two.astype(BF16)
    hidden = matrix_product(normed_two_low, ffn_in)
    activated, gelu_hidden_back = jax.vjp(jax.nn.gelu, hidden)
    activated_low = activated.astype(BF16)
    narrow = matrix_product(normed_two_low, adapter_down)
    narrow_act, gelu_narrow_back = jax.vjp(jax.nn.gelu, narrow)
    narrow_low = narrow_act.astype(BF16)
    branch_part = matrix_product(activated_low, ffn_out) + 4.0 * matrix_product(
        narrow_low, adapter_up
    )
    branch = head_sum(branch_part)
    normed_three, norm_three_back = norm_parts(normed_two + branch, norm3_gain, norm3_bias)
    grad_third, grad_gain_three, grad_bias_three = norm_back(
        norm_three_back, cotangent.reshape(rows, model_width).astype(F32)
    )
    grad_branch = grad_third.astype(BF16)
    grad_hidden = gelu_hidden_back(times_transposed(grad_branch, ffn_out))[0].astype(BF16)
    grad_narrow = gelu_narrow_back(4.0 * times_transposed(grad_branch, adapter_up))[0].astype(BF16)
    grad_two_part = times_transposed(grad_hidden, ffn_in) + times_transposed(
        grad_narrow, adapter_down
    )
    grad_two = grad_third + head_sum(grad_two_part)
    grad_second, grad_gain_two, grad_bias_two = norm_back(norm_two_back, grad_two)
    grad_second_low = grad_second.astype(BF16)
    message = cross_message(
        grad_second_low, cross_out, attended_cross.reshape(-1, HEAD_DIM, rows), log_cross.reshape(-1, rows)
    )
    cross_g = spread_queries(message)
    own_part, other_part, cross_dkv = attention_backward(
        cross_shape, cross_bounds, place, *cross_q, *cross_g, cross_kv
    )
    grad_query_cross = collect_query_grads(own_part, other_part)
    source_dkv = to_near(cross_dkv)
    grad_one_sum = head_sum(transposed_times(grad_query_cross, contract_t(cross_query)))
    grad_first, grad_gain_one, grad_bias_one = norm_back(norm_one_back, grad_second + grad_one_sum)
    grad_first_low = grad_first.astype(BF16)
    grad_mixed_self = times_transposed(self_out, grad_first_low).astype(BF16)
    grad_source = head_sum_low(source_grads(source_dkv, cross_key, cross_value))
    middle = middle_weight_grads(
        grad_second_low, mixed_cross, grad_first_low, mixed_self, normed_one_low, grad_query_cross,
        flat_encoded, source_dkv, grad_branch, narrow_low, normed_two_low, grad_narrow,
    )
    if by_pack:
        message = grad_mixed_self.reshape(pairs_here, PAIR, pack_count, row_count)
        grad_heads = to_all(message.transpose(2, 0, 1, 3).reshape(chips, PAIR, row_count))
        grad_heads, middle = lax.optimization_barrier((grad_heads, middle))
        dq, own_dkv, other_dkv = row_backward(
            row_shape, self_bounds[0], row_place, self_q, self_heads, self_logs, grad_heads,
            self_kv, self_kv_other,
        )
        dkv = (own_dkv.astype(F32) + swap_core(other_dkv).astype(F32)).astype(BF16)
        back = to_all(jnp.concatenate([dq[:, None], dkv], axis=1))
        grad_inputs = grad_first + head_sum_low(
            input_grads(back, self_query, self_key, self_value, pack_count)
        )
        self_parts = self_weight_grads(flat_inputs, back, pack_count)
    else:
        self_g = spread_grads(grad_mixed_self, attended_self, log_self)
        own_part, other_part, self_dkv = attention_backward(
            self_shape, self_bounds, place, *self_q, *self_g, self_kv
        )
        grad_query_self = collect_query_grads(own_part, other_part)
        grad_key_self, grad_value_self = join_rows(to_near(self_dkv))
        grad_in_part = (
            transposed_times(grad_query_self, contract_t(self_query))
            + times_transposed(grad_key_self, self_key)
            + times_transposed(grad_value_self, self_value)
        )
        grad_inputs = grad_first + head_sum(grad_in_part)
        grad_self_query = contract(flat_inputs, grad_query_self, 0, 1)
        grad_self_key = transposed_times(flat_inputs, grad_key_self)
        grad_self_value = transposed_times(flat_inputs, grad_value_self)
        self_parts = jnp.concatenate(
            [part.astype(BF16) for part in (grad_self_query, grad_self_key, grad_self_value)], axis=1
        )

    def scatter(joined):
        return lax.psum_scatter(joined, "seq", scatter_dimension=0, tiled=True)

    def step(values, bit, axis):
        mine = position // bit % 2

        def half(which):
            return [lax.dynamic_index_in_dim(value, which, axis, keepdims=False) for value in values]

        send = sum(value.astype(F32) for value in half(1 - mine)).astype(BF16)
        met = lax.ppermute(send, "seq", [(i, i ^ bit) for i in range(seq_size)])
        return half(mine) + [met]

    def scatter_by_halves(joined):
        if seq_size != 16:
            return scatter(joined)
        width = joined.shape[1]
        values = step([joined.reshape(2, 2, 2, 2, -1, width)], 1, 3)
        first = [value[..., : width // 2] for value in values]
        second = [value[..., width // 2 :] for value in values]
        first, second = step(first, 2, 2), step(second, 4, 1)
        first, second = step(first, 4, 1), step(second, 2, 1)
        first, second = step(first, 8, 0), step(second, 8, 0)
        return jnp.concatenate(
            [sum(value.astype(F32) for value in part) for part in (first, second)], axis=-1
        )

    def gather_by_doubling(piece):
        if seq_size != 16:
            return lax.all_gather(piece, "seq", axis=0, tiled=True)
        value = piece
        for number, bit in enumerate((8, 4, 2, 1)):
            met = lax.ppermute(value, "seq", [(i, i ^ bit) for i in range(seq_size)])
            low = position // bit % 2 == 0
            value = jnp.stack(
                [jnp.where(low, value, met), jnp.where(low, met, value)], axis=number
            )
        return value.reshape(-1, piece.shape[1])

    def sum_small(value):
        bit = 1
        while bit < seq_size:
            value = value + lax.ppermute(value, "seq", [(i, i ^ bit) for i in range(seq_size)])
            bit *= 2
        return value

    middle = scatter(middle)
    adapters = gather_by_doubling(middle[:, 5 * local_width :]).astype(F32)
    cross_out_t, self_out_t, cross_query_g, cross_key_g, cross_value_g = jnp.split(
        middle[:, : 5 * local_width].astype(F32), 5, axis=1
    )
    self_query_g, self_key_g, self_value_g = jnp.split(
        scatter_by_halves(self_parts).astype(F32), 3, axis=1
    )
    small = sum_small(
        jnp.stack(
            [
                grad_gain_one,
                grad_bias_one,
                grad_gain_two,
                grad_bias_two,
                grad_gain_three,
                grad_bias_three,
            ]
        )
    )
    half = adapter_up.shape[0]
    return (
        normed_three.reshape(pack_count, row_count, model_width),
        grad_inputs.reshape(pack_count, row_count, model_width),
        grad_source.reshape(pack_count, source_rows, model_width),
        self_query_g,
        self_key_g,
        self_value_g,
        self_out_t.T,
        cross_query_g,
        cross_key_g,
        cross_value_g,
        cross_out_t.T,
        adapters[:, half:],
        adapters[:, :half].T,
        small[0],
        small[1],
        small[2],
        small[3],
        small[4],
        small[5],
    )


def contract_t(weight):
    return weight.T


def solution(mesh):
    placed = (
        P(None, "seq", None),
        P(None, "seq", None),
        P(),
        P(),
        P(None, "head"),
        P(None, "head"),
        P(None, "head"),
        P("head", None),
        P(None, "head"),
        P(None, "head"),
        P(None, "head"),
        P("head", None),
        P(None, "head"),
        P("head", None),
        P(None, "head"),
        P("head", None),
        P(),
        P(),
        P(),
        P(),
        P(),
        P(),
        P(None, "seq", None),
    )
    return jax.shard_map(
        functools.partial(on_device, mesh.shape["seq"], mesh.shape["head"]),
        mesh=mesh,
        in_specs=placed,
        out_specs=(
            P(None, "seq", None),
            P(None, "seq", None),
            P(None, "seq", None),
            P("seq", "head"),
            P("seq", "head"),
            P("seq", "head"),
            P("head", "seq"),
            P("seq", "head"),
            P("seq", "head"),
            P("seq", "head"),
            P("head", "seq"),
            P(None, "head"),
            P("head", None),
            P(),
            P(),
            P(),
            P(),
            P(),
            P(),
        ),
        check_vma=False,
    )
```

```python
import functools

import jax
import jax.numpy as jnp
from jax import lax
from jax.experimental import pallas as pl
from jax.experimental.pallas import tpu as pltpu
from jax.sharding import PartitionSpec as P

HEAD_DIM = 64
PAIR = 2 * HEAD_DIM
STATS = 16
LOWEST = -1e29
EXCLUDED = -1e30
F32 = jnp.float32
BF16 = jnp.bfloat16


def matrix_product(left, right):
    return jnp.dot(left, right, preferred_element_type=F32)


def contract(left, right, left_dim, right_dim):
    return lax.dot_general(
        left, right, (((left_dim,), (right_dim,)), ((), ())), preferred_element_type=F32
    )


def times_transposed(left, right):
    return contract(left, right, 1, 1)


def transposed_times(left, right):
    return contract(left, right, 0, 0)


class Shape:
    def __init__(self, chips, groups, packs, rows, source_rows, starts, causal):
        self.chips, self.groups, self.packs, self.rows = chips, groups, packs, rows
        self.source_rows, self.starts, self.causal = source_rows, starts, causal
        self.step = groups
        while self.step > 1 and self.step * source_rows > 768:
            self.step //= 2
        self.steps = groups // self.step
        self.tile = 2 * rows
        self.length = 2 * chips * rows
        self.source_length = 2 * chips * source_rows


def position_range(shape, places, pack, target_bounds, source_bounds):
    starts = shape.starts
    low = jnp.zeros_like(places)
    high = jnp.zeros_like(places) + source_bounds[pack * starts]
    for entry in range(starts):
        later = places >= target_bounds[pack * starts + entry]
        low = jnp.where(later, source_bounds[pack * starts + entry], low)
        if entry + 1 < starts:
            following = source_bounds[pack * starts + entry + 1]
        else:
            following = jnp.int32(shape.source_length)
        high = jnp.where(later, following, high)
    if shape.causal:
        high = places + 1
    return low, high


def lane_places(shape, chip, core):
    lanes = lax.broadcasted_iota(jnp.int32, (1, shape.tile), 1)
    own = (2 * chip + core) * shape.rows + lanes
    other = (2 * chip + 1 - core) * shape.rows + lanes - shape.rows
    return jnp.where(lanes < shape.rows, own, other)


def step_conditions(shape, chip, pack, first_group, place, target_bounds, source_bounds):
    base, core = place[0], place[1]
    head = chip * (2 * shape.rows)
    tail = head + 2 * shape.rows - 1
    low_first, high_first = position_range(shape, head, pack, target_bounds, source_bounds)
    low_last, high_last = position_range(shape, tail, pack, target_bounds, source_bounds)
    begin = (base + 2 * first_group + core) * shape.source_rows
    end = begin + (2 * shape.step - 1) * shape.source_rows
    some = jnp.logical_and(low_first < end, high_last > begin)
    whole = jnp.logical_and(low_last <= begin, high_first >= end)
    return begin, some, whole


def source_places(shape, begin):
    size = shape.step * shape.source_rows
    rows = lax.broadcasted_iota(jnp.int32, (size, shape.tile), 0)
    places = begin + rows
    for group in range(1, shape.step):
        places = places + jnp.where(rows >= group * shape.source_rows, shape.source_rows, 0)
    return places


def both(own_ref, other_ref, chip, first, last, pack, rows):
    lanes = slice(pack * rows, (pack + 1) * rows)
    return jnp.concatenate(
        [own_ref[chip, first:last, lanes], other_ref[chip, first:last, lanes]], axis=1
    )


def one_head(pair_rows, head):
    feature = lax.broadcasted_iota(jnp.int32, pair_rows.shape, 0)
    mine = (feature >= HEAD_DIM) if head else (feature < HEAD_DIM)
    return jnp.where(mine, pair_rows, jnp.zeros_like(pair_rows))


def split_low(value):
    high = value.astype(BF16).astype(F32)
    return high, value - high


def split_parts(value):
    high = lax.reduce_precision(value, 8, 7)
    return high, value - high


def stat_rows(rows, width):
    index = lax.broadcasted_iota(jnp.int32, (STATS, width), 0)
    total = jnp.zeros((STATS, width), F32)
    for number, row in enumerate(rows):
        total = jnp.where(index == number, row, total)
    return total.astype(BF16)


def forward_kernel(
    shape, target_bounds, source_bounds, place, own_q, other_q, keys_values, own_out, other_out,
    value_t, maxima, total,
):
    step_rows = shape.step * shape.source_rows
    for group in range(shape.groups):
        for pack in range(shape.packs):
            part = slice(pack * shape.source_rows, (pack + 1) * shape.source_rows)
            lanes = slice(group * shape.source_rows, (group + 1) * shape.source_rows)
            turned = keys_values[group, 1, part, :].T
            for head in range(2):
                value_t[pack, head, :HEAD_DIM, lanes] = turned[head * HEAD_DIM : (head + 1) * HEAD_DIM]
    value_t[:, :, HEAD_DIM:, :] = jnp.ones((shape.packs, 2, STATS, value_t.shape[3]), BF16)

    for pack in range(shape.packs):
        part = slice(pack * shape.source_rows, (pack + 1) * shape.source_rows)

        def per_chip(chip, unused, pack=pack, part=part):
            query = both(own_q, other_q, chip, 0, PAIR, pack, shape.rows)
            low, high = position_range(
                shape, lane_places(shape, chip, place[1]), pack, target_bounds, source_bounds
            )
            maxima[...] = jnp.full_like(maxima, LOWEST)
            total[...] = jnp.zeros_like(total)
            for step in range(shape.steps):
                groups = slice(step * shape.step, (step + 1) * shape.step)
                begin, some, whole = step_conditions(
                    shape, chip, pack, step * shape.step, place, target_bounds, source_bounds
                )

                def fold(masked, step=step, groups=groups, begin=begin):
                    key_rows = keys_values[groups, 0, part, :].reshape(step_rows, PAIR)
                    if masked:
                        places = source_places(shape, begin)
                        allowed = jnp.logical_and(places >= low, places < high)
                    befores = [maxima[head : head + 1, :] for head in range(2)]
                    scores = [matrix_product(key_rows, one_head(query, head)) for head in range(2)]
                    if masked:
                        scores = [jnp.where(allowed, score, EXCLUDED) for score in scores]
                    nows = [
                        jnp.maximum(before, jnp.max(score, axis=0, keepdims=True))
                        for before, score in zip(befores, scores)
                    ]
                    weights = [jnp.exp(score - now) for score, now in zip(scores, nows)]
                    products = []
                    for head in range(2):
                        values = value_t[pack, head, :, step * step_rows : (step + 1) * step_rows]
                        products.append(matrix_product(values, weights[head].astype(BF16)))
                    for head in range(2):
                        fading = jnp.exp(befores[head] - nows[head])
                        maxima[head : head + 1, :] = nows[head]
                        total[head] = total[head] * fading + products[head]

                pl.when(jnp.logical_and(some, whole))(functools.partial(fold, False))
                pl.when(jnp.logical_and(some, jnp.logical_not(whole)))(
                    functools.partial(fold, True)
                )
            statistics = []
            for head in range(2):
                features = slice(head * HEAD_DIM, (head + 1) * HEAD_DIM)
                found = total[head, HEAD_DIM : HEAD_DIM + 1, :]
                divisor = jnp.maximum(found, 1e-37)
                filled = found > 0.0
                logs = jnp.where(filled, maxima[head : head + 1, :] + jnp.log(divisor), LOWEST)
                statistics.extend(split_low(logs))
                result = (total[head, :HEAD_DIM, :] / divisor).astype(BF16)
                for ref, offset in ((own_out, 0), (other_out, shape.rows)):
                    ref[chip, features, pack * shape.rows : (pack + 1) * shape.rows] = result[
                        :, offset : offset + shape.rows
                    ]
            statistics = stat_rows(statistics, shape.tile)
            for ref, offset in ((own_out, 0), (other_out, shape.rows)):
                ref[chip, PAIR : PAIR + STATS, pack * shape.rows : (pack + 1) * shape.rows] = (
                    statistics[:, offset : offset + shape.rows]
                )
            return 0

        lax.fori_loop(0, shape.chips, per_chip, 0)


def backward_kernel(
    shape, target_bounds, source_bounds, place, own_q, other_q, own_g, other_g, keys_values,
    own_dq, other_dq, key_grads, key_t, grad_key, grad_value, grad_query,
):
    step_rows = shape.step * shape.source_rows
    grad_key[...] = jnp.zeros_like(grad_key)
    grad_value[...] = jnp.zeros_like(grad_value)
    for group in range(shape.groups):
        for pack in range(shape.packs):
            part = slice(pack * shape.source_rows, (pack + 1) * shape.source_rows)
            key_t[pack, :, group * shape.source_rows : (group + 1) * shape.source_rows] = (
                keys_values[group, 0, part, :].T
            )

    for pack in range(shape.packs):
        part = slice(pack * shape.source_rows, (pack + 1) * shape.source_rows)

        def per_chip(chip, unused, pack=pack, part=part):
            query = both(own_q, other_q, chip, 0, PAIR, pack, shape.rows)
            grads = both(own_g, other_g, chip, 0, PAIR, pack, shape.rows)
            statistics = both(own_g, other_g, chip, PAIR, PAIR + STATS, pack, shape.rows).astype(F32)
            low, high = position_range(
                shape, lane_places(shape, chip, place[1]), pack, target_bounds, source_bounds
            )
            queries = [one_head(query, head) for head in range(2)]
            gradients = [one_head(grads, head) for head in range(2)]
            log_rows = [statistics[2 * head : 2 * head + 1] + statistics[2 * head + 1 : 2 * head + 2] for head in range(2)]
            deltas = [statistics[2 * head + 4 : 2 * head + 5] + statistics[2 * head + 5 : 2 * head + 6] for head in range(2)]
            grad_query[...] = jnp.zeros_like(grad_query)
            for step in range(shape.steps):
                groups = slice(step * shape.step, (step + 1) * shape.step)
                begin, some, whole = step_conditions(
                    shape, chip, pack, step * shape.step, place, target_bounds, source_bounds
                )

                def fold(masked, step=step, groups=groups, begin=begin):
                    key_rows = keys_values[groups, 0, part, :].reshape(step_rows, PAIR)
                    value_rows = keys_values[groups, 1, part, :].reshape(step_rows, PAIR)
                    if masked:
                        places = source_places(shape, begin)
                        allowed = jnp.logical_and(places >= low, places < high)
                    lanes = slice(step * step_rows, (step + 1) * step_rows)
                    scores = [matrix_product(key_rows, queries[head]) for head in range(2)]
                    changes = [matrix_product(value_rows, gradients[head]) for head in range(2)]
                    if masked:
                        scores = [jnp.where(allowed, score, EXCLUDED) for score in scores]
                    weights = [jnp.exp(score - row) for score, row in zip(scores, log_rows)]
                    diffs = [
                        (weight * (change - delta)).astype(BF16)
                        for weight, change, delta in zip(weights, changes, deltas)
                    ]
                    key_part = times_transposed(
                        jnp.concatenate(diffs, axis=1), jnp.concatenate(queries, axis=1)
                    )
                    value_part = times_transposed(
                        jnp.concatenate([weight.astype(BF16) for weight in weights], axis=1),
                        jnp.concatenate(gradients, axis=1),
                    )
                    query_parts = [
                        matrix_product(
                            key_t[pack, head * HEAD_DIM : (head + 1) * HEAD_DIM, lanes], diffs[head]
                        )
                        for head in range(2)
                    ]
                    grad_query[...] += jnp.concatenate(query_parts, axis=0)
                    grad_key[pack, lanes, :] += key_part
                    grad_value[pack, lanes, :] += value_part

                pl.when(jnp.logical_and(some, whole))(functools.partial(fold, False))
                pl.when(jnp.logical_and(some, jnp.logical_not(whole)))(
                    functools.partial(fold, True)
                )
            result = (grad_query[...] * HEAD_DIM**-0.5).astype(BF16)
            for ref, offset in ((own_dq, 0), (other_dq, shape.rows)):
                ref[chip, :, pack * shape.rows : (pack + 1) * shape.rows] = result[
                    :, offset : offset + shape.rows
                ]
            return 0

        lax.fori_loop(0, shape.chips, per_chip, 0)

    for group in range(shape.groups):
        for pack in range(shape.packs):
            part = slice(pack * shape.source_rows, (pack + 1) * shape.source_rows)
            lanes = slice(group * shape.source_rows, (group + 1) * shape.source_rows)
            key_grads[group, 0, part, :] = grad_key[pack, lanes, :].astype(BF16)
            key_grads[group, 1, part, :] = grad_value[pack, lanes, :].astype(BF16)


def smem():
    return pl.BlockSpec(memory_space=pltpu.SMEM)


def vmem():
    return pl.BlockSpec(memory_space=pltpu.VMEM)


PARAMS = dict(vmem_limit_bytes=16 * 1024 * 1024)


def attention_forward(shape, bounds, place, own_q, other_q, keys_values):
    width = shape.packs * shape.rows
    pairs = shape.packs * shape.length * shape.groups * shape.source_rows
    message = jax.ShapeDtypeStruct((shape.chips, PAIR + STATS, width), BF16)
    return pl.pallas_call(
        functools.partial(forward_kernel, shape),
        out_shape=(message, message),
        in_specs=[smem()] * 3 + [vmem()] * 3,
        out_specs=(vmem(), vmem()),
        scratch_shapes=[
            pltpu.VMEM((shape.packs, 2, HEAD_DIM + STATS, shape.groups * shape.source_rows), BF16),
            pltpu.VMEM((8, shape.tile), F32),
            pltpu.VMEM((2, HEAD_DIM + STATS, shape.tile), F32),
        ],
        compiler_params=pltpu.CompilerParams(**PARAMS),
        cost_estimate=pl.CostEstimate(
            flops=8 * pairs * HEAD_DIM, bytes_accessed=6 * 1024 * 1024, transcendentals=2 * pairs
        ),
    )(bounds[0], bounds[1], place, own_q, other_q, keys_values)


def attention_backward(shape, bounds, place, own_q, other_q, own_g, other_g, keys_values):
    width = shape.packs * shape.rows
    pairs = shape.packs * shape.length * shape.groups * shape.source_rows
    source = shape.groups * shape.source_rows
    message = jax.ShapeDtypeStruct((shape.chips, PAIR, width), BF16)
    return pl.pallas_call(
        functools.partial(backward_kernel, shape),
        out_shape=(message, message, jax.ShapeDtypeStruct(keys_values.shape, BF16)),
        in_specs=[smem()] * 3 + [vmem()] * 5,
        out_specs=(vmem(), vmem(), vmem()),
        scratch_shapes=[
            pltpu.VMEM((shape.packs, PAIR, source), BF16),
            pltpu.VMEM((shape.packs, source, PAIR), F32),
            pltpu.VMEM((shape.packs, source, PAIR), F32),
            pltpu.VMEM((PAIR, shape.tile), F32),
        ],
        compiler_params=pltpu.CompilerParams(**PARAMS),
        cost_estimate=pl.CostEstimate(
            flops=20 * pairs * HEAD_DIM, bytes_accessed=8 * 1024 * 1024, transcendentals=2 * pairs
        ),
    )(bounds[0], bounds[1], place, own_q, other_q, own_g, other_g, keys_values)


class RowShape:
    def __init__(self, chips, rows, starts):
        self.chips, self.rows, self.starts = chips, rows, starts
        self.source_length, self.causal = 2 * chips * rows, True
        self.span = 2 if chips % 2 == 0 else 1
        self.tiles = chips // self.span
        self.tile = self.span * rows
        self.step = 2 * self.span * rows


def own_places(shape, tile, core):
    lanes = lax.broadcasted_iota(jnp.int32, (1, shape.tile), 1)
    places = 2 * tile * shape.span * shape.rows + core * shape.rows + lanes
    for block in range(1, shape.span):
        places = places + jnp.where(lanes >= block * shape.rows, shape.rows, 0)
    return places


def chip_places(shape, step, core):
    rows = lax.broadcasted_iota(jnp.int32, (shape.step, shape.tile), 0)
    places = step * shape.step + rows
    for block in range(2 * shape.span):
        here = jnp.logical_and(rows >= block * shape.rows, rows < (block + 1) * shape.rows)
        shift = shape.rows * core if block % 2 == 0 else -shape.rows * core
        places = places + jnp.where(here, shift, 0)
    return places


def row_conditions(shape, tile, step, pack, bounds):
    head = tile * shape.step
    tail = head + shape.step - 1
    begin = step * shape.step
    end = begin + shape.step
    low_first, _ = position_range(shape, head, pack, bounds, bounds)
    low_last, _ = position_range(shape, tail, pack, bounds, bounds)
    some = low_first < end
    whole = jnp.logical_and(low_last <= begin, end <= head + 1)
    return some, whole


def fill_rows(shape, own_kv, other_kv, which, target, transposed):
    for chip in range(shape.chips):
        for side, ref in enumerate((own_kv, other_kv)):
            first = (2 * chip + side) * shape.rows
            block = ref[chip, which]
            if transposed and len(target.shape) == 3:
                for head in range(2):
                    target[head, :HEAD_DIM, first : first + shape.rows] = block.T[
                        head * HEAD_DIM : (head + 1) * HEAD_DIM
                    ]
            elif transposed:
                target[:, first : first + shape.rows] = block.T
            else:
                target[first : first + shape.rows, :] = block


def tile_lanes(ref, tile, span):
    return jnp.concatenate([ref[tile * span + block] for block in range(span)], axis=1)


def row_forward_kernel(
    shape, bounds, place, queries, own_kv, other_kv, out, logs, key_all, value_t, maxima, total
):
    pack, core = place[0], place[1]
    fill_rows(shape, own_kv, other_kv, 0, key_all, False)
    fill_rows(shape, own_kv, other_kv, 1, value_t, True)
    value_t[:, HEAD_DIM:, :] = jnp.ones((2, STATS, value_t.shape[2]), BF16)

    def per_tile(tile, unused):
        query = tile_lanes(queries, tile, shape.span)
        low, high = position_range(shape, own_places(shape, tile, core), pack, bounds, bounds)
        heads = [one_head(query, head) for head in range(2)]
        maxima[...] = jnp.full_like(maxima, LOWEST)
        total[...] = jnp.zeros_like(total)

        def per_step(step, unused):
            some, whole = row_conditions(shape, tile, step, pack, bounds)
            first = pl.multiple_of(step * shape.step, shape.step)

            def fold(masked):
                key_rows = key_all[pl.ds(first, shape.step), :]
                if masked:
                    places = chip_places(shape, step, core)
                    allowed = jnp.logical_and(places >= low, places < high)
                befores = [maxima[head : head + 1, :] for head in range(2)]
                scores = [matrix_product(key_rows, heads[head]) for head in range(2)]
                if masked:
                    scores = [jnp.where(allowed, score, EXCLUDED) for score in scores]
                nows = [
                    jnp.maximum(before, jnp.max(score, axis=0, keepdims=True))
                    for before, score in zip(befores, scores)
                ]
                weights = [jnp.exp(score - now) for score, now in zip(scores, nows)]
                products = [
                    matrix_product(value_t[head, :, pl.ds(first, shape.step)], weights[head].astype(BF16))
                    for head in range(2)
                ]
                for head in range(2):
                    fading = jnp.exp(befores[head] - nows[head])
                    maxima[head : head + 1, :] = nows[head]
                    total[head] = total[head] * fading + products[head]

            pl.when(jnp.logical_and(some, whole))(functools.partial(fold, False))
            pl.when(jnp.logical_and(some, jnp.logical_not(whole)))(functools.partial(fold, True))
            return 0

        lax.fori_loop(0, tile + 1, per_step, 0)
        for head in range(2):
            features = slice(head * HEAD_DIM, (head + 1) * HEAD_DIM)
            divisor = total[head, HEAD_DIM : HEAD_DIM + 1, :]
            result = (total[head, :HEAD_DIM, :] / divisor).astype(BF16)
            found = maxima[head : head + 1, :] + jnp.log(divisor)
            for block in range(shape.span):
                lanes = slice(block * shape.rows, (block + 1) * shape.rows)
                out[tile * shape.span + block, features, :] = result[:, lanes]
                logs[tile * shape.span + block, head : head + 1, :] = found[:, lanes]
        return 0

    lax.fori_loop(0, shape.tiles, per_tile, 0)


def row_backward_kernel(
    shape, bounds, place, queries, outputs, logs, grads, own_kv, other_kv,
    query_grads, own_dkv, other_dkv, key_all, value_all, key_t, grad_key, grad_value, grad_query,
):
    pack, core = place[0], place[1]
    fill_rows(shape, own_kv, other_kv, 0, key_all, False)
    fill_rows(shape, own_kv, other_kv, 1, value_all, False)
    fill_rows(shape, own_kv, other_kv, 0, key_t, True)
    grad_key[...] = jnp.zeros_like(grad_key)
    grad_value[...] = jnp.zeros_like(grad_value)

    def per_tile(tile, unused):
        query = tile_lanes(queries, tile, shape.span)
        grad = tile_lanes(grads, tile, shape.span)
        product = grad.astype(F32) * tile_lanes(outputs, tile, shape.span).astype(F32)
        log_rows = tile_lanes(logs, tile, shape.span)
        low, high = position_range(shape, own_places(shape, tile, core), pack, bounds, bounds)
        heads = []
        for head in range(2):
            features = slice(head * HEAD_DIM, (head + 1) * HEAD_DIM)
            delta = jnp.sum(product[features], axis=0, keepdims=True)
            heads.append((one_head(query, head), one_head(grad, head), log_rows[head : head + 1], delta))
        grad_query[...] = jnp.zeros_like(grad_query)

        def per_step(step, unused):
            some, whole = row_conditions(shape, tile, step, pack, bounds)
            first = pl.multiple_of(step * shape.step, shape.step)

            def fold(masked):
                part = pl.ds(first, shape.step)
                key_rows, value_rows = key_all[part, :], value_all[part, :]
                if masked:
                    places = chip_places(shape, step, core)
                    allowed = jnp.logical_and(places >= low, places < high)
                scores = [matrix_product(key_rows, head[0]) for head in heads]
                changes = [matrix_product(value_rows, head[1]) for head in heads]
                if masked:
                    scores = [jnp.where(allowed, score, EXCLUDED) for score in scores]
                weights = [jnp.exp(score - head[2]) for score, head in zip(scores, heads)]
                diffs = [
                    (weight * (change - head[3])).astype(BF16)
                    for weight, change, head in zip(weights, changes, heads)
                ]
                key_part = times_transposed(
                    jnp.concatenate(diffs, axis=1),
                    jnp.concatenate([heads[0][0], heads[1][0]], axis=1),
                )
                value_part = times_transposed(
                    jnp.concatenate([weight.astype(BF16) for weight in weights], axis=1),
                    jnp.concatenate([heads[0][1], heads[1][1]], axis=1),
                )
                query_parts = [
                    matrix_product(key_t[head * HEAD_DIM : (head + 1) * HEAD_DIM, part], diffs[head])
                    for head in range(2)
                ]
                grad_query[...] += jnp.concatenate(query_parts, axis=0)
                grad_key[part, :] += key_part
                grad_value[part, :] += value_part

            pl.when(jnp.logical_and(some, whole))(functools.partial(fold, False))
            pl.when(jnp.logical_and(some, jnp.logical_not(whole)))(functools.partial(fold, True))
            return 0

        lax.fori_loop(0, tile + 1, per_step, 0)
        result = (grad_query[...] * HEAD_DIM**-0.5).astype(BF16)
        for block in range(shape.span):
            query_grads[tile * shape.span + block] = result[
                :, block * shape.rows : (block + 1) * shape.rows
            ]
        return 0

    lax.fori_loop(0, shape.tiles, per_tile, 0)
    for chip in range(shape.chips):
        for side, ref in enumerate((own_dkv, other_dkv)):
            first = (2 * chip + side) * shape.rows
            ref[chip, 0] = grad_key[first : first + shape.rows, :].astype(BF16)
            ref[chip, 1] = grad_value[first : first + shape.rows, :].astype(BF16)


def row_forward(shape, bounds, place, queries, own_kv, other_kv):
    length = shape.source_length
    return pl.pallas_call(
        functools.partial(row_forward_kernel, shape),
        out_shape=(
            jax.ShapeDtypeStruct(queries.shape, BF16),
            jax.ShapeDtypeStruct((shape.chips, 2, shape.rows), F32),
        ),
        in_specs=[smem()] * 2 + [vmem()] * 3,
        out_specs=(vmem(), vmem()),
        scratch_shapes=[
            pltpu.VMEM((length, PAIR), BF16),
            pltpu.VMEM((2, HEAD_DIM + STATS, length), BF16),
            pltpu.VMEM((8, shape.tile), F32),
            pltpu.VMEM((2, HEAD_DIM + STATS, shape.tile), F32),
        ],
        compiler_params=pltpu.CompilerParams(**PARAMS),
        cost_estimate=pl.CostEstimate(
            flops=6 * length * length * HEAD_DIM,
            bytes_accessed=4 * 1024 * 1024,
            transcendentals=length * length,
        ),
    )(bounds, place, queries, own_kv, other_kv)


def row_backward(shape, bounds, place, queries, outputs, logs, grads, own_kv, other_kv):
    length = shape.source_length
    return pl.pallas_call(
        functools.partial(row_backward_kernel, shape),
        out_shape=(
            jax.ShapeDtypeStruct(queries.shape, BF16),
            jax.ShapeDtypeStruct(own_kv.shape, BF16),
            jax.ShapeDtypeStruct(own_kv.shape, BF16),
        ),
        in_specs=[smem()] * 2 + [vmem()] * 6,
        out_specs=(vmem(), vmem(), vmem()),
        scratch_shapes=[
            pltpu.VMEM((length, PAIR), BF16),
            pltpu.VMEM((length, PAIR), BF16),
            pltpu.VMEM((PAIR, length), BF16),
            pltpu.VMEM((length, PAIR), F32),
            pltpu.VMEM((length, PAIR), F32),
            pltpu.VMEM((PAIR, shape.tile), F32),
        ],
        compiler_params=pltpu.CompilerParams(**PARAMS),
        cost_estimate=pl.CostEstimate(
            flops=12 * length * length * HEAD_DIM,
            bytes_accessed=6 * 1024 * 1024,
            transcendentals=length * length,
        ),
    )(bounds, place, queries, outputs, logs, grads, own_kv, other_kv)


def blocks(array):
    return pl.BlockSpec(array.shape, lambda step, zeros=(0,) * array.ndim: zeros)


def call(kernel, out_shape, args, grid=None, in_specs=None, out_specs=None, scratch=(), flops=0):
    if in_specs is None:
        in_specs = [vmem()] * len(args)
    if out_specs is None:
        out_specs = jax.tree.map(lambda _: vmem(), out_shape)
    extra = {} if grid is None else {"grid": grid}
    return pl.pallas_call(
        kernel,
        out_shape=out_shape,
        in_specs=in_specs,
        out_specs=out_specs,
        scratch_shapes=list(scratch),
        compiler_params=pltpu.CompilerParams(**PARAMS),
        cost_estimate=pl.CostEstimate(flops=flops, bytes_accessed=8 << 20, transcendentals=0),
        **extra,
    )(*args)


def project_self(x, wq, wk, wv, packs):
    rows, width = x.shape[0], wq.shape[1]
    pairs, each = width // PAIR, rows // packs

    def kernel(x_ref, wq_ref, wk_ref, wv_ref, out):
        value = x_ref[...]
        query = (matrix_product(value, wq_ref[...]) * HEAD_DIM**-0.5).astype(BF16)
        for pack in range(packs):
            for pair in range(pairs):
                part = query[pack * each : (pack + 1) * each, pair * PAIR : (pair + 1) * PAIR]
                out[pack * pairs + pair, 0] = part.T
        for number, ref in ((1, wk_ref), (2, wv_ref)):
            result = matrix_product(value, ref[...]).astype(BF16)
            for pack in range(packs):
                for pair in range(pairs):
                    out[pack * pairs + pair, number] = result[
                        pack * each : (pack + 1) * each, pair * PAIR : (pair + 1) * PAIR
                    ]

    return call(
        kernel,
        jax.ShapeDtypeStruct((packs * pairs, 3, each, PAIR), BF16),
        (x, wq, wk, wv),
        flops=6 * rows * x.shape[1] * width,
    )


def project_sources(x, wk, wv):
    rows, depth = x.shape
    pairs = wk.shape[1] // PAIR
    size = rows // 3 if rows % 48 == 0 else rows

    def kernel(x_ref, wk_ref, wv_ref, out):
        for number, ref in enumerate((wk_ref, wv_ref)):
            result = matrix_product(x_ref[...], ref[...]).astype(BF16)
            for pair in range(pairs):
                out[pair, number] = result[:, pair * PAIR : (pair + 1) * PAIR]

    return call(
        kernel,
        jax.ShapeDtypeStruct((pairs, 2, rows, PAIR), BF16),
        (x, wk, wv),
        grid=(rows // size,),
        in_specs=[pl.BlockSpec((size, depth), lambda i: (i, 0)), blocks(wk), blocks(wv)],
        out_specs=pl.BlockSpec((pairs, 2, size, PAIR), lambda i: (0, 0, i, 0)),
        flops=4 * rows * depth * wk.shape[1],
    )


def source_grads(grads, wk, wv):
    pairs, _, rows, _ = grads.shape
    size = rows // 3 if rows % 48 == 0 else rows
    depth = wk.shape[0]

    def kernel(grads_ref, wk_ref, wv_ref, out):
        keys = jnp.concatenate([grads_ref[pair, 0] for pair in range(pairs)], axis=1)
        values = jnp.concatenate([grads_ref[pair, 1] for pair in range(pairs)], axis=1)
        total = times_transposed(keys, wk_ref[...]) + times_transposed(values, wv_ref[...])
        out[...] = total.astype(BF16)

    return call(
        kernel,
        jax.ShapeDtypeStruct((rows, depth), BF16),
        (grads, wk, wv),
        grid=(rows // size,),
        in_specs=[
            pl.BlockSpec((pairs, 2, size, PAIR), lambda i: (0, 0, i, 0)),
            blocks(wk),
            blocks(wv),
        ],
        out_specs=pl.BlockSpec((size, depth), lambda i: (i, 0)),
        flops=4 * rows * depth * wk.shape[1],
    )


def input_grads(back, wq, wk, wv, packs):
    pairs = back.shape[0] // packs
    each = PAIR
    depth = wq.shape[0]

    def kernel(back_ref, wq_ref, wk_ref, wv_ref, out):
        for pack in range(packs):
            first = pack * pairs
            parts = [
                jnp.concatenate([back_ref[first + pair, 0 * PAIR : 1 * PAIR].T for pair in range(pairs)], axis=1),
                jnp.concatenate([back_ref[first + pair, 1 * PAIR : 2 * PAIR] for pair in range(pairs)], axis=1),
                jnp.concatenate([back_ref[first + pair, 2 * PAIR : 3 * PAIR] for pair in range(pairs)], axis=1),
            ]
            total = times_transposed(parts[0], wq_ref[...])
            total += times_transposed(parts[1], wk_ref[...])
            total += times_transposed(parts[2], wv_ref[...])
            out[pack * each : (pack + 1) * each, :] = total.astype(BF16)

    return call(
        kernel,
        jax.ShapeDtypeStruct((packs * each, depth), BF16),
        (back, wq, wk, wv),
        flops=6 * packs * each * depth * wq.shape[1],
    )


def self_weight_grads(x, back, packs, core):
    pairs = back.shape[0] // packs
    rows, depth = x.shape
    width = pairs * PAIR
    chips = back.shape[0]
    small = depth // (2 * chips)

    def kernel(core_ref, x_ref, back_ref, keep, send, turned):
        turned[...] = x_ref[...].T.reshape(turned.shape)
        mine = core_ref[0]
        for which, out in ((mine, keep), (1 - mine, send)):
            value = jnp.concatenate([turned[2 * chip + which] for chip in range(chips)], axis=0)
            for number in range(3):
                parts = []
                for pair in range(pairs):
                    here = slice(number * PAIR, (number + 1) * PAIR)
                    found = [back_ref[pack * pairs + pair, here] for pack in range(packs)]
                    parts.append(jnp.concatenate(found, axis=1 if number == 0 else 0))
                if number == 0:
                    result = times_transposed(value, jnp.concatenate(parts, axis=0))
                else:
                    result = matrix_product(value, jnp.concatenate(parts, axis=1))
                out[:, :, number * width : (number + 1) * width] = result.astype(BF16).reshape(
                    chips, small, width
                )

    shape = jax.ShapeDtypeStruct((chips, small, 3 * width), BF16)
    return call(
        kernel,
        (shape, shape),
        (core.reshape(1), x, back),
        in_specs=[smem(), vmem(), vmem()],
        scratch=[pltpu.VMEM((2 * chips, small, rows), BF16)],
        flops=2 * rows * depth * 3 * width,
    )


def halve(values, mine, axes, cuts):
    flat = [array for group in values for array in group]
    outs = []
    for group, axis, cut in zip(values, axes, cuts):
        shape = list(group[0].shape)
        del shape[axis]
        shape[-1] = cut[1] - cut[0]
        outs.extend([jax.ShapeDtypeStruct(tuple(shape), F32), jax.ShapeDtypeStruct(tuple(shape), BF16)])

    def kernel(mine_ref, *refs):
        sources, targets = refs[: len(flat)], refs[len(flat) :]
        first = 0
        for number, (group, axis, cut) in enumerate(zip(values, axes, cuts)):
            refs_here = sources[first : first + len(group)]
            first += len(group)
            which = mine_ref[number]
            for index, target in ((which, targets[2 * number]), (1 - which, targets[2 * number + 1])):
                place = (slice(None),) * axis + (index, Ellipsis, slice(*cut))
                total = sum(ref[place].astype(F32) for ref in refs_here)
                target[...] = total.astype(target.dtype)

    found = call(
        kernel,
        tuple(outs),
        (jnp.stack(mine).astype(jnp.int32), *flat),
        in_specs=[smem()] + [vmem()] * len(flat),
    )
    return list(zip(found[0::2], found[1::2]))


def last_sums(first, second, pieces):
    rows, half = first[0].shape
    width = 2 * half // pieces

    def kernel(*refs):
        left = refs[0][...] + refs[1][...].astype(F32)
        right = refs[2][...] + refs[3][...].astype(F32)
        whole = jnp.concatenate([left, right], axis=1)
        for number, out in enumerate(refs[4:]):
            out[...] = whole[:, number * width : (number + 1) * width]

    return call(
        kernel,
        tuple(jax.ShapeDtypeStruct((rows, width), F32) for _ in range(pieces)),
        (*first, *second),
    )


def spread_adapters(gathered, half):
    depth = gathered.shape[0]

    def kernel(source, up, down, sums):
        up[...] = source[:, :half].T.astype(F32)
        down[...] = source[:, half : 2 * half].astype(F32)
        sums[...] = source[:, 2 * half :].T[:4].astype(F32)

    return call(
        kernel,
        (
            jax.ShapeDtypeStruct((half, depth), F32),
            jax.ShapeDtypeStruct((depth, half), F32),
            jax.ShapeDtypeStruct((4, depth), F32),
        ),
        (gathered,),
    )


def spread_middle(early, middle):
    rows, width = early.shape

    def kernel(early_ref, middle_ref, cross_out, self_out, query, key, value):
        cross_out[...] = early_ref[...].astype(F32).T
        self_out[...] = middle_ref[:, :width].astype(F32).T
        for number, ref in enumerate((query, key, value)):
            ref[...] = middle_ref[:, (number + 1) * width : (number + 2) * width].astype(F32)

    turned, straight = jax.ShapeDtypeStruct((width, rows), F32), jax.ShapeDtypeStruct((rows, width), F32)
    return call(kernel, (turned, turned, straight, straight, straight), (early, middle))


GELU_ROOT = 0.7978845608028654
GELU_CUBE = 0.044715


def gelu_and_slope(value):
    square = value * value
    bend = jnp.tanh(GELU_ROOT * (value + GELU_CUBE * value * square))
    slope = 0.5 * (1.0 + bend) + 0.5 * value * (1.0 - bend * bend) * GELU_ROOT * (
        1.0 + 3.0 * GELU_CUBE * square
    )
    return 0.5 * value * (1.0 + bend), slope


def row(vector):
    return vector.reshape(1, -1)


def whole_sum(pair):
    return pair[0][...].astype(F32) + pair[1][...].astype(F32)


def normed(values):
    average = jnp.mean(values, axis=-1, keepdims=True)
    centred = values - average
    scale = lax.rsqrt(jnp.mean(centred * centred, axis=-1, keepdims=True) + 1e-05)
    return centred * scale, scale


def norm_rows_back(unit, scale, gain, grad, sums_ref):
    scaled = grad * gain
    first = jnp.mean(scaled, axis=-1, keepdims=True)
    second = jnp.mean(scaled * unit, axis=-1, keepdims=True)
    sums_ref[0:1, :] = jnp.sum(grad * unit, axis=0, keepdims=True)
    sums_ref[1:2, :] = jnp.sum(grad, axis=0, keepdims=True)
    return (scaled - first - unit * second) * scale


def first_norm(inputs, part, met, gain, bias, query_weight):
    rows, depth = inputs.shape
    pairs = query_weight.shape[1] // PAIR

    def kernel(inputs_ref, part_ref, met_ref, gain_ref, bias_ref, weight_ref, one, scale_ref, out):
        unit, scale = normed(inputs_ref[...].astype(F32) + whole_sum((part_ref, met_ref)))
        value = unit * gain_ref[...] + bias_ref[...]
        one[...], scale_ref[...] = value, scale
        query = (matrix_product(value.astype(BF16), weight_ref[...]).astype(BF16).astype(F32) * HEAD_DIM**-0.5).astype(BF16)
        for pair in range(pairs):
            out[pair] = query[:, pair * PAIR : (pair + 1) * PAIR].T

    return call(
        kernel,
        (
            jax.ShapeDtypeStruct((rows, depth), F32),
            jax.ShapeDtypeStruct((rows, 1), F32),
            jax.ShapeDtypeStruct((pairs, PAIR, rows), BF16),
        ),
        (inputs, part, met, row(gain), row(bias), query_weight),
        flops=2 * rows * depth * pairs * PAIR,
    )


def feed_forward(one, part, met, gain, bias, ffn_in, ffn_out, down, up):
    rows, depth = one.shape
    hidden, narrow_width = ffn_in.shape[1], down.shape[1]
    size = 512 if hidden % 512 == 0 else hidden
    steps = hidden // size

    def kernel(
        one_ref, part_ref, met_ref, gain_ref, bias_ref, in_ref, out_ref, down_ref, up_ref,
        two, scale_ref, slope_ref, narrow_ref, narrow_slope_ref, branch,
    ):
        unit, scale = normed(one_ref[...] + whole_sum((part_ref, met_ref)))
        value = unit * gain_ref[...] + bias_ref[...]
        rounded = value.astype(BF16)
        two[...], scale_ref[...] = value, scale
        act, slope = gelu_and_slope(matrix_product(rounded, down_ref[...]))
        narrow_ref[...] = act.astype(BF16)
        narrow_slope_ref[...] = slope.astype(BF16)
        total = 4.0 * matrix_product(act.astype(BF16), up_ref[...])
        for step in range(steps):
            part = slice(step * size, (step + 1) * size)
            act, slope = gelu_and_slope(matrix_product(rounded, in_ref[:, part]))
            slope_ref[:, part] = slope.astype(BF16)
            total += matrix_product(act.astype(BF16), out_ref[part, :])
        branch[...] = total.astype(BF16)

    args = (one, part, met, row(gain), row(bias), ffn_in, ffn_out, down, up)
    outs = (
        jax.ShapeDtypeStruct((rows, depth), F32),
        jax.ShapeDtypeStruct((rows, 1), F32),
        jax.ShapeDtypeStruct((rows, hidden), BF16),
        jax.ShapeDtypeStruct((rows, narrow_width), BF16),
        jax.ShapeDtypeStruct((rows, narrow_width), BF16),
        jax.ShapeDtypeStruct((rows, depth), BF16),
    )
    return call(kernel, outs, args, flops=4 * rows * depth * hidden)


def feed_backward(two, part, met, gain, bias, cotangent, slope, narrow_slope, ffn_in, ffn_out, down, up):
    rows, depth = two.shape
    hidden, narrow_width = ffn_in.shape[1], down.shape[1]
    size = 512 if hidden % 512 == 0 else hidden
    steps = hidden // size

    def kernel(
        two_ref, part_ref, met_ref, gain_ref, bias_ref, grad_ref, slope_ref, narrow_slope_ref,
        in_ref, out_ref, down_ref, up_ref, output, third, dnarrow, sums, share,
    ):
        unit, scale = normed(two_ref[...] + whole_sum((part_ref, met_ref)))
        output[...] = unit * gain_ref[...] + bias_ref[...]
        value = norm_rows_back(unit, scale, gain_ref[...], grad_ref[...].astype(F32), sums)
        rounded = value.astype(BF16)
        third[...] = value
        narrow = 4.0 * times_transposed(rounded, up_ref[...])
        narrow = (narrow * narrow_slope_ref[...].astype(F32)).astype(BF16)
        dnarrow[...] = narrow
        total = times_transposed(narrow, down_ref[...])
        for step in range(steps):
            part = slice(step * size, (step + 1) * size)
            grads = times_transposed(rounded, out_ref[part, :]) * slope_ref[:, part].astype(F32)
            total += times_transposed(grads.astype(BF16), in_ref[:, part])
        share[...] = total.astype(BF16)

    args = (two, part, met, row(gain), row(bias), cotangent, slope, narrow_slope, ffn_in, ffn_out, down, up)
    outs = (
        jax.ShapeDtypeStruct((rows, depth), F32),
        jax.ShapeDtypeStruct((rows, depth), F32),
        jax.ShapeDtypeStruct((rows, narrow_width), BF16),
        jax.ShapeDtypeStruct((2, depth), F32),
        jax.ShapeDtypeStruct((rows, depth), BF16),
    )
    return call(kernel, outs, args, flops=4 * rows * depth * hidden)


def second_norm_back(third, part, met, two, scale, gain, bias, weight, attended, logs):
    rows, depth = third.shape
    pairs = weight.shape[0] // PAIR

    def kernel(
        third_ref, part_ref, met_ref, two_ref, scale_ref, gain_ref, bias_ref, weight_ref, attended_ref, logs_ref,
        second, sums, out,
    ):
        grad = third_ref[...] + whole_sum((part_ref, met_ref))
        unit = (two_ref[...] - bias_ref[...]) * (1.0 / gain_ref[...])
        value = norm_rows_back(unit, scale_ref[...], gain_ref[...], grad, sums)
        second[...] = value
        grads = times_transposed(weight_ref[...], value.astype(BF16)).astype(BF16)
        for pair in range(pairs):
            low = grads[pair * PAIR : (pair + 1) * PAIR]
            out[pair, :PAIR, :] = low
            low = low.astype(F32)
            first, later = [], []
            for side in range(2):
                head = 2 * pair + side
                product = low[side * HEAD_DIM : (side + 1) * HEAD_DIM] * attended_ref[head]
                first.extend(split_low(logs_ref[head : head + 1, :]))
                later.extend(split_low(jnp.sum(product, axis=0, keepdims=True)))
            out[pair, PAIR : PAIR + STATS, :] = stat_rows(first + later, rows)

    return call(
        kernel,
        (
            jax.ShapeDtypeStruct((rows, depth), F32),
            jax.ShapeDtypeStruct((2, depth), F32),
            jax.ShapeDtypeStruct((pairs, PAIR + STATS, rows), BF16),
        ),
        (third, part, met, two, scale, row(gain), row(bias), weight, attended, logs),
        flops=2 * rows * depth * pairs * PAIR,
    )


def first_norm_back(second, part, met, one, scale, gain, bias, weight, packs):
    rows, depth = second.shape
    pairs, each = weight.shape[0] // PAIR, rows // packs

    def kernel(
        second_ref, part_ref, met_ref, one_ref, scale_ref, gain_ref, bias_ref, weight_ref, first, sums, out
    ):
        grad = second_ref[...] + whole_sum((part_ref, met_ref))
        unit = (one_ref[...] - bias_ref[...]) * (1.0 / gain_ref[...])
        value = norm_rows_back(unit, scale_ref[...], gain_ref[...], grad, sums)
        first[...] = value
        grads = times_transposed(weight_ref[...], value.astype(BF16)).astype(BF16)
        for pack in range(packs):
            for pair in range(pairs):
                out[pack, pair] = grads[pair * PAIR : (pair + 1) * PAIR, pack * each : (pack + 1) * each]

    return call(
        kernel,
        (
            jax.ShapeDtypeStruct((rows, depth), F32),
            jax.ShapeDtypeStruct((2, depth), F32),
            jax.ShapeDtypeStruct((packs, pairs, PAIR, each), BF16),
        ),
        (second, part, met, one, scale, row(gain), row(bias), weight),
        flops=2 * rows * depth * pairs * PAIR,
    )


def early_weight_grads(second, mixed_cross, third, narrow, two, narrow_grads, second_sums, third_sums):
    depth, width = second.shape[1], mixed_cross.shape[0]
    half = narrow.shape[1]

    def kernel(
        second_ref, cross_ref, third_ref, narrow_ref, two_ref, dnarrow_ref, second_sums_ref, third_sums_ref, out
    ):
        out[:, :width] = times_transposed(second_ref[...].astype(BF16).T, cross_ref[...]).astype(BF16)
        up = 4.0 * matrix_product(third_ref[...].astype(BF16).T, narrow_ref[...])
        out[:, width : width + half] = up.astype(BF16)
        down = matrix_product(two_ref[...].astype(BF16).T, dnarrow_ref[...])
        out[:, width + half : 2 * width] = down.astype(BF16)
        sums = jnp.concatenate(
            [second_sums_ref[...], third_sums_ref[...], jnp.zeros((PAIR - 4, depth), F32)], axis=0
        )
        out[:, 2 * width :] = sums.T.astype(BF16)

    args = (second, mixed_cross, third, narrow, two, narrow_grads, second_sums, third_sums)
    return call(
        kernel,
        jax.ShapeDtypeStruct((depth, 2 * width + PAIR), BF16),
        args,
        flops=4 * depth * width * second.shape[0],
    )


def middle_weight_grads(first, mixed_self, one, query_grads, source, source_dkv):
    depth = first.shape[1]
    width = mixed_self.shape[0]
    pairs = width // PAIR

    def kernel(first_ref, self_ref, one_ref, query_ref, source_ref, dkv_ref, out):
        step = pl.program_id(0)

        def rows_by_features(left, right):
            out[...] = times_transposed(left[...].astype(BF16).T, right[...]).astype(BF16)

        pl.when(step == 0)(lambda: rows_by_features(first_ref, self_ref))
        pl.when(step == 1)(lambda: rows_by_features(one_ref, query_ref))

        def sources(number):
            right = jnp.concatenate([dkv_ref[pair, number] for pair in range(pairs)], axis=1)
            out[...] = matrix_product(source_ref[...].T, right).astype(BF16)

        pl.when(step == 2)(lambda: sources(0))
        pl.when(step == 3)(lambda: sources(1))

GELU_ROOT = 0.7978845608028654
GELU_CUBE = 0.044715


def gelu_and_slope(value):
    square = value * value
    bend = jnp.tanh(GELU_ROOT * (value + GELU_CUBE * value * square))
    slope = 0.5 * (1.0 + bend) + 0.5 * value * (1.0 - bend * bend) * GELU_ROOT * (
        1.0 + 3.0 * GELU_CUBE * square
    )
    return 0.5 * value * (1.0 + bend), slope


def row(vector):
    return vector.reshape(1, -1)


def whole_sum(pair):
    return pair[0][...].astype(F32) + pair[1][...].astype(F32)


def normed(values):
    average = jnp.mean(values, axis=-1, keepdims=True)
    centred = values - average
    scale = lax.rsqrt(jnp.mean(centred * centred, axis=-1, keepdims=True) + 1e-05)
    return centred * scale, scale


def norm_rows_back(unit, scale, gain, grad, sums_ref):
    scaled = grad * gain
    first = jnp.mean(scaled, axis=-1, keepdims=True)
    second = jnp.mean(scaled * unit, axis=-1, keepdims=True)
    sums_ref[0:1, :] = jnp.sum(grad * unit, axis=0, keepdims=True)
    sums_ref[1:2, :] = jnp.sum(grad, axis=0, keepdims=True)
    return (scaled - first - unit * second) * scale


def first_norm(inputs, part, met, gain, bias, query_weight):
    rows, depth = inputs.shape
    pairs = query_weight.shape[1] // PAIR

    def kernel(inputs_ref, part_ref, met_ref, gain_ref, bias_ref, weight_ref, one, scale_ref, out):
        unit, scale = normed(inputs_ref[...].astype(F32) + whole_sum((part_ref, met_ref)))
        value = unit * gain_ref[...] + bias_ref[...]
        one[...], scale_ref[...] = value, scale
        query = (matrix_product(value.astype(BF16), weight_ref[...]).astype(BF16).astype(F32) * HEAD_DIM**-0.5).astype(BF16)
        for pair in range(pairs):
            out[pair] = query[:, pair * PAIR : (pair + 1) * PAIR].T

    return call(
        kernel,
        (
            jax.ShapeDtypeStruct((rows, depth), F32),
            jax.ShapeDtypeStruct((rows, 1), F32),
            jax.ShapeDtypeStruct((pairs, PAIR, rows), BF16),
        ),
        (inputs, part, met, row(gain), row(bias), query_weight),
        flops=2 * rows * depth * pairs * PAIR,
    )


def feed_forward(one, part, met, gain, bias, ffn_in, ffn_out, down, up):
    rows, depth = one.shape
    hidden, narrow_width = ffn_in.shape[1], down.shape[1]
    size = 512 if hidden % 512 == 0 else hidden
    steps = hidden // size

    def kernel(
        one_ref, part_ref, met_ref, gain_ref, bias_ref, in_ref, out_ref, down_ref, up_ref,
        two, scale_ref, slope_ref, narrow_ref, narrow_slope_ref, branch,
    ):
        unit, scale = normed(one_ref[...] + whole_sum((part_ref, met_ref)))
        value = unit * gain_ref[...] + bias_ref[...]
        rounded = value.astype(BF16)
        two[...], scale_ref[...] = value, scale
        act, slope = gelu_and_slope(matrix_product(rounded, down_ref[...]))
        narrow_ref[...] = act.astype(BF16)
        narrow_slope_ref[...] = slope.astype(BF16)
        total = 4.0 * matrix_product(act.astype(BF16), up_ref[...])
        for step in range(steps):
            part = slice(step * size, (step + 1) * size)
            act, slope = gelu_and_slope(matrix_product(rounded, in_ref[:, part]))
            slope_ref[:, part] = slope.astype(BF16)
            total += matrix_product(act.astype(BF16), out_ref[part, :])
        branch[...] = total.astype(BF16)

    args = (one, part, met, row(gain), row(bias), ffn_in, ffn_out, down, up)
    outs = (
        jax.ShapeDtypeStruct((rows, depth), F32),
        jax.ShapeDtypeStruct((rows, 1), F32),
        jax.ShapeDtypeStruct((rows, hidden), BF16),
        jax.ShapeDtypeStruct((rows, narrow_width), BF16),
        jax.ShapeDtypeStruct((rows, narrow_width), BF16),
        jax.ShapeDtypeStruct((rows, depth), BF16),
    )
    return call(kernel, outs, args, flops=4 * rows * depth * hidden)


def feed_backward(two, part, met, gain, bias, cotangent, slope, narrow_slope, ffn_in, ffn_out, down, up):
    rows, depth = two.shape
    hidden, narrow_width = ffn_in.shape[1], down.shape[1]
    size = 512 if hidden % 512 == 0 else hidden
    steps = hidden // size

    def kernel(
        two_ref, part_ref, met_ref, gain_ref, bias_ref, grad_ref, slope_ref, narrow_slope_ref,
        in_ref, out_ref, down_ref, up_ref, output, third, dnarrow, sums, share,
    ):
        unit, scale = normed(two_ref[...] + whole_sum((part_ref, met_ref)))
        output[...] = unit * gain_ref[...] + bias_ref[...]
        value = norm_rows_back(unit, scale, gain_ref[...], grad_ref[...].astype(F32), sums)
        rounded = value.astype(BF16)
        third[...] = value
        narrow = 4.0 * times_transposed(rounded, up_ref[...])
        narrow = (narrow * narrow_slope_ref[...].astype(F32)).astype(BF16)
        dnarrow[...] = narrow
        total = times_transposed(narrow, down_ref[...])
        for step in range(steps):
            part = slice(step * size, (step + 1) * size)
            grads = times_transposed(rounded, out_ref[part, :]) * slope_ref[:, part].astype(F32)
            total += times_transposed(grads.astype(BF16), in_ref[:, part])
        share[...] = total.astype(BF16)

    args = (two, part, met, row(gain), row(bias), cotangent, slope, narrow_slope, ffn_in, ffn_out, down, up)
    outs = (
        jax.ShapeDtypeStruct((rows, depth), F32),
        jax.ShapeDtypeStruct((rows, depth), F32),
        jax.ShapeDtypeStruct((rows, narrow_width), BF16),
        jax.ShapeDtypeStruct((2, depth), F32),
        jax.ShapeDtypeStruct((rows, depth), BF16),
    )
    return call(kernel, outs, args, flops=4 * rows * depth * hidden)


def second_norm_back(third, part, met, two, scale, gain, bias, weight, attended, logs):
    rows, depth = third.shape
    pairs = weight.shape[0] // PAIR

    def kernel(
        third_ref, part_ref, met_ref, two_ref, scale_ref, gain_ref, bias_ref, weight_ref, attended_ref, logs_ref,
        second, sums, out,
    ):
        grad = third_ref[...] + whole_sum((part_ref, met_ref))
        unit = (two_ref[...] - bias_ref[...]) * (1.0 / gain_ref[...])
        value = norm_rows_back(unit, scale_ref[...], gain_ref[...], grad, sums)
        second[...] = value
        grads = times_transposed(weight_ref[...], value.astype(BF16)).astype(BF16)
        for pair in range(pairs):
            low = grads[pair * PAIR : (pair + 1) * PAIR]
            out[pair, :PAIR, :] = low
            low = low.astype(F32)
            first, later = [], []
            for side in range(2):
                head = 2 * pair + side
                product = low[side * HEAD_DIM : (side + 1) * HEAD_DIM] * attended_ref[head]
                first.extend(split_low(logs_ref[head : head + 1, :]))
                later.extend(split_low(jnp.sum(product, axis=0, keepdims=True)))
            out[pair, PAIR : PAIR + STATS, :] = stat_rows(first + later, rows)

    return call(
        kernel,
        (
            jax.ShapeDtypeStruct((rows, depth), F32),
            jax.ShapeDtypeStruct((2, depth), F32),
            jax.ShapeDtypeStruct((pairs, PAIR + STATS, rows), BF16),
        ),
        (third, part, met, two, scale, row(gain), row(bias), weight, attended, logs),
        flops=2 * rows * depth * pairs * PAIR,
    )


def first_norm_back(second, part, met, one, scale, gain, bias, weight, packs):
    rows, depth = second.shape
    pairs, each = weight.shape[0] // PAIR, rows // packs

    def kernel(
        second_ref, part_ref, met_ref, one_ref, scale_ref, gain_ref, bias_ref, weight_ref, first, sums, out
    ):
        grad = second_ref[...] + whole_sum((part_ref, met_ref))
        unit = (one_ref[...] - bias_ref[...]) * (1.0 / gain_ref[...])
        value = norm_rows_back(unit, scale_ref[...], gain_ref[...], grad, sums)
        first[...] = value
        grads = times_transposed(weight_ref[...], value.astype(BF16)).astype(BF16)
        for pack in range(packs):
            for pair in range(pairs):
                out[pack, pair] = grads[pair * PAIR : (pair + 1) * PAIR, pack * each : (pack + 1) * each]

    return call(
        kernel,
        (
            jax.ShapeDtypeStruct((rows, depth), F32),
            jax.ShapeDtypeStruct((2, depth), F32),
            jax.ShapeDtypeStruct((packs, pairs, PAIR, each), BF16),
        ),
        (second, part, met, one, scale, row(gain), row(bias), weight),
        flops=2 * rows * depth * pairs * PAIR,
    )


def early_weight_grads(second, mixed_cross, third, narrow, two, narrow_grads, second_sums, third_sums):
    depth, width = second.shape[1], mixed_cross.shape[0]
    half = narrow.shape[1]

    def kernel(
        second_ref, cross_ref, third_ref, narrow_ref, two_ref, dnarrow_ref, second_sums_ref, third_sums_ref, out
    ):
        out[:, :width] = times_transposed(second_ref[...].astype(BF16).T, cross_ref[...]).astype(BF16)
        up = 4.0 * matrix_product(third_ref[...].astype(BF16).T, narrow_ref[...])
        out[:, width : width + half] = up.astype(BF16)
        down = matrix_product(two_ref[...].astype(BF16).T, dnarrow_ref[...])
        out[:, width + half : 2 * width] = down.astype(BF16)
        sums = jnp.concatenate(
            [second_sums_ref[...], third_sums_ref[...], jnp.zeros((PAIR - 4, depth), F32)], axis=0
        )
        out[:, 2 * width :] = sums.T.astype(BF16)

    args = (second, mixed_cross, third, narrow, two, narrow_grads, second_sums, third_sums)
    return call(
        kernel,
        jax.ShapeDtypeStruct((depth, 2 * width + PAIR), BF16),
        args,
        flops=4 * depth * width * second.shape[0],
    )


def middle_weight_grads(first, mixed_self, one, query_grads, source, source_dkv):
    depth = first.shape[1]
    width = mixed_self.shape[0]
    pairs = width // PAIR

    def kernel(first_ref, self_ref, one_ref, query_ref, source_ref, dkv_ref, out):
        step = pl.program_id(0)

        def rows_by_features(left, right):
            out[...] = times_transposed(left[...].astype(BF16).T, right[...]).astype(BF16)

        pl.when(step == 0)(lambda: rows_by_features(first_ref, self_ref))
        pl.when(step == 1)(lambda: rows_by_features(one_ref, query_ref))

        def sources(number):
            right = jnp.concatenate([dkv_ref[pair, number] for pair in range(pairs)], axis=1)
            out[...] = matrix_product(source_ref[...].T, right).astype(BF16)

        pl.when(step == 2)(lambda: sources(0))
        pl.when(step == 3)(lambda: sources(1))

    args = (first, mixed_self, one, query_grads, source, source_dkv)
    return call(
        kernel,
        jax.ShapeDtypeStruct((depth, 4 * width), BF16),
        args,
        grid=(4,),
        in_specs=[blocks(value) for value in args],
        out_specs=pl.BlockSpec((depth, width), lambda i: (0, i)),
        flops=2 * depth * width * 2048,
    )


def on_device(
    seq_size,
    head_size,
    inputs,
    encoded,
    tgt_bounds,
    src_bounds,
    self_query,
    self_key,
    self_value,
    self_out,
    cross_query,
    cross_key,
    cross_value,
    cross_out,
    ffn_in,
    ffn_out,
    adapter_down,
    adapter_up,
    norm1_gain,
    norm1_bias,
    norm2_gain,
    norm2_bias,
    norm3_gain,
    norm3_bias,
    cotangent,
):
    pack_count, row_count, model_width = inputs.shape
    source_rows = encoded.shape[1]
    local_width = self_query.shape[1]
    pairs_here = local_width // PAIR
    chips = seq_size // 2
    copies = chips // pairs_here
    rows = pack_count * row_count
    starts = tgt_bounds.shape[1]
    position = lax.axis_index("seq")
    core = position % 2
    base = position // (2 * pairs_here) * (2 * pairs_here)
    place = jnp.stack([base, core]).astype(jnp.int32)
    by_pack = pairs_here * pack_count == chips and seq_size == 16 and row_count == PAIR
    row_place = jnp.stack([position // (2 * pairs_here), core]).astype(jnp.int32)
    row_shape = RowShape(chips, row_count, starts)
    self_bounds = (tgt_bounds.reshape(-1), tgt_bounds.reshape(-1))
    cross_bounds = (tgt_bounds.reshape(-1), src_bounds.reshape(-1))
    self_shape = Shape(chips, pairs_here, pack_count, row_count, row_count, starts, True)
    cross_shape = Shape(chips, pairs_here, pack_count, row_count, source_rows, starts, False)
    flat_inputs = inputs.reshape(rows, model_width)
    flat_encoded = encoded.reshape(pack_count * source_rows, model_width)

    all_chips = [[2 * chip + side for chip in range(chips)] for side in range(2)]
    near_chips = [
        [2 * (copy * pairs_here + pair) + side for pair in range(pairs_here)]
        for copy in range(copies)
        for side in range(2)
    ]

    def swap_core(value):
        return lax.ppermute(value, "seq", [(i, i ^ 1) for i in range(seq_size)])

    def to_all(value):
        return lax.all_to_all(value, "seq", 0, 0, axis_index_groups=all_chips, tiled=True)

    def to_near(value):
        if pairs_here == 1:
            return value
        return lax.all_to_all(value, "seq", 0, 0, axis_index_groups=near_chips, tiled=True)

    def exchange(value):
        low = value.astype(BF16)
        if head_size == 2:
            return low, lax.ppermute(low, "head", [(0, 1), (1, 0)])
        return lax.psum(low.astype(F32), "head"), jnp.zeros_like(low)

    def spread_queries(features):
        message = features.reshape(pairs_here, -1, rows)
        own = to_all(jnp.tile(message, (copies, 1, 1)))
        return own, swap_core(own)

    def pair_rows(keys, values):
        def cut(value):
            return value.reshape(-1, pairs_here, PAIR).transpose(1, 0, 2)

        return jnp.stack([cut(keys), cut(values)], axis=1)

    def join_rows(message):
        return message.transpose(1, 2, 0, 3).reshape(2, -1, local_width)

    def logs_of(message):
        stats = message[:, PAIR : PAIR + 4, :].astype(F32)
        return stats[:, 0::2] + stats[:, 1::2]

    def weighted(parts, logs):
        highest = jnp.max(logs, axis=0)
        weights = jnp.exp(logs - highest)
        denominator = jnp.sum(weights, axis=0)
        shares = weights / denominator
        split = parts.reshape(parts.shape[:-2] + (2, HEAD_DIM, rows)).astype(F32)
        merged = jnp.sum(split * shares[:, :, :, None, :], axis=0)
        return merged, highest + jnp.log(denominator)

    def collect(own_part, other_part):
        met = swap_core(other_part)
        parts = jnp.stack([own_part, met])
        logs = jnp.stack([logs_of(own_part), logs_of(met)])
        merged, total = weighted(parts[:, :, :PAIR], logs)
        high, low = split_parts(total)
        statistics = jnp.stack([high, low], axis=2).reshape(chips, 4, rows)
        statistics = jnp.pad(statistics, ((0, 0), (0, STATS - 4), (0, 0)))
        message = jnp.concatenate(
            [merged.reshape(chips, PAIR, rows).astype(BF16), statistics.astype(BF16)], axis=1
        )
        back = to_all(message)
        logs = logs_of(back).reshape(copies, pairs_here, 2, rows)
        features = back[:, :PAIR].reshape(copies, pairs_here, PAIR, rows)
        merged, total = weighted(features, logs)
        return merged, total

    def spread_grads(grad_features, merged, total):
        split = grad_features.reshape(pairs_here, 2, HEAD_DIM, rows).astype(F32)
        delta = jnp.sum(split * merged, axis=2)
        statistics = jnp.concatenate(
            [
                jnp.stack(split_parts(total), axis=2).reshape(pairs_here, 4, rows),
                jnp.stack(split_parts(delta), axis=2).reshape(pairs_here, 4, rows),
                jnp.zeros((pairs_here, STATS - 8, rows), F32),
            ],
            axis=1,
        ).astype(BF16)
        message = jnp.concatenate([grad_features.reshape(pairs_here, PAIR, rows), statistics], axis=1)
        return spread_queries(message)

    def collect_query_grads(own_part, other_part):
        total = (own_part.astype(F32) + swap_core(other_part).astype(F32)).astype(BF16)
        back = to_all(total).reshape(copies, local_width, rows)
        return jnp.sum(back.astype(F32), axis=0).astype(BF16)

    def scatter(joined):
        return lax.psum_scatter(joined, "seq", scatter_dimension=0, tiled=True)

    def scatter_by_halves(keep, send, done):
        width = keep.shape[2]

        def pass_on(value, bit):
            return lax.ppermute(value, "seq", [(i, i ^ bit) for i in range(seq_size)])

        values = [value.reshape(2, 2, 2, -1, width) for value in (keep, swap_core(send))]
        cuts = [(0, width // 2), (width // 2, width)]
        values = [values, values]
        for bits, axes in (((2, 4), (2, 1)), ((4, 2), (1, 1)), ((8, 8), (0, 0))):
            found = halve(values, [position // bit % 2 for bit in bits], axes, cuts)
            if bits == (8, 8):
                found, done = lax.optimization_barrier((found, done))
            values = [[kept, pass_on(sent, bit)] for (kept, sent), bit in zip(found, bits)]
            cuts = [(0, width // 2)] * 2
        return last_sums(*values, 3), done

    scaling = HEAD_DIM**-0.5
    cross_kv = project_sources(flat_encoded, cross_key, cross_value)
    if by_pack:
        message = project_self(flat_inputs, self_query, self_key, self_value, pack_count)
        met = to_all(message)
        self_q, self_kv = met[:, 0], met[:, 1:]
        self_kv_other = swap_core(self_kv)
        self_heads, self_logs = row_forward(
            row_shape, self_bounds[0], row_place, self_q, self_kv, self_kv_other
        )
        back = to_all(self_heads)
        back, cross_kv = lax.optimization_barrier((back, cross_kv))
        back = back.reshape(pack_count, pairs_here, PAIR, row_count)
        mixed_self = back.transpose(1, 2, 0, 3).reshape(local_width, rows)
    else:
        query_self = (contract(self_query, flat_inputs, 0, 1) * scaling).astype(BF16)
        key_self = matrix_product(flat_inputs, self_key).astype(BF16)
        value_self = matrix_product(flat_inputs, self_value).astype(BF16)
        self_q = spread_queries(query_self)
        self_kv = to_near(pair_rows(key_self, value_self))
        own_part, other_part = attention_forward(self_shape, self_bounds, place, *self_q, self_kv)
        attended_self, log_self = collect(own_part, other_part)
        mixed_self = attended_self.reshape(local_width, rows).astype(BF16)
    part, met = exchange(transposed_times(mixed_self, self_out))
    normed_one, scale_one, query_cross = first_norm(
        flat_inputs, part, met, norm1_gain, norm1_bias, cross_query
    )
    cross_kv = to_near(cross_kv)
    query_cross, cross_kv = lax.optimization_barrier((query_cross, cross_kv))
    cross_q = spread_queries(query_cross)
    own_part, other_part = attention_forward(cross_shape, cross_bounds, place, *cross_q, cross_kv)
    attended_cross, log_cross = collect(own_part, other_part)
    mixed_cross = attended_cross.reshape(local_width, rows).astype(BF16)
    part, met = exchange(transposed_times(mixed_cross, cross_out))
    normed_two, scale_two, slope, narrow_low, narrow_slope, branch = feed_forward(
        normed_one, part, met, norm2_gain, norm2_bias, ffn_in, ffn_out, adapter_down, adapter_up
    )
    part, met = exchange(branch)
    output, grad_third, grad_narrow, third_sums, grad_two_part = feed_backward(
        normed_two, part, met, norm3_gain, norm3_bias, cotangent.reshape(rows, model_width),
        slope, narrow_slope, ffn_in, ffn_out, adapter_down, adapter_up,
    )
    part, met = exchange(grad_two_part)
    grad_second, second_sums, message = second_norm_back(
        grad_third, part, met, normed_two, scale_two, norm2_gain, norm2_bias, cross_out,
        attended_cross.reshape(-1, HEAD_DIM, rows), log_cross.reshape(-1, rows),
    )
    early = early_weight_grads(
        grad_second, mixed_cross, grad_third, narrow_low, normed_two, grad_narrow,
        second_sums, third_sums,
    )
    cross_g = spread_queries(message)
    early = scatter(early)
    own_part, other_part, cross_dkv = attention_backward(
        cross_shape, cross_bounds, place, *cross_q, *cross_g, cross_kv
    )
    grad_query_cross = collect_query_grads(own_part, other_part)
    grad_query_cross, early = lax.optimization_barrier((grad_query_cross, early))
    adapters_up, adapters_down, norms = spread_adapters(
        lax.all_gather(early[:, local_width:], "seq", axis=0, tiled=True), adapter_up.shape[0]
    )
    source_dkv = to_near(cross_dkv)
    part, met = exchange(transposed_times(grad_query_cross, contract_t(cross_query)))
    grad_first, first_sums, grad_heads = first_norm_back(
        grad_second, part, met, normed_one, scale_one, norm1_gain, norm1_bias, self_out, pack_count
    )
    source_part = source_grads(source_dkv, cross_key, cross_value)
    middle = middle_weight_grads(
        grad_first, mixed_self, normed_one, grad_query_cross, flat_encoded, source_dkv
    )
    if by_pack:
        grad_heads = to_all(grad_heads.reshape(chips, PAIR, row_count))
        grad_heads, middle, source_part = lax.optimization_barrier((grad_heads, middle, source_part))
        source_part, source_met = exchange(source_part)
        dq, own_dkv, other_dkv = row_backward(
            row_shape, self_bounds[0], row_place, self_q, self_heads, self_logs, grad_heads,
            self_kv, self_kv_other,
        )
        dkv = (own_dkv.astype(F32) + swap_core(other_dkv).astype(F32)).astype(BF16)
        high, low = split_parts(first_sums + swap_core(first_sums))
        sums = jnp.concatenate([high, low]).astype(BF16).reshape(1, 1, -1, PAIR)
        sums = jnp.broadcast_to(sums, (chips,) + sums.shape[1:])[:, 0]
        message = jnp.concatenate([dq, dkv[:, 0], dkv[:, 1], sums], axis=1)
        back = to_all(message)
        first_sums = back[:, 3 * row_count :].astype(F32).reshape(chips, 2, 2, model_width)
        first_sums = jnp.sum(first_sums[:, 0] + first_sums[:, 1], axis=0)
        back, source_met = lax.optimization_barrier((back, source_met))
        keep, send = self_weight_grads(flat_inputs, back, pack_count, core)
        back, keep, send = lax.optimization_barrier((back, keep, send))
        self_grads, middle = scatter_by_halves(keep, send, scatter(middle))
        part, met = exchange(input_grads(back, self_query, self_key, self_value, pack_count))
        grad_inputs = grad_first + (part.astype(F32) + met.astype(F32))
    else:
        source_part, source_met = exchange(source_part)
        grad_mixed_self = grad_heads.transpose(1, 2, 0, 3).reshape(local_width, rows)
        self_g = spread_grads(grad_mixed_self, attended_self, log_self)
        own_part, other_part, self_dkv = attention_backward(
            self_shape, self_bounds, place, *self_q, *self_g, self_kv
        )
        grad_query_self = collect_query_grads(own_part, other_part)
        grad_key_self, grad_value_self = join_rows(to_near(self_dkv))
        grad_in_part = (
            transposed_times(grad_query_self, contract_t(self_query))
            + times_transposed(grad_key_self, self_key)
            + times_transposed(grad_value_self, self_value)
        )
        part, met = exchange(grad_in_part)
        grad_inputs = grad_first + (part.astype(F32) + met.astype(F32))
        grad_self_query = contract(flat_inputs, grad_query_self, 0, 1)
        grad_self_key = transposed_times(flat_inputs, grad_key_self)
        grad_self_value = transposed_times(flat_inputs, grad_value_self)
        self_parts = jnp.concatenate(
            [part.astype(BF16) for part in (grad_self_query, grad_self_key, grad_self_value)], axis=1
        )
        self_grads = jnp.split(scatter(self_parts).astype(F32), 3, axis=1)
        middle = scatter(middle)
        first_sums = jnp.sum(lax.all_gather(first_sums, "seq"), axis=0)

    grad_source = source_part.astype(F32) + source_met.astype(F32)
    cross_out_g, self_out_g, cross_query_g, cross_key_g, cross_value_g = spread_middle(
        early[:, :local_width], middle
    )
    self_query_g, self_key_g, self_value_g = self_grads
    return (
        output.reshape(pack_count, row_count, model_width),
        grad_inputs.reshape(pack_count, row_count, model_width),
        grad_source.reshape(pack_count, source_rows, model_width),
        self_query_g,
        self_key_g,
        self_value_g,
        self_out_g,
        cross_query_g,
        cross_key_g,
        cross_value_g,
        cross_out_g,
        adapters_down,
        adapters_up,
        first_sums[0],
        first_sums[1],
        norms[0],
        norms[1],
        norms[2],
        norms[3],
    )


def contract_t(weight):
    return weight.T


def solution(mesh):
    placed = (
        P(None, "seq", None),
        P(None, "seq", None),
        P(),
        P(),
        P(None, "head"),
        P(None, "head"),
        P(None, "head"),
        P("head", None),
        P(None, "head"),
        P(None, "head"),
        P(None, "head"),
        P("head", None),
        P(None, "head"),
        P("head", None),
        P(None, "head"),
        P("head", None),
        P(),
        P(),
        P(),
        P(),
        P(),
        P(),
        P(None, "seq", None),
    )
    return jax.shard_map(
        functools.partial(on_device, mesh.shape["seq"], mesh.shape["head"]),
        mesh=mesh,
        in_specs=placed,
        out_specs=(
            P(None, "seq", None),
            P(None, "seq", None),
            P(None, "seq", None),
            P("seq", "head"),
            P("seq", "head"),
            P("seq", "head"),
            P("head", "seq"),
            P("seq", "head"),
            P("seq", "head"),
            P("seq", "head"),
            P("head", "seq"),
            P(None, "head"),
            P("head", None),
            P(),
            P(),
            P(),
            P(),
            P(),
            P(),
        ),
        check_vma=False,
    )
```

```python
import functools

import jax
import jax.numpy as jnp
from jax import lax
from jax.experimental import pallas as pl
from jax.experimental.pallas import tpu as pltpu
from jax.sharding import PartitionSpec as P

HEAD_DIM = 64
PAIR = 2 * HEAD_DIM
STATS = 16
LOWEST = -1e29
EXCLUDED = -1e30
F32 = jnp.float32
BF16 = jnp.bfloat16


def matrix_product(left, right):
    return jnp.dot(left, right, preferred_element_type=F32)


def contract(left, right, left_dim, right_dim):
    return lax.dot_general(
        left, right, (((left_dim,), (right_dim,)), ((), ())), preferred_element_type=F32
    )


def times_transposed(left, right):
    return contract(left, right, 1, 1)


def transposed_times(left, right):
    return contract(left, right, 0, 0)


class Shape:
    def __init__(self, chips, groups, packs, rows, source_rows, starts, causal):
        self.chips, self.groups, self.packs, self.rows = chips, groups, packs, rows
        self.source_rows, self.starts, self.causal = source_rows, starts, causal
        self.step = groups
        while self.step > 1 and self.step * source_rows > 768:
            self.step //= 2
        self.steps = groups // self.step
        self.tile = 2 * rows
        self.length = 2 * chips * rows
        self.source_length = 2 * chips * source_rows


def position_range(shape, places, pack, target_bounds, source_bounds):
    starts = shape.starts
    low = jnp.zeros_like(places)
    high = jnp.zeros_like(places) + source_bounds[pack * starts]
    for entry in range(starts):
        later = places >= target_bounds[pack * starts + entry]
        low = jnp.where(later, source_bounds[pack * starts + entry], low)
        if entry + 1 < starts:
            following = source_bounds[pack * starts + entry + 1]
        else:
            following = jnp.int32(shape.source_length)
        high = jnp.where(later, following, high)
    if shape.causal:
        high = places + 1
    return low, high


def lane_places(shape, chip, core):
    lanes = lax.broadcasted_iota(jnp.int32, (1, shape.tile), 1)
    own = (2 * chip + core) * shape.rows + lanes
    other = (2 * chip + 1 - core) * shape.rows + lanes - shape.rows
    return jnp.where(lanes < shape.rows, own, other)


def step_conditions(shape, chip, pack, first_group, place, target_bounds, source_bounds):
    base, core = place[0], place[1]
    head = chip * (2 * shape.rows)
    tail = head + 2 * shape.rows - 1
    low_first, high_first = position_range(shape, head, pack, target_bounds, source_bounds)
    low_last, high_last = position_range(shape, tail, pack, target_bounds, source_bounds)
    begin = (base + 2 * first_group + core) * shape.source_rows
    end = begin + (2 * shape.step - 1) * shape.source_rows
    some = jnp.logical_and(low_first < end, high_last > begin)
    whole = jnp.logical_and(low_last <= begin, high_first >= end)
    return begin, some, whole


def source_places(shape, begin):
    size = shape.step * shape.source_rows
    rows = lax.broadcasted_iota(jnp.int32, (size, shape.tile), 0)
    places = begin + rows
    for group in range(1, shape.step):
        places = places + jnp.where(rows >= group * shape.source_rows, shape.source_rows, 0)
    return places


def both(own_ref, other_ref, chip, first, last, pack, rows):
    lanes = slice(pack * rows, (pack + 1) * rows)
    return jnp.concatenate(
        [own_ref[chip, first:last, lanes], other_ref[chip, first:last, lanes]], axis=1
    )


def one_head(pair_rows, head):
    feature = lax.broadcasted_iota(jnp.int32, pair_rows.shape, 0)
    mine = (feature >= HEAD_DIM) if head else (feature < HEAD_DIM)
    return jnp.where(mine, pair_rows, jnp.zeros_like(pair_rows))


def split_low(value):
    high = value.astype(BF16).astype(F32)
    return high, value - high


def split_parts(value):
    high = lax.reduce_precision(value, 8, 7)
    return high, value - high


def stat_rows(rows, width):
    index = lax.broadcasted_iota(jnp.int32, (STATS, width), 0)
    total = jnp.zeros((STATS, width), F32)
    for number, row in enumerate(rows):
        total = jnp.where(index == number, row, total)
    return total.astype(BF16)


def forward_kernel(
    shape, target_bounds, source_bounds, place, own_q, other_q, keys_values, own_out, other_out,
    value_t, maxima, total,
):
    step_rows = shape.step * shape.source_rows
    for group in range(shape.groups):
        for pack in range(shape.packs):
            part = slice(pack * shape.source_rows, (pack + 1) * shape.source_rows)
            lanes = slice(group * shape.source_rows, (group + 1) * shape.source_rows)
            turned = keys_values[group, 1, part, :].T
            for head in range(2):
                value_t[pack, head, :HEAD_DIM, lanes] = turned[head * HEAD_DIM : (head + 1) * HEAD_DIM]
    value_t[:, :, HEAD_DIM:, :] = jnp.ones((shape.packs, 2, STATS, value_t.shape[3]), BF16)

    for pack in range(shape.packs):
        part = slice(pack * shape.source_rows, (pack + 1) * shape.source_rows)

        def per_chip(chip, unused, pack=pack, part=part):
            query = both(own_q, other_q, chip, 0, PAIR, pack, shape.rows)
            low, high = position_range(
                shape, lane_places(shape, chip, place[1]), pack, target_bounds, source_bounds
            )
            maxima[...] = jnp.full_like(maxima, LOWEST)
            total[...] = jnp.zeros_like(total)
            for step in range(shape.steps):
                groups = slice(step * shape.step, (step + 1) * shape.step)
                begin, some, whole = step_conditions(
                    shape, chip, pack, step * shape.step, place, target_bounds, source_bounds
                )

                def fold(masked, step=step, groups=groups, begin=begin):
                    key_rows = keys_values[groups, 0, part, :].reshape(step_rows, PAIR)
                    if masked:
                        places = source_places(shape, begin)
                        allowed = jnp.logical_and(places >= low, places < high)
                    befores = [maxima[head : head + 1, :] for head in range(2)]
                    scores = [matrix_product(key_rows, one_head(query, head)) for head in range(2)]
                    if masked:
                        scores = [jnp.where(allowed, score, EXCLUDED) for score in scores]
                    nows = [
                        jnp.maximum(before, jnp.max(score, axis=0, keepdims=True))
                        for before, score in zip(befores, scores)
                    ]
                    weights = [jnp.exp(score - now) for score, now in zip(scores, nows)]
                    products = []
                    for head in range(2):
                        values = value_t[pack, head, :, step * step_rows : (step + 1) * step_rows]
                        products.append(matrix_product(values, weights[head].astype(BF16)))
                    for head in range(2):
                        fading = jnp.exp(befores[head] - nows[head])
                        maxima[head : head + 1, :] = nows[head]
                        total[head] = total[head] * fading + products[head]

                pl.when(jnp.logical_and(some, whole))(functools.partial(fold, False))
                pl.when(jnp.logical_and(some, jnp.logical_not(whole)))(
                    functools.partial(fold, True)
                )
            statistics = []
            for head in range(2):
                features = slice(head * HEAD_DIM, (head + 1) * HEAD_DIM)
                found = total[head, HEAD_DIM : HEAD_DIM + 1, :]
                divisor = jnp.maximum(found, 1e-37)
                filled = found > 0.0
                logs = jnp.where(filled, maxima[head : head + 1, :] + jnp.log(divisor), LOWEST)
                statistics.extend(split_low(logs))
                result = (total[head, :HEAD_DIM, :] / divisor).astype(BF16)
                for ref, offset in ((own_out, 0), (other_out, shape.rows)):
                    ref[chip, features, pack * shape.rows : (pack + 1) * shape.rows] = result[
                        :, offset : offset + shape.rows
                    ]
            statistics = stat_rows(statistics, shape.tile)
            for ref, offset in ((own_out, 0), (other_out, shape.rows)):
                ref[chip, PAIR : PAIR + STATS, pack * shape.rows : (pack + 1) * shape.rows] = (
                    statistics[:, offset : offset + shape.rows]
                )
            return 0

        lax.fori_loop(0, shape.chips, per_chip, 0)


def backward_kernel(
    shape, target_bounds, source_bounds, place, own_q, other_q, own_g, other_g, keys_values,
    own_dq, other_dq, key_grads, key_t, grad_key, grad_value, grad_query,
):
    step_rows = shape.step * shape.source_rows
    grad_key[...] = jnp.zeros_like(grad_key)
    grad_value[...] = jnp.zeros_like(grad_value)
    for group in range(shape.groups):
        for pack in range(shape.packs):
            part = slice(pack * shape.source_rows, (pack + 1) * shape.source_rows)
            key_t[pack, :, group * shape.source_rows : (group + 1) * shape.source_rows] = (
                keys_values[group, 0, part, :].T
            )

    for pack in range(shape.packs):
        part = slice(pack * shape.source_rows, (pack + 1) * shape.source_rows)

        def per_chip(chip, unused, pack=pack, part=part):
            query = both(own_q, other_q, chip, 0, PAIR, pack, shape.rows)
            grads = both(own_g, other_g, chip, 0, PAIR, pack, shape.rows)
            statistics = both(own_g, other_g, chip, PAIR, PAIR + STATS, pack, shape.rows).astype(F32)
            low, high = position_range(
                shape, lane_places(shape, chip, place[1]), pack, target_bounds, source_bounds
            )
            queries = [one_head(query, head) for head in range(2)]
            gradients = [one_head(grads, head) for head in range(2)]
            log_rows = [statistics[2 * head : 2 * head + 1] + statistics[2 * head + 1 : 2 * head + 2] for head in range(2)]
            deltas = [statistics[2 * head + 4 : 2 * head + 5] + statistics[2 * head + 5 : 2 * head + 6] for head in range(2)]
            grad_query[...] = jnp.zeros_like(grad_query)
            for step in range(shape.steps):
                groups = slice(step * shape.step, (step + 1) * shape.step)
                begin, some, whole = step_conditions(
                    shape, chip, pack, step * shape.step, place, target_bounds, source_bounds
                )

                def fold(masked, step=step, groups=groups, begin=begin):
                    key_rows = keys_values[groups, 0, part, :].reshape(step_rows, PAIR)
                    value_rows = keys_values[groups, 1, part, :].reshape(step_rows, PAIR)
                    if masked:
                        places = source_places(shape, begin)
                        allowed = jnp.logical_and(places >= low, places < high)
                    lanes = slice(step * step_rows, (step + 1) * step_rows)
                    scores = [matrix_product(key_rows, queries[head]) for head in range(2)]
                    changes = [matrix_product(value_rows, gradients[head]) for head in range(2)]
                    if masked:
                        scores = [jnp.where(allowed, score, EXCLUDED) for score in scores]
                    weights = [jnp.exp(score - row) for score, row in zip(scores, log_rows)]
                    diffs = [
                        (weight * (change - delta)).astype(BF16)
                        for weight, change, delta in zip(weights, changes, deltas)
                    ]
                    key_part = times_transposed(
                        jnp.concatenate(diffs, axis=1), jnp.concatenate(queries, axis=1)
                    )
                    value_part = times_transposed(
                        jnp.concatenate([weight.astype(BF16) for weight in weights], axis=1),
                        jnp.concatenate(gradients, axis=1),
                    )
                    query_parts = [
                        matrix_product(
                            key_t[pack, head * HEAD_DIM : (head + 1) * HEAD_DIM, lanes], diffs[head]
                        )
                        for head in range(2)
                    ]
                    grad_query[...] += jnp.concatenate(query_parts, axis=0)
                    grad_key[pack, lanes, :] += key_part
                    grad_value[pack, lanes, :] += value_part

                pl.when(jnp.logical_and(some, whole))(functools.partial(fold, False))
                pl.when(jnp.logical_and(some, jnp.logical_not(whole)))(
                    functools.partial(fold, True)
                )
            result = (grad_query[...] * HEAD_DIM**-0.5).astype(BF16)
            for ref, offset in ((own_dq, 0), (other_dq, shape.rows)):
                ref[chip, :, pack * shape.rows : (pack + 1) * shape.rows] = result[
                    :, offset : offset + shape.rows
                ]
            return 0

        lax.fori_loop(0, shape.chips, per_chip, 0)

    for group in range(shape.groups):
        for pack in range(shape.packs):
            part = slice(pack * shape.source_rows, (pack + 1) * shape.source_rows)
            lanes = slice(group * shape.source_rows, (group + 1) * shape.source_rows)
            key_grads[group, 0, part, :] = grad_key[pack, lanes, :].astype(BF16)
            key_grads[group, 1, part, :] = grad_value[pack, lanes, :].astype(BF16)


def smem():
    return pl.BlockSpec(memory_space=pltpu.SMEM)


def vmem():
    return pl.BlockSpec(memory_space=pltpu.VMEM)


PARAMS = dict(vmem_limit_bytes=16 * 1024 * 1024)


def attention_forward(shape, bounds, place, own_q, other_q, keys_values):
    width = shape.packs * shape.rows
    pairs = shape.packs * shape.length * shape.groups * shape.source_rows
    message = jax.ShapeDtypeStruct((shape.chips, PAIR + STATS, width), BF16)
    return pl.pallas_call(
        functools.partial(forward_kernel, shape),
        out_shape=(message, message),
        in_specs=[smem()] * 3 + [vmem()] * 3,
        out_specs=(vmem(), vmem()),
        scratch_shapes=[
            pltpu.VMEM((shape.packs, 2, HEAD_DIM + STATS, shape.groups * shape.source_rows), BF16),
            pltpu.VMEM((8, shape.tile), F32),
            pltpu.VMEM((2, HEAD_DIM + STATS, shape.tile), F32),
        ],
        compiler_params=pltpu.CompilerParams(**PARAMS),
        cost_estimate=pl.CostEstimate(
            flops=8 * pairs * HEAD_DIM, bytes_accessed=6 * 1024 * 1024, transcendentals=2 * pairs
        ),
    )(bounds[0], bounds[1], place, own_q, other_q, keys_values)


def attention_backward(shape, bounds, place, own_q, other_q, own_g, other_g, keys_values):
    width = shape.packs * shape.rows
    pairs = shape.packs * shape.length * shape.groups * shape.source_rows
    source = shape.groups * shape.source_rows
    message = jax.ShapeDtypeStruct((shape.chips, PAIR, width), BF16)
    return pl.pallas_call(
        functools.partial(backward_kernel, shape),
        out_shape=(message, message, jax.ShapeDtypeStruct(keys_values.shape, BF16)),
        in_specs=[smem()] * 3 + [vmem()] * 5,
        out_specs=(vmem(), vmem(), vmem()),
        scratch_shapes=[
            pltpu.VMEM((shape.packs, PAIR, source), BF16),
            pltpu.VMEM((shape.packs, source, PAIR), F32),
            pltpu.VMEM((shape.packs, source, PAIR), F32),
            pltpu.VMEM((PAIR, shape.tile), F32),
        ],
        compiler_params=pltpu.CompilerParams(**PARAMS),
        cost_estimate=pl.CostEstimate(
            flops=20 * pairs * HEAD_DIM, bytes_accessed=8 * 1024 * 1024, transcendentals=2 * pairs
        ),
    )(bounds[0], bounds[1], place, own_q, other_q, own_g, other_g, keys_values)


class RowShape:
    def __init__(self, chips, rows, starts):
        self.chips, self.rows, self.starts = chips, rows, starts
        self.source_length, self.causal = 2 * chips * rows, True
        self.span = 2 if chips % 2 == 0 else 1
        self.tiles = chips // self.span
        self.tile = self.span * rows
        self.step = 2 * self.span * rows


def own_places(shape, tile, core):
    lanes = lax.broadcasted_iota(jnp.int32, (1, shape.tile), 1)
    places = 2 * tile * shape.span * shape.rows + core * shape.rows + lanes
    for block in range(1, shape.span):
        places = places + jnp.where(lanes >= block * shape.rows, shape.rows, 0)
    return places


def chip_places(shape, step, core):
    rows = lax.broadcasted_iota(jnp.int32, (shape.step, shape.tile), 0)
    places = step * shape.step + rows
    for block in range(2 * shape.span):
        here = jnp.logical_and(rows >= block * shape.rows, rows < (block + 1) * shape.rows)
        shift = shape.rows * core if block % 2 == 0 else -shape.rows * core
        places = places + jnp.where(here, shift, 0)
    return places


def row_conditions(shape, tile, step, pack, bounds):
    head = tile * shape.step
    tail = head + shape.step - 1
    begin = step * shape.step
    end = begin + shape.step
    low_first, _ = position_range(shape, head, pack, bounds, bounds)
    low_last, _ = position_range(shape, tail, pack, bounds, bounds)
    some = low_first < end
    whole = jnp.logical_and(low_last <= begin, end <= head + 1)
    return some, whole


def fill_rows(shape, own_kv, other_kv, which, target, transposed):
    for chip in range(shape.chips):
        for side, ref in enumerate((own_kv, other_kv)):
            first = (2 * chip + side) * shape.rows
            block = ref[chip, which]
            if transposed and len(target.shape) == 3:
                for head in range(2):
                    target[head, :HEAD_DIM, first : first + shape.rows] = block.T[
                        head * HEAD_DIM : (head + 1) * HEAD_DIM
                    ]
            elif transposed:
                target[:, first : first + shape.rows] = block.T
            else:
                target[first : first + shape.rows, :] = block


def tile_lanes(ref, tile, span):
    return jnp.concatenate([ref[tile * span + block] for block in range(span)], axis=1)


def row_forward_kernel(
    shape, bounds, place, queries, own_kv, other_kv, out, logs, key_all, value_t, maxima, total
):
    pack, core = place[0], place[1]
    fill_rows(shape, own_kv, other_kv, 0, key_all, False)
    fill_rows(shape, own_kv, other_kv, 1, value_t, True)
    value_t[:, HEAD_DIM:, :] = jnp.ones((2, STATS, value_t.shape[2]), BF16)

    def per_tile(tile, unused):
        query = tile_lanes(queries, tile, shape.span)
        low, high = position_range(shape, own_places(shape, tile, core), pack, bounds, bounds)
        heads = [one_head(query, head) for head in range(2)]
        maxima[...] = jnp.full_like(maxima, LOWEST)
        total[...] = jnp.zeros_like(total)

        def per_step(step, unused):
            some, whole = row_conditions(shape, tile, step, pack, bounds)
            first = pl.multiple_of(step * shape.step, shape.step)

            def fold(masked):
                key_rows = key_all[pl.ds(first, shape.step), :]
                if masked:
                    places = chip_places(shape, step, core)
                    allowed = jnp.logical_and(places >= low, places < high)
                befores = [maxima[head : head + 1, :] for head in range(2)]
                scores = [matrix_product(key_rows, heads[head]) for head in range(2)]
                if masked:
                    scores = [jnp.where(allowed, score, EXCLUDED) for score in scores]
                nows = [
                    jnp.maximum(before, jnp.max(score, axis=0, keepdims=True))
                    for before, score in zip(befores, scores)
                ]
                weights = [jnp.exp(score - now) for score, now in zip(scores, nows)]
                products = [
                    matrix_product(value_t[head, :, pl.ds(first, shape.step)], weights[head].astype(BF16))
                    for head in range(2)
                ]
                for head in range(2):
                    fading = jnp.exp(befores[head] - nows[head])
                    maxima[head : head + 1, :] = nows[head]
                    total[head] = total[head] * fading + products[head]

            pl.when(jnp.logical_and(some, whole))(functools.partial(fold, False))
            pl.when(jnp.logical_and(some, jnp.logical_not(whole)))(functools.partial(fold, True))
            return 0

        lax.fori_loop(0, tile + 1, per_step, 0)
        for head in range(2):
            features = slice(head * HEAD_DIM, (head + 1) * HEAD_DIM)
            divisor = total[head, HEAD_DIM : HEAD_DIM + 1, :]
            result = (total[head, :HEAD_DIM, :] / divisor).astype(BF16)
            found = maxima[head : head + 1, :] + jnp.log(divisor)
            for block in range(shape.span):
                lanes = slice(block * shape.rows, (block + 1) * shape.rows)
                out[tile * shape.span + block, features, :] = result[:, lanes]
                logs[tile * shape.span + block, head : head + 1, :] = found[:, lanes]
        return 0

    lax.fori_loop(0, shape.tiles, per_tile, 0)


def row_backward_kernel(
    shape, bounds, place, queries, outputs, logs, grads, own_kv, other_kv,
    query_grads, own_dkv, other_dkv, key_all, value_all, key_t, grad_key, grad_value, grad_query,
):
    pack, core = place[0], place[1]
    fill_rows(shape, own_kv, other_kv, 0, key_all, False)
    fill_rows(shape, own_kv, other_kv, 1, value_all, False)
    fill_rows(shape, own_kv, other_kv, 0, key_t, True)
    grad_key[...] = jnp.zeros_like(grad_key)
    grad_value[...] = jnp.zeros_like(grad_value)

    def per_tile(tile, unused):
        query = tile_lanes(queries, tile, shape.span)
        grad = tile_lanes(grads, tile, shape.span)
        product = grad.astype(F32) * tile_lanes(outputs, tile, shape.span).astype(F32)
        log_rows = tile_lanes(logs, tile, shape.span)
        low, high = position_range(shape, own_places(shape, tile, core), pack, bounds, bounds)
        heads = []
        for head in range(2):
            features = slice(head * HEAD_DIM, (head + 1) * HEAD_DIM)
            delta = jnp.sum(product[features], axis=0, keepdims=True)
            heads.append((one_head(query, head), one_head(grad, head), log_rows[head : head + 1], delta))
        grad_query[...] = jnp.zeros_like(grad_query)

        def per_step(step, unused):
            some, whole = row_conditions(shape, tile, step, pack, bounds)
            first = pl.multiple_of(step * shape.step, shape.step)

            def fold(masked):
                part = pl.ds(first, shape.step)
                key_rows, value_rows = key_all[part, :], value_all[part, :]
                if masked:
                    places = chip_places(shape, step, core)
                    allowed = jnp.logical_and(places >= low, places < high)
                scores = [matrix_product(key_rows, head[0]) for head in heads]
                changes = [matrix_product(value_rows, head[1]) for head in heads]
                if masked:
                    scores = [jnp.where(allowed, score, EXCLUDED) for score in scores]
                weights = [jnp.exp(score - head[2]) for score, head in zip(scores, heads)]
                diffs = [
                    (weight * (change - head[3])).astype(BF16)
                    for weight, change, head in zip(weights, changes, heads)
                ]
                key_part = times_transposed(
                    jnp.concatenate(diffs, axis=1),
                    jnp.concatenate([heads[0][0], heads[1][0]], axis=1),
                )
                value_part = times_transposed(
                    jnp.concatenate([weight.astype(BF16) for weight in weights], axis=1),
                    jnp.concatenate([heads[0][1], heads[1][1]], axis=1),
                )
                query_parts = [
                    matrix_product(key_t[head * HEAD_DIM : (head + 1) * HEAD_DIM, part], diffs[head])
                    for head in range(2)
                ]
                grad_query[...] += jnp.concatenate(query_parts, axis=0)
                grad_key[part, :] += key_part
                grad_value[part, :] += value_part

            pl.when(jnp.logical_and(some, whole))(functools.partial(fold, False))
            pl.when(jnp.logical_and(some, jnp.logical_not(whole)))(functools.partial(fold, True))
            return 0

        lax.fori_loop(0, tile + 1, per_step, 0)
        result = (grad_query[...] * HEAD_DIM**-0.5).astype(BF16)
        for block in range(shape.span):
            query_grads[tile * shape.span + block] = result[
                :, block * shape.rows : (block + 1) * shape.rows
            ]
        return 0

    lax.fori_loop(0, shape.tiles, per_tile, 0)
    for chip in range(shape.chips):
        for side, ref in enumerate((own_dkv, other_dkv)):
            first = (2 * chip + side) * shape.rows
            ref[chip, 0] = grad_key[first : first + shape.rows, :].astype(BF16)
            ref[chip, 1] = grad_value[first : first + shape.rows, :].astype(BF16)


def row_forward(shape, bounds, place, queries, own_kv, other_kv):
    length = shape.source_length
    return pl.pallas_call(
        functools.partial(row_forward_kernel, shape),
        out_shape=(
            jax.ShapeDtypeStruct(queries.shape, BF16),
            jax.ShapeDtypeStruct((shape.chips, 2, shape.rows), F32),
        ),
        in_specs=[smem()] * 2 + [vmem()] * 3,
        out_specs=(vmem(), vmem()),
        scratch_shapes=[
            pltpu.VMEM((length, PAIR), BF16),
            pltpu.VMEM((2, HEAD_DIM + STATS, length), BF16),
            pltpu.VMEM((8, shape.tile), F32),
            pltpu.VMEM((2, HEAD_DIM + STATS, shape.tile), F32),
        ],
        compiler_params=pltpu.CompilerParams(**PARAMS),
        cost_estimate=pl.CostEstimate(
            flops=6 * length * length * HEAD_DIM,
            bytes_accessed=4 * 1024 * 1024,
            transcendentals=length * length,
        ),
    )(bounds, place, queries, own_kv, other_kv)


def row_backward(shape, bounds, place, queries, outputs, logs, grads, own_kv, other_kv):
    length = shape.source_length
    return pl.pallas_call(
        functools.partial(row_backward_kernel, shape),
        out_shape=(
            jax.ShapeDtypeStruct(queries.shape, BF16),
            jax.ShapeDtypeStruct(own_kv.shape, BF16),
            jax.ShapeDtypeStruct(own_kv.shape, BF16),
        ),
        in_specs=[smem()] * 2 + [vmem()] * 6,
        out_specs=(vmem(), vmem(), vmem()),
        scratch_shapes=[
            pltpu.VMEM((length, PAIR), BF16),
            pltpu.VMEM((length, PAIR), BF16),
            pltpu.VMEM((PAIR, length), BF16),
            pltpu.VMEM((length, PAIR), F32),
            pltpu.VMEM((length, PAIR), F32),
            pltpu.VMEM((PAIR, shape.tile), F32),
        ],
        compiler_params=pltpu.CompilerParams(**PARAMS),
        cost_estimate=pl.CostEstimate(
            flops=12 * length * length * HEAD_DIM,
            bytes_accessed=6 * 1024 * 1024,
            transcendentals=length * length,
        ),
    )(bounds, place, queries, outputs, logs, grads, own_kv, other_kv)


def blocks(array):
    return pl.BlockSpec(array.shape, lambda step, zeros=(0,) * array.ndim: zeros)


def call(kernel, out_shape, args, grid=None, in_specs=None, out_specs=None, scratch=(), flops=0):
    if in_specs is None:
        in_specs = [vmem()] * len(args)
    if out_specs is None:
        out_specs = jax.tree.map(lambda _: vmem(), out_shape)
    extra = {} if grid is None else {"grid": grid}
    return pl.pallas_call(
        kernel,
        out_shape=out_shape,
        in_specs=in_specs,
        out_specs=out_specs,
        scratch_shapes=list(scratch),
        compiler_params=pltpu.CompilerParams(**PARAMS),
        cost_estimate=pl.CostEstimate(flops=flops, bytes_accessed=8 << 20, transcendentals=0),
        **extra,
    )(*args)


def project_self(x, wq, wk, wv, packs):
    rows, width = x.shape[0], wq.shape[1]
    pairs, each = width // PAIR, rows // packs

    def kernel(x_hbm, wq_hbm, wk_hbm, wv_hbm, out, x_ref, wq_ref, wk_ref, wv_ref, arrived):
        pairs_of = ((x_hbm, x_ref), (wq_hbm, wq_ref), (wk_hbm, wk_ref), (wv_hbm, wv_ref))
        copies = [
            pltpu.make_async_copy(source, target, arrived.at[number])
            for number, (source, target) in enumerate(pairs_of)
        ]
        for copy in copies:
            copy.start()
        copies[0].wait()
        copies[1].wait()
        value = x_ref[...]
        query = (matrix_product(value, wq_ref[...]) * HEAD_DIM**-0.5).astype(BF16)
        for pack in range(packs):
            for pair in range(pairs):
                part = query[pack * each : (pack + 1) * each, pair * PAIR : (pair + 1) * PAIR]
                out[pack * pairs + pair, 0] = part.T
        for number, ref in ((1, wk_ref), (2, wv_ref)):
            copies[number + 1].wait()
            result = matrix_product(value, ref[...]).astype(BF16)
            for pack in range(packs):
                for pair in range(pairs):
                    out[pack * pairs + pair, number] = result[
                        pack * each : (pack + 1) * each, pair * PAIR : (pair + 1) * PAIR
                    ]

    args = (x, wq, wk, wv)
    return pl.pallas_call(
        kernel,
        out_shape=jax.ShapeDtypeStruct((packs * pairs, 3, each, PAIR), BF16),
        in_specs=[pl.BlockSpec(memory_space=pl.ANY)] * 4,
        out_specs=vmem(),
        scratch_shapes=[pltpu.VMEM(value.shape, BF16) for value in args] + [pltpu.SemaphoreType.DMA((4,))],
        compiler_params=pltpu.CompilerParams(vmem_limit_bytes=60 * 1024 * 1024),
        cost_estimate=pl.CostEstimate(flops=6 * rows * x.shape[1] * width, bytes_accessed=8 << 20, transcendentals=0),
    )(*args)


def project_sources(x, wk, wv):
    rows, depth = x.shape
    pairs = wk.shape[1] // PAIR
    size = rows // 3 if rows % 48 == 0 else rows

    def kernel(x_ref, wk_ref, wv_ref, out):
        for number, ref in enumerate((wk_ref, wv_ref)):
            result = matrix_product(x_ref[...], ref[...]).astype(BF16)
            for pair in range(pairs):
                out[pair, number] = result[:, pair * PAIR : (pair + 1) * PAIR]

    return call(
        kernel,
        jax.ShapeDtypeStruct((pairs, 2, rows, PAIR), BF16),
        (x, wk, wv),
        grid=(rows // size,),
        in_specs=[pl.BlockSpec((size, depth), lambda i: (i, 0)), blocks(wk), blocks(wv)],
        out_specs=pl.BlockSpec((pairs, 2, size, PAIR), lambda i: (0, 0, i, 0)),
        flops=4 * rows * depth * wk.shape[1],
    )


def source_grads(grads, wk, wv):
    pairs, _, rows, _ = grads.shape
    size = rows // 3 if rows % 48 == 0 else rows
    depth = wk.shape[0]

    def kernel(grads_ref, wk_ref, wv_ref, out):
        keys = jnp.concatenate([grads_ref[pair, 0] for pair in range(pairs)], axis=1)
        values = jnp.concatenate([grads_ref[pair, 1] for pair in range(pairs)], axis=1)
        total = times_transposed(keys, wk_ref[...]) + times_transposed(values, wv_ref[...])
        out[...] = total.astype(BF16)

    return call(
        kernel,
        jax.ShapeDtypeStruct((rows, depth), BF16),
        (grads, wk, wv),
        grid=(rows // size,),
        in_specs=[
            pl.BlockSpec((pairs, 2, size, PAIR), lambda i: (0, 0, i, 0)),
            blocks(wk),
            blocks(wv),
        ],
        out_specs=pl.BlockSpec((size, depth), lambda i: (i, 0)),
        flops=4 * rows * depth * wk.shape[1],
    )


def input_grads(back, wq, wk, wv, packs):
    pairs = back.shape[0] // packs
    each = PAIR
    depth = wq.shape[0]

    def kernel(back_ref, wq_ref, wk_ref, wv_ref, out):
        for pack in range(packs):
            first = pack * pairs
            parts = [
                jnp.concatenate([back_ref[first + pair, 0 * PAIR : 1 * PAIR].T for pair in range(pairs)], axis=1),
                jnp.concatenate([back_ref[first + pair, 1 * PAIR : 2 * PAIR] for pair in range(pairs)], axis=1),
                jnp.concatenate([back_ref[first + pair, 2 * PAIR : 3 * PAIR] for pair in range(pairs)], axis=1),
            ]
            total = times_transposed(parts[0], wq_ref[...])
            total += times_transposed(parts[1], wk_ref[...])
            total += times_transposed(parts[2], wv_ref[...])
            out[pack * each : (pack + 1) * each, :] = total.astype(BF16)

    return call(
        kernel,
        jax.ShapeDtypeStruct((packs * each, depth), BF16),
        (back, wq, wk, wv),
        flops=6 * packs * each * depth * wq.shape[1],
    )


def self_weight_grads(x, back, packs, core):
    pairs = back.shape[0] // packs
    rows, depth = x.shape
    width = pairs * PAIR
    chips = back.shape[0]
    small = depth // (2 * chips)

    def kernel(core_ref, x_ref, back_ref, keep, send, turned):
        turned[...] = x_ref[...].T.reshape(turned.shape)
        mine = core_ref[0]
        for which, out in ((mine, keep), (1 - mine, send)):
            value = jnp.concatenate([turned[2 * chip + which] for chip in range(chips)], axis=0)
            for number in range(3):
                parts = []
                for pair in range(pairs):
                    here = slice(number * PAIR, (number + 1) * PAIR)
                    found = [back_ref[pack * pairs + pair, here] for pack in range(packs)]
                    parts.append(jnp.concatenate(found, axis=1 if number == 0 else 0))
                if number == 0:
                    result = times_transposed(value, jnp.concatenate(parts, axis=0))
                else:
                    result = matrix_product(value, jnp.concatenate(parts, axis=1))
                out[:, :, number * width : (number + 1) * width] = result.astype(BF16).reshape(
                    chips, small, width
                )

    shape = jax.ShapeDtypeStruct((chips, small, 3 * width), BF16)
    return call(
        kernel,
        (shape, shape),
        (core.reshape(1), x, back),
        in_specs=[smem(), vmem(), vmem()],
        scratch=[pltpu.VMEM((2 * chips, small, rows), BF16)],
        flops=2 * rows * depth * 3 * width,
    )


def halve(values, mine, axes, cuts):
    flat = [array for group in values for array in group]
    outs = []
    for group, axis, cut in zip(values, axes, cuts):
        shape = list(group[0].shape)
        del shape[axis]
        shape[-1] = cut[1] - cut[0]
        outs.extend([jax.ShapeDtypeStruct(tuple(shape), F32), jax.ShapeDtypeStruct(tuple(shape), BF16)])

    def kernel(mine_ref, *refs):
        sources, targets = refs[: len(flat)], refs[len(flat) :]
        first = 0
        for number, (group, axis, cut) in enumerate(zip(values, axes, cuts)):
            refs_here = sources[first : first + len(group)]
            first += len(group)
            which = mine_ref[number]
            for index, target in ((which, targets[2 * number]), (1 - which, targets[2 * number + 1])):
                place = (slice(None),) * axis + (index, Ellipsis, slice(*cut))
                total = sum(ref[place].astype(F32) for ref in refs_here)
                target[...] = total.astype(target.dtype)

    found = call(
        kernel,
        tuple(outs),
        (jnp.stack(mine).astype(jnp.int32), *flat),
        in_specs=[smem()] + [vmem()] * len(flat),
    )
    return list(zip(found[0::2], found[1::2]))


def last_sums(first, second, pieces):
    rows, half = first[0].shape
    width = 2 * half // pieces

    def kernel(*refs):
        left = refs[0][...] + refs[1][...].astype(F32)
        right = refs[2][...] + refs[3][...].astype(F32)
        whole = jnp.concatenate([left, right], axis=1)
        for number, out in enumerate(refs[4:]):
            out[...] = whole[:, number * width : (number + 1) * width]

    return call(
        kernel,
        tuple(jax.ShapeDtypeStruct((rows, width), F32) for _ in range(pieces)),
        (*first, *second),
    )


def spread_adapters(gathered, half):
    depth = gathered.shape[0]

    def kernel(source, up, down, sums):
        up[...] = source[:, :half].T.astype(F32)
        down[...] = source[:, half : 2 * half].astype(F32)
        sums[...] = source[:, 2 * half :].T[:4].astype(F32)

    return call(
        kernel,
        (
            jax.ShapeDtypeStruct((half, depth), F32),
            jax.ShapeDtypeStruct((depth, half), F32),
            jax.ShapeDtypeStruct((4, depth), F32),
        ),
        (gathered,),
    )


def spread_middle(early, middle):
    rows, width = early.shape

    def kernel(early_ref, middle_ref, cross_out, self_out, query, key, value):
        cross_out[...] = early_ref[...].astype(F32).T
        self_out[...] = middle_ref[:, :width].astype(F32).T
        for number, ref in enumerate((query, key, value)):
            ref[...] = middle_ref[:, (number + 1) * width : (number + 2) * width].astype(F32)

    turned, straight = jax.ShapeDtypeStruct((width, rows), F32), jax.ShapeDtypeStruct((rows, width), F32)
    return call(kernel, (turned, turned, straight, straight, straight), (early, middle))


GELU_ROOT = 0.7978845608028654
GELU_CUBE = 0.044715


def gelu_and_slope(value):
    square = value * value
    bend = jnp.tanh(GELU_ROOT * (value + GELU_CUBE * value * square))
    slope = 0.5 * (1.0 + bend) + 0.5 * value * (1.0 - bend * bend) * GELU_ROOT * (
        1.0 + 3.0 * GELU_CUBE * square
    )
    return 0.5 * value * (1.0 + bend), slope


def row(vector):
    return vector.reshape(1, -1)


def whole_sum(parts):
    if len(parts) == 2:
        return parts[0][...].astype(F32) + parts[1][...].astype(F32)
    own, met, own_weight, met_weight = parts
    return transposed_times(own[...], own_weight[...]) + transposed_times(met[...], met_weight[...])


def whole_sum_back(parts):
    if len(parts) == 2:
        return whole_sum(parts)
    own, met, own_weight, met_weight = parts
    return contract(own[...], own_weight[...], 0, 1) + contract(met[...], met_weight[...], 0, 1)


def normed(values):
    average = jnp.mean(values, axis=-1, keepdims=True)
    centred = values - average
    scale = lax.rsqrt(jnp.mean(centred * centred, axis=-1, keepdims=True) + 1e-05)
    return centred * scale, scale


def norm_rows_back(unit, scale, gain, grad, sums_ref):
    scaled = grad * gain
    first = jnp.mean(scaled, axis=-1, keepdims=True)
    second = jnp.mean(scaled * unit, axis=-1, keepdims=True)
    sums_ref[0:1, :] = jnp.sum(grad * unit, axis=0, keepdims=True)
    sums_ref[1:2, :] = jnp.sum(grad, axis=0, keepdims=True)
    return (scaled - first - unit * second) * scale


def first_norm(inputs, parts, gain, bias, query_weight, copies):
    rows, depth = inputs.shape
    pairs = query_weight.shape[1] // PAIR
    count = len(parts)

    def kernel(inputs_ref, *refs):
        gain_ref, bias_ref, weight_ref, one, out = refs[count:]
        unit, scale = normed(inputs_ref[...].astype(F32) + whole_sum(refs[:count]))
        value = unit * gain_ref[...] + bias_ref[...]
        one[:, :depth] = value
        one[:, depth:] = jnp.broadcast_to(scale, (rows, PAIR))
        query = matrix_product(value.astype(BF16), weight_ref[...]).astype(BF16).astype(F32)
        query = (query * HEAD_DIM**-0.5).astype(BF16)
        for pair in range(pairs):
            turned = query[:, pair * PAIR : (pair + 1) * PAIR].T
            for copy in range(copies):
                out[copy * pairs + pair] = turned

    return call(
        kernel,
        (
            jax.ShapeDtypeStruct((rows, depth + PAIR), F32),
            jax.ShapeDtypeStruct((copies * pairs, PAIR, rows), BF16),
        ),
        (inputs, *parts, row(gain), row(bias), query_weight),
        flops=4 * rows * depth * pairs * PAIR,
    )


def feed_forward(one, parts, gain, bias, ffn_in, ffn_out, down, up):
    rows, depth = one.shape[0], ffn_in.shape[0]
    count = len(parts)
    hidden, narrow_width = ffn_in.shape[1], down.shape[1]
    size = 512 if hidden % 512 == 0 else hidden
    steps = hidden // size

    def kernel(one_ref, *refs):
        gain_ref, bias_ref, in_ref, out_ref, down_ref, up_ref = refs[count : count + 6]
        two, slope_ref, narrow_ref, narrow_slope_ref, branch = refs[count + 6 :]
        unit, scale = normed(one_ref[:, :depth] + whole_sum(refs[:count]))
        value = unit * gain_ref[...] + bias_ref[...]
        rounded = value.astype(BF16)
        two[:, :depth] = value
        two[:, depth:] = jnp.broadcast_to(scale, (rows, PAIR))
        act, slope = gelu_and_slope(matrix_product(rounded, down_ref[...]))
        narrow_ref[...] = act.astype(BF16)
        narrow_slope_ref[...] = slope.astype(BF16)
        total = 4.0 * matrix_product(act.astype(BF16), up_ref[...])
        for step in range(steps):
            part = slice(step * size, (step + 1) * size)
            act, slope = gelu_and_slope(matrix_product(rounded, in_ref[:, part]))
            slope_ref[:, part] = slope.astype(BF16)
            total += matrix_product(act.astype(BF16), out_ref[part, :])
        branch[...] = total.astype(BF16)

    args = (one, *parts, row(gain), row(bias), ffn_in, ffn_out, down, up)
    outs = (
        jax.ShapeDtypeStruct((rows, depth + PAIR), F32),
        jax.ShapeDtypeStruct((rows, hidden), BF16),
        jax.ShapeDtypeStruct((rows, narrow_width), BF16),
        jax.ShapeDtypeStruct((rows, narrow_width), BF16),
        jax.ShapeDtypeStruct((rows, depth), BF16),
    )
    return call(kernel, outs, args, flops=4 * rows * depth * hidden)


def feed_backward(two, part, met, gain, bias, cotangent, slope, narrow_slope, ffn_in, ffn_out, down, up):
    rows, depth = two.shape[0], ffn_in.shape[0]
    hidden, narrow_width = ffn_in.shape[1], down.shape[1]
    size = 512 if hidden % 512 == 0 else hidden
    steps = hidden // size

    def kernel(
        two_ref, part_ref, met_ref, gain_ref, bias_ref, grad_ref, slope_ref, narrow_slope_ref,
        in_ref, out_ref, down_ref, up_ref, output, third, dnarrow, sums, share,
    ):
        unit, scale = normed(two_ref[:, :depth] + whole_sum((part_ref, met_ref)))
        output[...] = unit * gain_ref[...] + bias_ref[...]
        value = norm_rows_back(unit, scale, gain_ref[...], grad_ref[...].astype(F32), sums)
        rounded = value.astype(BF16)
        third[...] = value
        narrow = 4.0 * times_transposed(rounded, up_ref[...])
        narrow = (narrow * narrow_slope_ref[...].astype(F32)).astype(BF16)
        dnarrow[...] = narrow
        total = times_transposed(narrow, down_ref[...])
        for step in range(steps):
            part = slice(step * size, (step + 1) * size)
            grads = times_transposed(rounded, out_ref[part, :]) * slope_ref[:, part].astype(F32)
            total += times_transposed(grads.astype(BF16), in_ref[:, part])
        share[...] = total.astype(BF16)

    args = (two, part, met, row(gain), row(bias), cotangent, slope, narrow_slope, ffn_in, ffn_out, down, up)
    outs = (
        jax.ShapeDtypeStruct((rows, depth), F32),
        jax.ShapeDtypeStruct((rows, depth), F32),
        jax.ShapeDtypeStruct((rows, narrow_width), BF16),
        jax.ShapeDtypeStruct((2, depth), F32),
        jax.ShapeDtypeStruct((rows, depth), BF16),
    )
    return call(kernel, outs, args, flops=4 * rows * depth * hidden)


def second_norm_back(third, part, met, two, gain, bias, weight, attended, logs, copies):
    rows, depth = third.shape
    pairs = weight.shape[0] // PAIR

    def kernel(
        third_ref, part_ref, met_ref, two_ref, gain_ref, bias_ref, weight_ref, attended_ref, logs_ref,
        second, sums, out,
    ):
        grad = third_ref[...] + whole_sum((part_ref, met_ref))
        unit = (two_ref[:, :depth] - bias_ref[...]) * (1.0 / gain_ref[...])
        value = norm_rows_back(unit, two_ref[:, depth : depth + 1], gain_ref[...], grad, sums)
        second[...] = value
        grads = times_transposed(weight_ref[...], value.astype(BF16)).astype(BF16)
        for pair in range(pairs):
            low = grads[pair * PAIR : (pair + 1) * PAIR]
            for copy in range(copies):
                out[copy * pairs + pair, :PAIR, :] = low
            low = low.astype(F32)
            first, later = [], []
            for side in range(2):
                head = 2 * pair + side
                product = low[side * HEAD_DIM : (side + 1) * HEAD_DIM] * attended_ref[head]
                first.extend(split_low(logs_ref[head : head + 1, :]))
                later.extend(split_low(jnp.sum(product, axis=0, keepdims=True)))
            statistics = stat_rows(first + later, rows)
            for copy in range(copies):
                out[copy * pairs + pair, PAIR : PAIR + STATS, :] = statistics

    return call(
        kernel,
        (
            jax.ShapeDtypeStruct((rows, depth), F32),
            jax.ShapeDtypeStruct((2, depth), F32),
            jax.ShapeDtypeStruct((copies * pairs, PAIR + STATS, rows), BF16),
        ),
        (third, part, met, two, row(gain), row(bias), weight, attended, logs),
        flops=2 * rows * depth * pairs * PAIR,
    )


def first_norm_back(second, parts, one, gain, bias, weight, packs):
    rows, depth = second.shape
    pairs, each = weight.shape[0] // PAIR, rows // packs
    count = len(parts)

    def kernel(second_ref, *refs):
        one_ref, gain_ref, bias_ref, weight_ref, first, sums, out = refs[count:]
        grad = second_ref[...] + whole_sum_back(refs[:count])
        unit = (one_ref[:, :depth] - bias_ref[...]) * (1.0 / gain_ref[...])
        value = norm_rows_back(unit, one_ref[:, depth : depth + 1], gain_ref[...], grad, sums)
        first[...] = value
        grads = times_transposed(weight_ref[...], value.astype(BF16)).astype(BF16)
        for pack in range(packs):
            for pair in range(pairs):
                out[pack, pair] = grads[pair * PAIR : (pair + 1) * PAIR, pack * each : (pack + 1) * each]

    return call(
        kernel,
        (
            jax.ShapeDtypeStruct((rows, depth), F32),
            jax.ShapeDtypeStruct((2, depth), F32),
            jax.ShapeDtypeStruct((packs, pairs, PAIR, each), BF16),
        ),
        (second, *parts, one, row(gain), row(bias), weight),
        flops=2 * rows * depth * pairs * PAIR,
    )


def early_weight_grads(second, mixed_cross, third, narrow, two, narrow_grads, second_sums, third_sums):
    depth, width = second.shape[1], mixed_cross.shape[0]
    half = narrow.shape[1]

    def kernel(
        second_ref, cross_ref, third_ref, narrow_ref, two_ref, dnarrow_ref, second_sums_ref, third_sums_ref, out
    ):
        out[:, :width] = times_transposed(second_ref[...].astype(BF16).T, cross_ref[...]).astype(BF16)
        up = 4.0 * matrix_product(third_ref[...].astype(BF16).T, narrow_ref[...])
        out[:, width : width + half] = up.astype(BF16)
        down = matrix_product(two_ref[:, :depth].astype(BF16).T, dnarrow_ref[...])
        out[:, width + half : 2 * width] = down.astype(BF16)
        sums = jnp.concatenate(
            [second_sums_ref[...], third_sums_ref[...], jnp.zeros((PAIR - 4, depth), F32)], axis=0
        )
        out[:, 2 * width :] = sums.T.astype(BF16)

    args = (second, mixed_cross, third, narrow, two, narrow_grads, second_sums, third_sums)
    return call(
        kernel,
        jax.ShapeDtypeStruct((depth, 2 * width + PAIR), BF16),
        args,
        flops=4 * depth * width * second.shape[0],
    )


def middle_weight_grads(first, mixed_self, one, query_grads, source, source_dkv):
    depth = first.shape[1]
    width = mixed_self.shape[0]
    pairs = width // PAIR

    def kernel(first_ref, self_ref, one_ref, query_ref, source_ref, dkv_ref, out):
        step = pl.program_id(0)

        def rows_by_features(left, right):
            out[...] = times_transposed(left[:, :depth].astype(BF16).T, right[...]).astype(BF16)

        pl.when(step == 0)(lambda: rows_by_features(first_ref, self_ref))
        pl.when(step == 1)(lambda: rows_by_features(one_ref, query_ref))

        def sources(number):
            right = jnp.concatenate([dkv_ref[pair, number] for pair in range(pairs)], axis=1)
            out[...] = matrix_product(source_ref[...].T, right).astype(BF16)

        pl.when(step == 2)(lambda: sources(0))
        pl.when(step == 3)(lambda: sources(1))

    args = (first, mixed_self, one, query_grads, source, source_dkv)
    return call(
        kernel,
        jax.ShapeDtypeStruct((depth, 4 * width), BF16),
        args,
        grid=(4,),
        in_specs=[blocks(value) for value in args],
        out_specs=pl.BlockSpec((depth, width), lambda i: (0, i)),
        flops=2 * depth * width * 2048,
    )


def on_device(
    seq_size,
    head_size,
    inputs,
    encoded,
    tgt_bounds,
    src_bounds,
    self_query,
    self_key,
    self_value,
    self_out,
    cross_query,
    cross_key,
    cross_value,
    cross_out,
    ffn_in,
    ffn_out,
    adapter_down,
    adapter_up,
    norm1_gain,
    norm1_bias,
    norm2_gain,
    norm2_bias,
    norm3_gain,
    norm3_bias,
    cotangent,
):
    pack_count, row_count, model_width = inputs.shape
    source_rows = encoded.shape[1]
    local_width = self_query.shape[1]
    pairs_here = local_width // PAIR
    chips = seq_size // 2
    copies = chips // pairs_here
    rows = pack_count * row_count
    starts = tgt_bounds.shape[1]
    position = lax.axis_index("seq")
    core = position % 2
    base = position // (2 * pairs_here) * (2 * pairs_here)
    place = jnp.stack([base, core]).astype(jnp.int32)
    by_pack = pairs_here * pack_count == chips and seq_size == 16 and row_count == PAIR
    row_place = jnp.stack([position // (2 * pairs_here), core]).astype(jnp.int32)
    row_shape = RowShape(chips, row_count, starts)
    self_bounds = (tgt_bounds.reshape(-1), tgt_bounds.reshape(-1))
    cross_bounds = (tgt_bounds.reshape(-1), src_bounds.reshape(-1))
    self_shape = Shape(chips, pairs_here, pack_count, row_count, row_count, starts, True)
    cross_shape = Shape(chips, pairs_here, pack_count, row_count, source_rows, starts, False)
    flat_inputs = inputs.reshape(rows, model_width)
    flat_encoded = encoded.reshape(pack_count * source_rows, model_width)

    all_chips = [[2 * chip + side for chip in range(chips)] for side in range(2)]
    near_chips = [
        [2 * (copy * pairs_here + pair) + side for pair in range(pairs_here)]
        for copy in range(copies)
        for side in range(2)
    ]

    def swap_core(value):
        return lax.ppermute(value, "seq", [(i, i ^ 1) for i in range(seq_size)])

    def to_all(value):
        return lax.all_to_all(value, "seq", 0, 0, axis_index_groups=all_chips, tiled=True)

    def to_near(value):
        if pairs_here == 1:
            return value
        return lax.all_to_all(value, "seq", 0, 0, axis_index_groups=near_chips, tiled=True)

    def exchange(value):
        low = value.astype(BF16)
        if head_size == 2:
            return low, lax.ppermute(low, "head", [(0, 1), (1, 0)])
        return lax.psum(low.astype(F32), "head"), jnp.zeros_like(low)

    def spread(message):
        own = to_all(message)
        return own, swap_core(own)

    def spread_queries(features):
        return spread(jnp.tile(features.reshape(pairs_here, -1, rows), (copies, 1, 1)))

    def pair_rows(keys, values):
        def cut(value):
            return value.reshape(-1, pairs_here, PAIR).transpose(1, 0, 2)

        return jnp.stack([cut(keys), cut(values)], axis=1)

    def join_rows(message):
        return message.transpose(1, 2, 0, 3).reshape(2, -1, local_width)

    def logs_of(message):
        stats = message[:, PAIR : PAIR + 4, :].astype(F32)
        return stats[:, 0::2] + stats[:, 1::2]

    def weighted(parts, logs):
        highest = jnp.max(logs, axis=0)
        weights = jnp.exp(logs - highest)
        denominator = jnp.sum(weights, axis=0)
        shares = weights / denominator
        split = parts.reshape(parts.shape[:-2] + (2, HEAD_DIM, rows)).astype(F32)
        merged = jnp.sum(split * shares[:, :, :, None, :], axis=0)
        return merged, highest + jnp.log(denominator)

    def collect(own_part, other_part):
        met = swap_core(other_part)
        parts = jnp.stack([own_part, met])
        logs = jnp.stack([logs_of(own_part), logs_of(met)])
        merged, total = weighted(parts[:, :, :PAIR], logs)
        high, low = split_parts(total)
        statistics = jnp.stack([high, low], axis=2).reshape(chips, 4, rows)
        statistics = jnp.pad(statistics, ((0, 0), (0, STATS - 4), (0, 0)))
        message = jnp.concatenate(
            [merged.reshape(chips, PAIR, rows).astype(BF16), statistics.astype(BF16)], axis=1
        )
        back = to_all(message)
        logs = logs_of(back).reshape(copies, pairs_here, 2, rows)
        features = back[:, :PAIR].reshape(copies, pairs_here, PAIR, rows)
        merged, total = weighted(features, logs)
        return merged, total

    def spread_grads(grad_features, merged, total):
        split = grad_features.reshape(pairs_here, 2, HEAD_DIM, rows).astype(F32)
        delta = jnp.sum(split * merged, axis=2)
        statistics = jnp.concatenate(
            [
                jnp.stack(split_parts(total), axis=2).reshape(pairs_here, 4, rows),
                jnp.stack(split_parts(delta), axis=2).reshape(pairs_here, 4, rows),
                jnp.zeros((pairs_here, STATS - 8, rows), F32),
            ],
            axis=1,
        ).astype(BF16)
        message = jnp.concatenate([grad_features.reshape(pairs_here, PAIR, rows), statistics], axis=1)
        return spread_queries(message)

    def collect_query_grads(own_part, other_part):
        total = (own_part.astype(F32) + swap_core(other_part).astype(F32)).astype(BF16)
        back = to_all(total).reshape(copies, local_width, rows)
        return jnp.sum(back.astype(F32), axis=0).astype(BF16)

    def scatter(joined):
        return lax.psum_scatter(joined, "seq", scatter_dimension=0, tiled=True)

    def scatter_by_halves(keep, send, done):
        width = keep.shape[2]

        def pass_on(value, bit):
            return lax.ppermute(value, "seq", [(i, i ^ bit) for i in range(seq_size)])

        values = [value.reshape(2, 2, 2, -1, width) for value in (keep, swap_core(send))]
        cuts = [(0, width // 2), (width // 2, width)]
        values = [values, values]
        for bits, axes in (((2, 4), (2, 1)), ((4, 2), (1, 1)), ((8, 8), (0, 0))):
            found = halve(values, [position // bit % 2 for bit in bits], axes, cuts)
            if bits == (8, 8):
                found, done = lax.optimization_barrier((found, done))
            values = [[kept, pass_on(sent, bit)] for (kept, sent), bit in zip(found, bits)]
            cuts = [(0, width // 2)] * 2
        return last_sums(*values, 3), done

    scaling = HEAD_DIM**-0.5
    cross_kv = project_sources(flat_encoded, cross_key, cross_value)
    if by_pack:
        message = project_self(flat_inputs, self_query, self_key, self_value, pack_count)
        met = to_all(message)
        self_q, self_kv = met[:, 0], met[:, 1:]
        self_kv_other = swap_core(self_kv)
        self_heads, self_logs = row_forward(
            row_shape, self_bounds[0], row_place, self_q, self_kv, self_kv_other
        )
        back = to_all(self_heads)
        back, cross_kv = lax.optimization_barrier((back, cross_kv))
        back = back.reshape(pack_count, pairs_here, PAIR, row_count)
        mixed_self = back.transpose(1, 2, 0, 3).reshape(local_width, rows)
    else:
        query_self = (contract(self_query, flat_inputs, 0, 1) * scaling).astype(BF16)
        key_self = matrix_product(flat_inputs, self_key).astype(BF16)
        value_self = matrix_product(flat_inputs, self_value).astype(BF16)
        self_q = spread_queries(query_self)
        self_kv = to_near(pair_rows(key_self, value_self))
        own_part, other_part = attention_forward(self_shape, self_bounds, place, *self_q, self_kv)
        attended_self, log_self = collect(own_part, other_part)
        mixed_self = attended_self.reshape(local_width, rows).astype(BF16)
    parts = exchange(transposed_times(mixed_self, self_out))
    normed_one, query_cross = first_norm(
        flat_inputs, parts, norm1_gain, norm1_bias, cross_query, copies
    )
    cross_kv = to_near(cross_kv)
    query_cross, cross_kv = lax.optimization_barrier((query_cross, cross_kv))
    cross_q = spread(query_cross)
    own_part, other_part = attention_forward(cross_shape, cross_bounds, place, *cross_q, cross_kv)
    attended_cross, log_cross = collect(own_part, other_part)
    mixed_cross = attended_cross.reshape(local_width, rows).astype(BF16)
    parts = exchange(transposed_times(mixed_cross, cross_out))
    normed_two, slope, narrow_low, narrow_slope, branch = feed_forward(
        normed_one, parts, norm2_gain, norm2_bias, ffn_in, ffn_out, adapter_down, adapter_up
    )
    part, met = exchange(branch)
    output, grad_third, grad_narrow, third_sums, grad_two_part = feed_backward(
        normed_two, part, met, norm3_gain, norm3_bias, cotangent.reshape(rows, model_width),
        slope, narrow_slope, ffn_in, ffn_out, adapter_down, adapter_up,
    )
    part, met = exchange(grad_two_part)
    grad_second, second_sums, message = second_norm_back(
        grad_third, part, met, normed_two, norm2_gain, norm2_bias, cross_out,
        attended_cross.reshape(-1, HEAD_DIM, rows), log_cross.reshape(-1, rows), copies,
    )
    early = early_weight_grads(
        grad_second, mixed_cross, grad_third, narrow_low, normed_two, grad_narrow,
        second_sums, third_sums,
    )
    cross_g = spread(message)
    early = scatter(early)
    own_part, other_part, cross_dkv = attention_backward(
        cross_shape, cross_bounds, place, *cross_q, *cross_g, cross_kv
    )
    grad_query_cross = collect_query_grads(own_part, other_part)
    grad_query_cross, early = lax.optimization_barrier((grad_query_cross, early))
    part, met = exchange(contract(grad_query_cross, cross_query, 0, 1))
    adapters_up, adapters_down, norms = spread_adapters(
        lax.all_gather(early[:, local_width:], "seq", axis=0, tiled=True), adapter_up.shape[0]
    )
    source_dkv = to_near(cross_dkv)
    grad_first, first_sums, grad_heads = first_norm_back(
        grad_second, (part, met), normed_one, norm1_gain, norm1_bias, self_out, pack_count
    )
    source_part = source_grads(source_dkv, cross_key, cross_value)
    middle = middle_weight_grads(
        grad_first, mixed_self, normed_one, grad_query_cross, flat_encoded, source_dkv
    )
    if by_pack:
        grad_heads = to_all(grad_heads.reshape(chips, PAIR, row_count))
        grad_heads, middle, source_part = lax.optimization_barrier((grad_heads, middle, source_part))
        source_part, source_met = exchange(source_part)
        dq, own_dkv, other_dkv = row_backward(
            row_shape, self_bounds[0], row_place, self_q, self_heads, self_logs, grad_heads,
            self_kv, self_kv_other,
        )
        dkv = (own_dkv.astype(F32) + swap_core(other_dkv).astype(F32)).astype(BF16)
        high, low = split_parts(first_sums + swap_core(first_sums))
        sums = jnp.concatenate([high, low]).astype(BF16).reshape(1, 1, -1, PAIR)
        sums = jnp.broadcast_to(sums, (chips,) + sums.shape[1:])[:, 0]
        message = jnp.concatenate([dq, dkv[:, 0], dkv[:, 1], sums], axis=1)
        back = to_all(message)
        first_sums = back[:, 3 * row_count :].astype(F32).reshape(chips, 2, 2, model_width)
        first_sums = jnp.sum(first_sums[:, 0] + first_sums[:, 1], axis=0)
        back, source_met = lax.optimization_barrier((back, source_met))
        keep, send = self_weight_grads(flat_inputs, back, pack_count, core)
        back, keep, send = lax.optimization_barrier((back, keep, send))
        self_grads, middle = scatter_by_halves(keep, send, scatter(middle))
        part, met = exchange(input_grads(back, self_query, self_key, self_value, pack_count))
        grad_inputs = grad_first + (part.astype(F32) + met.astype(F32))
    else:
        source_part, source_met = exchange(source_part)
        grad_mixed_self = grad_heads.transpose(1, 2, 0, 3).reshape(local_width, rows)
        self_g = spread_grads(grad_mixed_self, attended_self, log_self)
        own_part, other_part, self_dkv = attention_backward(
            self_shape, self_bounds, place, *self_q, *self_g, self_kv
        )
        grad_query_self = collect_query_grads(own_part, other_part)
        grad_key_self, grad_value_self = join_rows(to_near(self_dkv))
        grad_in_part = (
            transposed_times(grad_query_self, contract_t(self_query))
            + times_transposed(grad_key_self, self_key)
            + times_transposed(grad_value_self, self_value)
        )
        part, met = exchange(grad_in_part)
        grad_inputs = grad_first + (part.astype(F32) + met.astype(F32))
        grad_self_query = contract(flat_inputs, grad_query_self, 0, 1)
        grad_self_key = transposed_times(flat_inputs, grad_key_self)
        grad_self_value = transposed_times(flat_inputs, grad_value_self)
        self_parts = jnp.concatenate(
            [part.astype(BF16) for part in (grad_self_query, grad_self_key, grad_self_value)], axis=1
        )
        self_grads = jnp.split(scatter(self_parts).astype(F32), 3, axis=1)
        middle = scatter(middle)
        first_sums = jnp.sum(lax.all_gather(first_sums, "seq"), axis=0)

    grad_source = source_part.astype(F32) + source_met.astype(F32)
    cross_out_g, self_out_g, cross_query_g, cross_key_g, cross_value_g = spread_middle(
        early[:, :local_width], middle
    )
    self_query_g, self_key_g, self_value_g = self_grads
    return (
        output.reshape(pack_count, row_count, model_width),
        grad_inputs.reshape(pack_count, row_count, model_width),
        grad_source.reshape(pack_count, source_rows, model_width),
        self_query_g,
        self_key_g,
        self_value_g,
        self_out_g,
        cross_query_g,
        cross_key_g,
        cross_value_g,
        cross_out_g,
        adapters_down,
        adapters_up,
        first_sums[0],
        first_sums[1],
        norms[0],
        norms[1],
        norms[2],
        norms[3],
    )


def contract_t(weight):
    return weight.T


def solution(mesh):
    placed = (
        P(None, "seq", None),
        P(None, "seq", None),
        P(),
        P(),
        P(None, "head"),
        P(None, "head"),
        P(None, "head"),
        P("head", None),
        P(None, "head"),
        P(None, "head"),
        P(None, "head"),
        P("head", None),
        P(None, "head"),
        P("head", None),
        P(None, "head"),
        P("head", None),
        P(),
        P(),
        P(),
        P(),
        P(),
        P(),
        P(None, "seq", None),
    )
    return jax.shard_map(
        functools.partial(on_device, mesh.shape["seq"], mesh.shape["head"]),
        mesh=mesh,
        in_specs=placed,
        out_specs=(
            P(None, "seq", None),
            P(None, "seq", None),
            P(None, "seq", None),
            P("seq", "head"),
            P("seq", "head"),
            P("seq", "head"),
            P("head", "seq"),
            P("seq", "head"),
            P("seq", "head"),
            P("seq", "head"),
            P("head", "seq"),
            P(None, "head"),
            P("head", None),
            P(),
            P(),
            P(),
            P(),
            P(),
            P(),
        ),
        check_vma=False,
    )
```

```python
import functools

import jax
import jax.numpy as jnp
from jax import lax
from jax.experimental import pallas as pl
from jax.experimental.pallas import tpu as pltpu
from jax.sharding import PartitionSpec as P

HEAD_DIM = 64
PAIR = 2 * HEAD_DIM
STATS = 16
LOWEST = -1e29
EXCLUDED = -1e30
F32 = jnp.float32
BF16 = jnp.bfloat16


def matrix_product(left, right):
    return jnp.dot(left, right, preferred_element_type=F32)


def contract(left, right, left_dim, right_dim):
    return lax.dot_general(
        left, right, (((left_dim,), (right_dim,)), ((), ())), preferred_element_type=F32
    )


def times_transposed(left, right):
    return contract(left, right, 1, 1)


def transposed_times(left, right):
    return contract(left, right, 0, 0)


class Shape:
    def __init__(self, chips, groups, packs, rows, source_rows, starts, causal):
        self.chips, self.groups, self.packs, self.rows = chips, groups, packs, rows
        self.source_rows, self.starts, self.causal = source_rows, starts, causal
        self.step = groups
        while self.step > 1 and self.step * source_rows > 768:
            self.step //= 2
        self.steps = groups // self.step
        self.tile = 2 * rows
        self.length = 2 * chips * rows
        self.source_length = 2 * chips * source_rows


def position_range(shape, places, pack, target_bounds, source_bounds):
    starts = shape.starts
    low = jnp.zeros_like(places)
    high = jnp.zeros_like(places) + source_bounds[pack * starts]
    for entry in range(starts):
        later = places >= target_bounds[pack * starts + entry]
        low = jnp.where(later, source_bounds[pack * starts + entry], low)
        if entry + 1 < starts:
            following = source_bounds[pack * starts + entry + 1]
        else:
            following = jnp.int32(shape.source_length)
        high = jnp.where(later, following, high)
    if shape.causal:
        high = places + 1
    return low, high


def lane_places(shape, chip, core):
    lanes = lax.broadcasted_iota(jnp.int32, (1, shape.tile), 1)
    own = (2 * chip + core) * shape.rows + lanes
    other = (2 * chip + 1 - core) * shape.rows + lanes - shape.rows
    return jnp.where(lanes < shape.rows, own, other)


def step_conditions(shape, chip, pack, first_group, place, target_bounds, source_bounds):
    base, core = place[0], place[1]
    head = chip * (2 * shape.rows)
    tail = head + 2 * shape.rows - 1
    low_first, high_first = position_range(shape, head, pack, target_bounds, source_bounds)
    low_last, high_last = position_range(shape, tail, pack, target_bounds, source_bounds)
    begin = (base + 2 * first_group + core) * shape.source_rows
    end = begin + (2 * shape.step - 1) * shape.source_rows
    some = jnp.logical_and(low_first < end, high_last > begin)
    whole = jnp.logical_and(low_last <= begin, high_first >= end)
    return begin, some, whole


def source_places(shape, begin):
    size = shape.step * shape.source_rows
    rows = lax.broadcasted_iota(jnp.int32, (size, shape.tile), 0)
    places = begin + rows
    for group in range(1, shape.step):
        places = places + jnp.where(rows >= group * shape.source_rows, shape.source_rows, 0)
    return places


def both(own_ref, other_ref, chip, first, last, pack, rows):
    lanes = slice(pack * rows, (pack + 1) * rows)
    return jnp.concatenate(
        [own_ref[chip, first:last, lanes], other_ref[chip, first:last, lanes]], axis=1
    )


def one_head(pair_rows, head):
    feature = lax.broadcasted_iota(jnp.int32, pair_rows.shape, 0)
    mine = (feature >= HEAD_DIM) if head else (feature < HEAD_DIM)
    return jnp.where(mine, pair_rows, jnp.zeros_like(pair_rows))


def split_low(value):
    high = value.astype(BF16).astype(F32)
    return high, value - high


def split_parts(value):
    high = lax.reduce_precision(value, 8, 7)
    return high, value - high


def stat_rows(rows, width):
    index = lax.broadcasted_iota(jnp.int32, (STATS, width), 0)
    total = jnp.zeros((STATS, width), F32)
    for number, row in enumerate(rows):
        total = jnp.where(index == number, row, total)
    return total.astype(BF16)


def forward_kernel(
    shape, target_bounds, source_bounds, place, own_q, other_q, keys_values, own_out, other_out,
    value_t, maxima, total,
):
    step_rows = shape.step * shape.source_rows
    for group in range(shape.groups):
        for pack in range(shape.packs):
            part = slice(pack * shape.source_rows, (pack + 1) * shape.source_rows)
            lanes = slice(group * shape.source_rows, (group + 1) * shape.source_rows)
            turned = keys_values[group, 1, part, :].T
            for head in range(2):
                value_t[pack, head, :HEAD_DIM, lanes] = turned[head * HEAD_DIM : (head + 1) * HEAD_DIM]
    value_t[:, :, HEAD_DIM:, :] = jnp.ones((shape.packs, 2, STATS, value_t.shape[3]), BF16)

    for pack in range(shape.packs):
        part = slice(pack * shape.source_rows, (pack + 1) * shape.source_rows)

        def per_chip(chip, unused, pack=pack, part=part):
            query = both(own_q, other_q, chip, 0, PAIR, pack, shape.rows)
            low, high = position_range(
                shape, lane_places(shape, chip, place[1]), pack, target_bounds, source_bounds
            )
            maxima[...] = jnp.full_like(maxima, LOWEST)
            total[...] = jnp.zeros_like(total)
            for step in range(shape.steps):
                groups = slice(step * shape.step, (step + 1) * shape.step)
                begin, some, whole = step_conditions(
                    shape, chip, pack, step * shape.step, place, target_bounds, source_bounds
                )

                def fold(masked, step=step, groups=groups, begin=begin):
                    key_rows = keys_values[groups, 0, part, :].reshape(step_rows, PAIR)
                    if masked:
                        places = source_places(shape, begin)
                        allowed = jnp.logical_and(places >= low, places < high)
                    befores = [maxima[head : head + 1, :] for head in range(2)]
                    scores = [matrix_product(key_rows, one_head(query, head)) for head in range(2)]
                    if masked:
                        scores = [jnp.where(allowed, score, EXCLUDED) for score in scores]
                    nows = [
                        jnp.maximum(before, jnp.max(score, axis=0, keepdims=True))
                        for before, score in zip(befores, scores)
                    ]
                    weights = [jnp.exp(score - now) for score, now in zip(scores, nows)]
                    products = []
                    for head in range(2):
                        values = value_t[pack, head, :, step * step_rows : (step + 1) * step_rows]
                        products.append(matrix_product(values, weights[head].astype(BF16)))
                    for head in range(2):
                        fading = jnp.exp(befores[head] - nows[head])
                        maxima[head : head + 1, :] = nows[head]
                        total[head] = total[head] * fading + products[head]

                pl.when(jnp.logical_and(some, whole))(functools.partial(fold, False))
                pl.when(jnp.logical_and(some, jnp.logical_not(whole)))(
                    functools.partial(fold, True)
                )
            statistics = []
            for head in range(2):
                features = slice(head * HEAD_DIM, (head + 1) * HEAD_DIM)
                found = total[head, HEAD_DIM : HEAD_DIM + 1, :]
                divisor = jnp.maximum(found, 1e-37)
                filled = found > 0.0
                logs = jnp.where(filled, maxima[head : head + 1, :] + jnp.log(divisor), LOWEST)
                statistics.extend(split_low(logs))
                result = (total[head, :HEAD_DIM, :] / divisor).astype(BF16)
                for ref, offset in ((own_out, 0), (other_out, shape.rows)):
                    ref[chip, features, pack * shape.rows : (pack + 1) * shape.rows] = result[
                        :, offset : offset + shape.rows
                    ]
            statistics = stat_rows(statistics, shape.tile)
            for ref, offset in ((own_out, 0), (other_out, shape.rows)):
                ref[chip, PAIR : PAIR + STATS, pack * shape.rows : (pack + 1) * shape.rows] = (
                    statistics[:, offset : offset + shape.rows]
                )
            return 0

        lax.fori_loop(0, shape.chips, per_chip, 0)


def backward_kernel(
    shape, target_bounds, source_bounds, place, own_q, other_q, own_g, other_g, keys_values,
    own_dq, other_dq, key_grads, key_t, grad_key, grad_value, grad_query,
):
    step_rows = shape.step * shape.source_rows
    grad_key[...] = jnp.zeros_like(grad_key)
    grad_value[...] = jnp.zeros_like(grad_value)
    for group in range(shape.groups):
        for pack in range(shape.packs):
            part = slice(pack * shape.source_rows, (pack + 1) * shape.source_rows)
            key_t[pack, :, group * shape.source_rows : (group + 1) * shape.source_rows] = (
                keys_values[group, 0, part, :].T
            )

    for pack in range(shape.packs):
        part = slice(pack * shape.source_rows, (pack + 1) * shape.source_rows)

        def per_chip(chip, unused, pack=pack, part=part):
            query = both(own_q, other_q, chip, 0, PAIR, pack, shape.rows)
            grads = both(own_g, other_g, chip, 0, PAIR, pack, shape.rows)
            statistics = both(own_g, other_g, chip, PAIR, PAIR + STATS, pack, shape.rows).astype(F32)
            low, high = position_range(
                shape, lane_places(shape, chip, place[1]), pack, target_bounds, source_bounds
            )
            queries = [one_head(query, head) for head in range(2)]
            gradients = [one_head(grads, head) for head in range(2)]
            log_rows = [statistics[2 * head : 2 * head + 1] + statistics[2 * head + 1 : 2 * head + 2] for head in range(2)]
            deltas = [statistics[2 * head + 4 : 2 * head + 5] + statistics[2 * head + 5 : 2 * head + 6] for head in range(2)]
            grad_query[...] = jnp.zeros_like(grad_query)
            for step in range(shape.steps):
                groups = slice(step * shape.step, (step + 1) * shape.step)
                begin, some, whole = step_conditions(
                    shape, chip, pack, step * shape.step, place, target_bounds, source_bounds
                )

                def fold(masked, step=step, groups=groups, begin=begin):
                    key_rows = keys_values[groups, 0, part, :].reshape(step_rows, PAIR)
                    value_rows = keys_values[groups, 1, part, :].reshape(step_rows, PAIR)
                    if masked:
                        places = source_places(shape, begin)
                        allowed = jnp.logical_and(places >= low, places < high)
                    lanes = slice(step * step_rows, (step + 1) * step_rows)
                    scores = [matrix_product(key_rows, queries[head]) for head in range(2)]
                    changes = [matrix_product(value_rows, gradients[head]) for head in range(2)]
                    if masked:
                        scores = [jnp.where(allowed, score, EXCLUDED) for score in scores]
                    weights = [jnp.exp(score - row) for score, row in zip(scores, log_rows)]
                    diffs = [
                        (weight * (change - delta)).astype(BF16)
                        for weight, change, delta in zip(weights, changes, deltas)
                    ]
                    key_part = times_transposed(
                        jnp.concatenate(diffs, axis=1), jnp.concatenate(queries, axis=1)
                    )
                    value_part = times_transposed(
                        jnp.concatenate([weight.astype(BF16) for weight in weights], axis=1),
                        jnp.concatenate(gradients, axis=1),
                    )
                    query_parts = [
                        matrix_product(
                            key_t[pack, head * HEAD_DIM : (head + 1) * HEAD_DIM, lanes], diffs[head]
                        )
                        for head in range(2)
                    ]
                    grad_query[...] += jnp.concatenate(query_parts, axis=0)
                    grad_key[pack, lanes, :] += key_part
                    grad_value[pack, lanes, :] += value_part

                pl.when(jnp.logical_and(some, whole))(functools.partial(fold, False))
                pl.when(jnp.logical_and(some, jnp.logical_not(whole)))(
                    functools.partial(fold, True)
                )
            result = (grad_query[...] * HEAD_DIM**-0.5).astype(BF16)
            for ref, offset in ((own_dq, 0), (other_dq, shape.rows)):
                ref[chip, :, pack * shape.rows : (pack + 1) * shape.rows] = result[
                    :, offset : offset + shape.rows
                ]
            return 0

        lax.fori_loop(0, shape.chips, per_chip, 0)

    for group in range(shape.groups):
        for pack in range(shape.packs):
            part = slice(pack * shape.source_rows, (pack + 1) * shape.source_rows)
            lanes = slice(group * shape.source_rows, (group + 1) * shape.source_rows)
            key_grads[group, 0, part, :] = grad_key[pack, lanes, :].astype(BF16)
            key_grads[group, 1, part, :] = grad_value[pack, lanes, :].astype(BF16)


def smem():
    return pl.BlockSpec(memory_space=pltpu.SMEM)


def vmem():
    return pl.BlockSpec(memory_space=pltpu.VMEM)


PARAMS = dict(vmem_limit_bytes=16 * 1024 * 1024)


def attention_forward(shape, bounds, place, own_q, other_q, keys_values):
    width = shape.packs * shape.rows
    pairs = shape.packs * shape.length * shape.groups * shape.source_rows
    message = jax.ShapeDtypeStruct((shape.chips, PAIR + STATS, width), BF16)
    return pl.pallas_call(
        functools.partial(forward_kernel, shape),
        out_shape=(message, message),
        in_specs=[smem()] * 3 + [vmem()] * 3,
        out_specs=(vmem(), vmem()),
        scratch_shapes=[
            pltpu.VMEM((shape.packs, 2, HEAD_DIM + STATS, shape.groups * shape.source_rows), BF16),
            pltpu.VMEM((8, shape.tile), F32),
            pltpu.VMEM((2, HEAD_DIM + STATS, shape.tile), F32),
        ],
        compiler_params=pltpu.CompilerParams(**PARAMS),
        cost_estimate=pl.CostEstimate(
            flops=8 * pairs * HEAD_DIM, bytes_accessed=6 * 1024 * 1024, transcendentals=2 * pairs
        ),
    )(bounds[0], bounds[1], place, own_q, other_q, keys_values)


def attention_backward(shape, bounds, place, own_q, other_q, own_g, other_g, keys_values):
    width = shape.packs * shape.rows
    pairs = shape.packs * shape.length * shape.groups * shape.source_rows
    source = shape.groups * shape.source_rows
    message = jax.ShapeDtypeStruct((shape.chips, PAIR, width), BF16)
    return pl.pallas_call(
        functools.partial(backward_kernel, shape),
        out_shape=(message, message, jax.ShapeDtypeStruct(keys_values.shape, BF16)),
        in_specs=[smem()] * 3 + [vmem()] * 5,
        out_specs=(vmem(), vmem(), vmem()),
        scratch_shapes=[
            pltpu.VMEM((shape.packs, PAIR, source), BF16),
            pltpu.VMEM((shape.packs, source, PAIR), F32),
            pltpu.VMEM((shape.packs, source, PAIR), F32),
            pltpu.VMEM((PAIR, shape.tile), F32),
        ],
        compiler_params=pltpu.CompilerParams(**PARAMS),
        cost_estimate=pl.CostEstimate(
            flops=20 * pairs * HEAD_DIM, bytes_accessed=8 * 1024 * 1024, transcendentals=2 * pairs
        ),
    )(bounds[0], bounds[1], place, own_q, other_q, own_g, other_g, keys_values)


class RowShape:
    def __init__(self, chips, rows, starts):
        self.chips, self.rows, self.starts = chips, rows, starts
        self.source_length, self.causal = 2 * chips * rows, True
        self.span = 2 if chips % 2 == 0 else 1
        self.tiles = chips // self.span
        self.tile = self.span * rows
        self.step = 2 * self.span * rows


def own_places(shape, tile, core):
    lanes = lax.broadcasted_iota(jnp.int32, (1, shape.tile), 1)
    places = 2 * tile * shape.span * shape.rows + core * shape.rows + lanes
    for block in range(1, shape.span):
        places = places + jnp.where(lanes >= block * shape.rows, shape.rows, 0)
    return places


def chip_places(shape, step, core):
    rows = lax.broadcasted_iota(jnp.int32, (shape.step, shape.tile), 0)
    places = step * shape.step + rows
    for block in range(2 * shape.span):
        here = jnp.logical_and(rows >= block * shape.rows, rows < (block + 1) * shape.rows)
        shift = shape.rows * core if block % 2 == 0 else -shape.rows * core
        places = places + jnp.where(here, shift, 0)
    return places


def row_conditions(shape, tile, step, pack, bounds):
    head = tile * shape.step
    tail = head + shape.step - 1
    begin = step * shape.step
    end = begin + shape.step
    low_first, _ = position_range(shape, head, pack, bounds, bounds)
    low_last, _ = position_range(shape, tail, pack, bounds, bounds)
    some = low_first < end
    whole = jnp.logical_and(low_last <= begin, end <= head + 1)
    return some, whole


def fill_rows(shape, own_kv, other_kv, which, target, transposed):
    for chip in range(shape.chips):
        for side, ref in enumerate((own_kv, other_kv)):
            first = (2 * chip + side) * shape.rows
            block = ref[chip, which]
            if transposed and len(target.shape) == 3:
                for head in range(2):
                    target[head, :HEAD_DIM, first : first + shape.rows] = block.T[
                        head * HEAD_DIM : (head + 1) * HEAD_DIM
                    ]
            elif transposed:
                target[:, first : first + shape.rows] = block.T
            else:
                target[first : first + shape.rows, :] = block


def tile_lanes(ref, tile, span):
    return jnp.concatenate([ref[tile * span + block] for block in range(span)], axis=1)


def row_forward_kernel(
    shape, bounds, place, queries, own_kv, other_kv, out, logs, key_all, value_t, maxima, total
):
    pack, core = place[0], place[1]
    fill_rows(shape, own_kv, other_kv, 0, key_all, False)
    fill_rows(shape, own_kv, other_kv, 1, value_t, True)
    value_t[:, HEAD_DIM:, :] = jnp.ones((2, STATS, value_t.shape[2]), BF16)

    def per_tile(tile, unused):
        query = tile_lanes(queries, tile, shape.span)
        low, high = position_range(shape, own_places(shape, tile, core), pack, bounds, bounds)
        heads = [one_head(query, head) for head in range(2)]
        maxima[...] = jnp.full_like(maxima, LOWEST)
        total[...] = jnp.zeros_like(total)

        def per_step(step, unused):
            some, whole = row_conditions(shape, tile, step, pack, bounds)
            first = pl.multiple_of(step * shape.step, shape.step)

            def fold(masked):
                key_rows = key_all[pl.ds(first, shape.step), :]
                if masked:
                    places = chip_places(shape, step, core)
                    allowed = jnp.logical_and(places >= low, places < high)
                befores = [maxima[head : head + 1, :] for head in range(2)]
                scores = [matrix_product(key_rows, heads[head]) for head in range(2)]
                if masked:
                    scores = [jnp.where(allowed, score, EXCLUDED) for score in scores]
                nows = [
                    jnp.maximum(before, jnp.max(score, axis=0, keepdims=True))
                    for before, score in zip(befores, scores)
                ]
                weights = [jnp.exp(score - now) for score, now in zip(scores, nows)]
                products = [
                    matrix_product(value_t[head, :, pl.ds(first, shape.step)], weights[head].astype(BF16))
                    for head in range(2)
                ]
                for head in range(2):
                    fading = jnp.exp(befores[head] - nows[head])
                    maxima[head : head + 1, :] = nows[head]
                    total[head] = total[head] * fading + products[head]

            pl.when(jnp.logical_and(some, whole))(functools.partial(fold, False))
            pl.when(jnp.logical_and(some, jnp.logical_not(whole)))(functools.partial(fold, True))
            return 0

        lax.fori_loop(0, tile + 1, per_step, 0)
        for head in range(2):
            features = slice(head * HEAD_DIM, (head + 1) * HEAD_DIM)
            divisor = total[head, HEAD_DIM : HEAD_DIM + 1, :]
            result = (total[head, :HEAD_DIM, :] / divisor).astype(BF16)
            found = maxima[head : head + 1, :] + jnp.log(divisor)
            for block in range(shape.span):
                lanes = slice(block * shape.rows, (block + 1) * shape.rows)
                out[tile * shape.span + block, features, :] = result[:, lanes]
                logs[tile * shape.span + block, head : head + 1, :] = found[:, lanes]
        return 0

    lax.fori_loop(0, shape.tiles, per_tile, 0)


def row_backward_kernel(
    shape, bounds, place, queries, outputs, logs, grads, own_kv, other_kv,
    query_grads, own_dkv, other_dkv, key_all, value_all, key_t, grad_key, grad_value, grad_query,
):
    pack, core = place[0], place[1]
    fill_rows(shape, own_kv, other_kv, 0, key_all, False)
    fill_rows(shape, own_kv, other_kv, 1, value_all, False)
    fill_rows(shape, own_kv, other_kv, 0, key_t, True)
    grad_key[...] = jnp.zeros_like(grad_key)
    grad_value[...] = jnp.zeros_like(grad_value)

    def per_tile(tile, unused):
        query = tile_lanes(queries, tile, shape.span)
        grad = tile_lanes(grads, tile, shape.span)
        product = grad.astype(F32) * tile_lanes(outputs, tile, shape.span).astype(F32)
        log_rows = tile_lanes(logs, tile, shape.span)
        low, high = position_range(shape, own_places(shape, tile, core), pack, bounds, bounds)
        heads = []
        for head in range(2):
            features = slice(head * HEAD_DIM, (head + 1) * HEAD_DIM)
            delta = jnp.sum(product[features], axis=0, keepdims=True)
            heads.append((one_head(query, head), one_head(grad, head), log_rows[head : head + 1], delta))
        grad_query[...] = jnp.zeros_like(grad_query)

        def per_step(step, unused):
            some, whole = row_conditions(shape, tile, step, pack, bounds)
            first = pl.multiple_of(step * shape.step, shape.step)

            def fold(masked):
                part = pl.ds(first, shape.step)
                key_rows, value_rows = key_all[part, :], value_all[part, :]
                if masked:
                    places = chip_places(shape, step, core)
                    allowed = jnp.logical_and(places >= low, places < high)
                scores = [matrix_product(key_rows, head[0]) for head in heads]
                changes = [matrix_product(value_rows, head[1]) for head in heads]
                if masked:
                    scores = [jnp.where(allowed, score, EXCLUDED) for score in scores]
                weights = [jnp.exp(score - head[2]) for score, head in zip(scores, heads)]
                diffs = [
                    (weight * (change - head[3])).astype(BF16)
                    for weight, change, head in zip(weights, changes, heads)
                ]
                key_part = times_transposed(
                    jnp.concatenate(diffs, axis=1),
                    jnp.concatenate([heads[0][0], heads[1][0]], axis=1),
                )
                value_part = times_transposed(
                    jnp.concatenate([weight.astype(BF16) for weight in weights], axis=1),
                    jnp.concatenate([heads[0][1], heads[1][1]], axis=1),
                )
                query_parts = [
                    matrix_product(key_t[head * HEAD_DIM : (head + 1) * HEAD_DIM, part], diffs[head])
                    for head in range(2)
                ]
                grad_query[...] += jnp.concatenate(query_parts, axis=0)
                grad_key[part, :] += key_part
                grad_value[part, :] += value_part

            pl.when(jnp.logical_and(some, whole))(functools.partial(fold, False))
            pl.when(jnp.logical_and(some, jnp.logical_not(whole)))(functools.partial(fold, True))
            return 0

        lax.fori_loop(0, tile + 1, per_step, 0)
        result = (grad_query[...] * HEAD_DIM**-0.5).astype(BF16)
        for block in range(shape.span):
            query_grads[tile * shape.span + block] = result[
                :, block * shape.rows : (block + 1) * shape.rows
            ]
        return 0

    lax.fori_loop(0, shape.tiles, per_tile, 0)
    for chip in range(shape.chips):
        for side, ref in enumerate((own_dkv, other_dkv)):
            first = (2 * chip + side) * shape.rows
            ref[chip, 0] = grad_key[first : first + shape.rows, :].astype(BF16)
            ref[chip, 1] = grad_value[first : first + shape.rows, :].astype(BF16)


def row_forward(shape, bounds, place, queries, own_kv, other_kv):
    length = shape.source_length
    return pl.pallas_call(
        functools.partial(row_forward_kernel, shape),
        out_shape=(
            jax.ShapeDtypeStruct(queries.shape, BF16),
            jax.ShapeDtypeStruct((shape.chips, 2, shape.rows), F32),
        ),
        in_specs=[smem()] * 2 + [vmem()] * 3,
        out_specs=(vmem(), vmem()),
        scratch_shapes=[
            pltpu.VMEM((length, PAIR), BF16),
            pltpu.VMEM((2, HEAD_DIM + STATS, length), BF16),
            pltpu.VMEM((8, shape.tile), F32),
            pltpu.VMEM((2, HEAD_DIM + STATS, shape.tile), F32),
        ],
        compiler_params=pltpu.CompilerParams(**PARAMS),
        cost_estimate=pl.CostEstimate(
            flops=6 * length * length * HEAD_DIM,
            bytes_accessed=4 * 1024 * 1024,
            transcendentals=length * length,
        ),
    )(bounds, place, queries, own_kv, other_kv)


def row_backward(shape, bounds, place, queries, outputs, logs, grads, own_kv, other_kv):
    length = shape.source_length
    return pl.pallas_call(
        functools.partial(row_backward_kernel, shape),
        out_shape=(
            jax.ShapeDtypeStruct(queries.shape, BF16),
            jax.ShapeDtypeStruct(own_kv.shape, BF16),
            jax.ShapeDtypeStruct(own_kv.shape, BF16),
        ),
        in_specs=[smem()] * 2 + [vmem()] * 6,
        out_specs=(vmem(), vmem(), vmem()),
        scratch_shapes=[
            pltpu.VMEM((length, PAIR), BF16),
            pltpu.VMEM((length, PAIR), BF16),
            pltpu.VMEM((PAIR, length), BF16),
            pltpu.VMEM((length, PAIR), F32),
            pltpu.VMEM((length, PAIR), F32),
            pltpu.VMEM((PAIR, shape.tile), F32),
        ],
        compiler_params=pltpu.CompilerParams(**PARAMS),
        cost_estimate=pl.CostEstimate(
            flops=12 * length * length * HEAD_DIM,
            bytes_accessed=6 * 1024 * 1024,
            transcendentals=length * length,
        ),
    )(bounds, place, queries, outputs, logs, grads, own_kv, other_kv)


def blocks(array):
    return pl.BlockSpec(array.shape, lambda step, zeros=(0,) * array.ndim: zeros)


def call(kernel, out_shape, args, grid=None, in_specs=None, out_specs=None, scratch=(), flops=0):
    if in_specs is None:
        in_specs = [vmem()] * len(args)
    if out_specs is None:
        out_specs = jax.tree.map(lambda _: vmem(), out_shape)
    extra = {} if grid is None else {"grid": grid}
    return pl.pallas_call(
        kernel,
        out_shape=out_shape,
        in_specs=in_specs,
        out_specs=out_specs,
        scratch_shapes=list(scratch),
        compiler_params=pltpu.CompilerParams(**PARAMS),
        cost_estimate=pl.CostEstimate(flops=flops, bytes_accessed=8 << 20, transcendentals=0),
        **extra,
    )(*args)


def project_self(x, wq, wk, wv, packs):
    rows, width = x.shape[0], wq.shape[1]
    pairs, each = width // PAIR, rows // packs

    def kernel(x_hbm, wq_hbm, wk_hbm, wv_hbm, out, x_ref, wq_ref, wk_ref, wv_ref, arrived):
        pairs_of = ((x_hbm, x_ref), (wq_hbm, wq_ref), (wk_hbm, wk_ref), (wv_hbm, wv_ref))
        copies = [
            pltpu.make_async_copy(source, target, arrived.at[number])
            for number, (source, target) in enumerate(pairs_of)
        ]
        for copy in copies:
            copy.start()
        copies[0].wait()
        copies[1].wait()
        value = x_ref[...]
        query = (matrix_product(value, wq_ref[...]) * HEAD_DIM**-0.5).astype(BF16)
        for pack in range(packs):
            for pair in range(pairs):
                part = query[pack * each : (pack + 1) * each, pair * PAIR : (pair + 1) * PAIR]
                out[pack * pairs + pair, 0] = part.T
        for number, ref in ((1, wk_ref), (2, wv_ref)):
            copies[number + 1].wait()
            result = matrix_product(value, ref[...]).astype(BF16)
            for pack in range(packs):
                for pair in range(pairs):
                    out[pack * pairs + pair, number] = result[
                        pack * each : (pack + 1) * each, pair * PAIR : (pair + 1) * PAIR
                    ]

    args = (x, wq, wk, wv)
    return pl.pallas_call(
        kernel,
        out_shape=jax.ShapeDtypeStruct((packs * pairs, 3, each, PAIR), BF16),
        in_specs=[pl.BlockSpec(memory_space=pl.ANY)] * 4,
        out_specs=vmem(),
        scratch_shapes=[pltpu.VMEM(value.shape, BF16) for value in args] + [pltpu.SemaphoreType.DMA((4,))],
        compiler_params=pltpu.CompilerParams(vmem_limit_bytes=60 * 1024 * 1024),
        cost_estimate=pl.CostEstimate(flops=6 * rows * x.shape[1] * width, bytes_accessed=8 << 20, transcendentals=0),
    )(*args)


def project_sources(x, wk, wv):
    rows, depth = x.shape
    pairs = wk.shape[1] // PAIR
    size = rows // 3 if rows % 48 == 0 else rows

    def kernel(x_ref, wk_ref, wv_ref, out):
        for number, ref in enumerate((wk_ref, wv_ref)):
            result = matrix_product(x_ref[...], ref[...]).astype(BF16)
            for pair in range(pairs):
                out[pair, number] = result[:, pair * PAIR : (pair + 1) * PAIR]

    return call(
        kernel,
        jax.ShapeDtypeStruct((pairs, 2, rows, PAIR), BF16),
        (x, wk, wv),
        grid=(rows // size,),
        in_specs=[pl.BlockSpec((size, depth), lambda i: (i, 0)), blocks(wk), blocks(wv)],
        out_specs=pl.BlockSpec((pairs, 2, size, PAIR), lambda i: (0, 0, i, 0)),
        flops=4 * rows * depth * wk.shape[1],
    )


def source_grads(grads, wk, wv):
    pairs, _, rows, _ = grads.shape
    size = rows // 3 if rows % 48 == 0 else rows
    depth = wk.shape[0]

    def kernel(grads_ref, wk_ref, wv_ref, out):
        keys = jnp.concatenate([grads_ref[pair, 0] for pair in range(pairs)], axis=1)
        values = jnp.concatenate([grads_ref[pair, 1] for pair in range(pairs)], axis=1)
        total = times_transposed(keys, wk_ref[...]) + times_transposed(values, wv_ref[...])
        out[...] = total.astype(BF16)

    return call(
        kernel,
        jax.ShapeDtypeStruct((rows, depth), BF16),
        (grads, wk, wv),
        grid=(rows // size,),
        in_specs=[
            pl.BlockSpec((pairs, 2, size, PAIR), lambda i: (0, 0, i, 0)),
            blocks(wk),
            blocks(wv),
        ],
        out_specs=pl.BlockSpec((size, depth), lambda i: (i, 0)),
        flops=4 * rows * depth * wk.shape[1],
    )


def input_grads(back, wq, wk, wv, packs):
    pairs = back.shape[0] // packs
    each = PAIR
    depth = wq.shape[0]

    def kernel(back_ref, wq_ref, wk_ref, wv_ref, out):
        for pack in range(packs):
            first = pack * pairs
            parts = [
                jnp.concatenate([back_ref[first + pair, 0 * PAIR : 1 * PAIR].T for pair in range(pairs)], axis=1),
                jnp.concatenate([back_ref[first + pair, 1 * PAIR : 2 * PAIR] for pair in range(pairs)], axis=1),
                jnp.concatenate([back_ref[first + pair, 2 * PAIR : 3 * PAIR] for pair in range(pairs)], axis=1),
            ]
            total = times_transposed(parts[0], wq_ref[...])
            total += times_transposed(parts[1], wk_ref[...])
            total += times_transposed(parts[2], wv_ref[...])
            out[pack * each : (pack + 1) * each, :] = total.astype(BF16)

    return call(
        kernel,
        jax.ShapeDtypeStruct((packs * each, depth), BF16),
        (back, wq, wk, wv),
        flops=6 * packs * each * depth * wq.shape[1],
    )


def self_weight_grads(x, back, packs, core):
    pairs = back.shape[0] // packs
    rows, depth = x.shape
    width = pairs * PAIR
    chips = back.shape[0]
    small = depth // (2 * chips)

    def kernel(core_ref, x_ref, back_ref, keep, send, turned):
        turned[...] = x_ref[...].T.reshape(turned.shape)
        mine = core_ref[0]
        for which, out in ((mine, keep), (1 - mine, send)):
            value = jnp.concatenate([turned[2 * chip + which] for chip in range(chips)], axis=0)
            for number in range(3):
                parts = []
                for pair in range(pairs):
                    here = slice(number * PAIR, (number + 1) * PAIR)
                    found = [back_ref[pack * pairs + pair, here] for pack in range(packs)]
                    parts.append(jnp.concatenate(found, axis=1 if number == 0 else 0))
                if number == 0:
                    result = times_transposed(value, jnp.concatenate(parts, axis=0))
                else:
                    result = matrix_product(value, jnp.concatenate(parts, axis=1))
                out[:, :, number * width : (number + 1) * width] = result.astype(BF16).reshape(
                    chips, small, width
                )

    shape = jax.ShapeDtypeStruct((chips, small, 3 * width), BF16)
    return call(
        kernel,
        (shape, shape),
        (core.reshape(1), x, back),
        in_specs=[smem(), vmem(), vmem()],
        scratch=[pltpu.VMEM((2 * chips, small, rows), BF16)],
        flops=2 * rows * depth * 3 * width,
    )


def merge_heads(parts, head):
    features = slice(head * HEAD_DIM, (head + 1) * HEAD_DIM)
    logs = []
    for part in parts:
        statistics = part[PAIR : PAIR + STATS, :].astype(F32)
        logs.append(statistics[2 * head : 2 * head + 1] + statistics[2 * head + 1 : 2 * head + 2])
    highest = functools.reduce(jnp.maximum, logs)
    weights = [jnp.exp(log - highest) for log in logs]
    total = sum(weights)
    merged = sum(part[features, :].astype(F32) * (weight / total) for part, weight in zip(parts, weights))
    return merged, highest + jnp.log(total)


def merge_cores(own, met):
    chips, _, rows = own.shape

    def kernel(own_ref, met_ref, out):
        for chip in range(chips):
            statistics = []
            for head in range(2):
                merged, total = merge_heads((own_ref[chip], met_ref[chip]), head)
                out[chip, head * HEAD_DIM : (head + 1) * HEAD_DIM, :] = merged.astype(BF16)
                statistics.extend(split_low(total))
            out[chip, PAIR : PAIR + STATS, :] = stat_rows(statistics, rows)

    return call(kernel, jax.ShapeDtypeStruct(own.shape, BF16), (own, met))


def finish_rows(back, weight, copies):
    pairs, rows = back.shape[0] // copies, back.shape[2]
    width, depth = weight.shape

    def kernel(back_ref, weight_ref, attended, logs, mixed, out):
        for pair in range(pairs):
            parts = [back_ref[copy * pairs + pair] for copy in range(copies)]
            for side in range(2):
                head = 2 * pair + side
                merged, total = merge_heads(parts, side)
                attended[head] = merged
                logs[head : head + 1, :] = total
                mixed[head * HEAD_DIM : (head + 1) * HEAD_DIM, :] = merged.astype(BF16)
        out[...] = transposed_times(mixed[...], weight_ref[...]).astype(BF16)

    return call(
        kernel,
        (
            jax.ShapeDtypeStruct((2 * pairs, HEAD_DIM, rows), F32),
            jax.ShapeDtypeStruct((2 * pairs, rows), F32),
            jax.ShapeDtypeStruct((width, rows), BF16),
            jax.ShapeDtypeStruct((rows, depth), BF16),
        ),
        (back, weight),
        flops=2 * rows * width * depth,
    )


def halve(values, mine, axes, cuts):
    flat = [array for group in values for array in group]
    outs = []
    for group, axis, cut in zip(values, axes, cuts):
        shape = list(group[0].shape)
        del shape[axis]
        shape[-1] = cut[1] - cut[0]
        outs.extend([jax.ShapeDtypeStruct(tuple(shape), F32), jax.ShapeDtypeStruct(tuple(shape), BF16)])

    def kernel(mine_ref, *refs):
        sources, targets = refs[: len(flat)], refs[len(flat) :]
        first = 0
        for number, (group, axis, cut) in enumerate(zip(values, axes, cuts)):
            refs_here = sources[first : first + len(group)]
            first += len(group)
            which = mine_ref[number]
            for index, target in ((which, targets[2 * number]), (1 - which, targets[2 * number + 1])):
                place = (slice(None),) * axis + (index, Ellipsis, slice(*cut))
                total = sum(ref[place].astype(F32) for ref in refs_here)
                target[...] = total.astype(target.dtype)

    found = call(
        kernel,
        tuple(outs),
        (jnp.stack(mine).astype(jnp.int32), *flat),
        in_specs=[smem()] + [vmem()] * len(flat),
    )
    return list(zip(found[0::2], found[1::2]))


def last_sums(first, second, pieces):
    rows, half = first[0].shape
    width = 2 * half // pieces

    def kernel(*refs):
        left = refs[0][...] + refs[1][...].astype(F32)
        right = refs[2][...] + refs[3][...].astype(F32)
        whole = jnp.concatenate([left, right], axis=1)
        for number, out in enumerate(refs[4:]):
            out[...] = whole[:, number * width : (number + 1) * width]

    return call(
        kernel,
        tuple(jax.ShapeDtypeStruct((rows, width), F32) for _ in range(pieces)),
        (*first, *second),
    )


def spread_adapters(gathered, half):
    depth = gathered.shape[0]

    def kernel(source, up, down, sums):
        up[...] = source[:, :half].T.astype(F32)
        down[...] = source[:, half : 2 * half].astype(F32)
        sums[...] = source[:, 2 * half :].T[:4].astype(F32)

    return call(
        kernel,
        (
            jax.ShapeDtypeStruct((half, depth), F32),
            jax.ShapeDtypeStruct((depth, half), F32),
            jax.ShapeDtypeStruct((4, depth), F32),
        ),
        (gathered,),
    )


def spread_middle(early, middle):
    rows, width = early.shape

    def kernel(early_ref, middle_ref, cross_out, self_out, query, key, value):
        cross_out[...] = early_ref[...].astype(F32).T
        self_out[...] = middle_ref[:, :width].astype(F32).T
        for number, ref in enumerate((query, key, value)):
            ref[...] = middle_ref[:, (number + 1) * width : (number + 2) * width].astype(F32)

    turned, straight = jax.ShapeDtypeStruct((width, rows), F32), jax.ShapeDtypeStruct((rows, width), F32)
    return call(kernel, (turned, turned, straight, straight, straight), (early, middle))


GELU_ROOT = 0.7978845608028654
GELU_CUBE = 0.044715


def gelu_and_slope(value):
    square = value * value
    bend = jnp.tanh(GELU_ROOT * (value + GELU_CUBE * value * square))
    slope = 0.5 * (1.0 + bend) + 0.5 * value * (1.0 - bend * bend) * GELU_ROOT * (
        1.0 + 3.0 * GELU_CUBE * square
    )
    return 0.5 * value * (1.0 + bend), slope


def row(vector):
    return vector.reshape(1, -1)


def whole_sum(parts):
    if len(parts) == 2:
        return parts[0][...].astype(F32) + parts[1][...].astype(F32)
    own, met, own_weight, met_weight = parts
    return transposed_times(own[...], own_weight[...]) + transposed_times(met[...], met_weight[...])


def whole_sum_back(parts):
    if len(parts) == 2:
        return whole_sum(parts)
    own, met, own_weight, met_weight = parts
    return contract(own[...], own_weight[...], 0, 1) + contract(met[...], met_weight[...], 0, 1)


def normed(values):
    average = jnp.mean(values, axis=-1, keepdims=True)
    centred = values - average
    scale = lax.rsqrt(jnp.mean(centred * centred, axis=-1, keepdims=True) + 1e-05)
    return centred * scale, scale


def norm_rows_back(unit, scale, gain, grad, sums_ref):
    scaled = grad * gain
    first = jnp.mean(scaled, axis=-1, keepdims=True)
    second = jnp.mean(scaled * unit, axis=-1, keepdims=True)
    sums_ref[0:1, :] = jnp.sum(grad * unit, axis=0, keepdims=True)
    sums_ref[1:2, :] = jnp.sum(grad, axis=0, keepdims=True)
    return (scaled - first - unit * second) * scale


def first_norm(inputs, parts, gain, bias, query_weight, copies):
    rows, depth = inputs.shape
    pairs = query_weight.shape[1] // PAIR
    count = len(parts)

    def kernel(inputs_ref, *refs):
        gain_ref, bias_ref, weight_ref, one, out = refs[count:]
        unit, scale = normed(inputs_ref[...].astype(F32) + whole_sum(refs[:count]))
        value = unit * gain_ref[...] + bias_ref[...]
        one[:, :depth] = value
        one[:, depth:] = jnp.broadcast_to(scale, (rows, PAIR))
        query = matrix_product(value.astype(BF16), weight_ref[...]).astype(BF16).astype(F32)
        query = (query * HEAD_DIM**-0.5).astype(BF16)
        for pair in range(pairs):
            turned = query[:, pair * PAIR : (pair + 1) * PAIR].T
            for copy in range(copies):
                out[copy * pairs + pair] = turned

    return call(
        kernel,
        (
            jax.ShapeDtypeStruct((rows, depth + PAIR), F32),
            jax.ShapeDtypeStruct((copies * pairs, PAIR, rows), BF16),
        ),
        (inputs, *parts, row(gain), row(bias), query_weight),
        flops=4 * rows * depth * pairs * PAIR,
    )


def feed_forward(one, parts, gain, bias, ffn_in, ffn_out, down, up):
    rows, depth = one.shape[0], ffn_in.shape[0]
    count = len(parts)
    hidden, narrow_width = ffn_in.shape[1], down.shape[1]
    size = 512 if hidden % 512 == 0 else hidden
    steps = hidden // size

    def kernel(one_ref, *refs):
        gain_ref, bias_ref, in_ref, out_ref, down_ref, up_ref = refs[count : count + 6]
        two, slope_ref, narrow_ref, narrow_slope_ref, branch = refs[count + 6 :]
        unit, scale = normed(one_ref[:, :depth] + whole_sum(refs[:count]))
        value = unit * gain_ref[...] + bias_ref[...]
        rounded = value.astype(BF16)
        two[:, :depth] = value
        two[:, depth:] = jnp.broadcast_to(scale, (rows, PAIR))
        act, slope = gelu_and_slope(matrix_product(rounded, down_ref[...]))
        narrow_ref[...] = act.astype(BF16)
        narrow_slope_ref[...] = slope.astype(BF16)
        total = 4.0 * matrix_product(act.astype(BF16), up_ref[...])
        for step in range(steps):
            part = slice(step * size, (step + 1) * size)
            act, slope = gelu_and_slope(matrix_product(rounded, in_ref[:, part]))
            slope_ref[:, part] = slope.astype(BF16)
            total += matrix_product(act.astype(BF16), out_ref[part, :])
        branch[...] = total.astype(BF16)

    args = (one, *parts, row(gain), row(bias), ffn_in, ffn_out, down, up)
    outs = (
        jax.ShapeDtypeStruct((rows, depth + PAIR), F32),
        jax.ShapeDtypeStruct((rows, hidden), BF16),
        jax.ShapeDtypeStruct((rows, narrow_width), BF16),
        jax.ShapeDtypeStruct((rows, narrow_width), BF16),
        jax.ShapeDtypeStruct((rows, depth), BF16),
    )
    return call(kernel, outs, args, flops=4 * rows * depth * hidden)


def feed_backward(two, part, met, gain, bias, cotangent, slope, narrow_slope, ffn_in, ffn_out, down, up):
    rows, depth = two.shape[0], ffn_in.shape[0]
    hidden, narrow_width = ffn_in.shape[1], down.shape[1]
    size = 512 if hidden % 512 == 0 else hidden
    steps = hidden // size

    def kernel(
        two_ref, part_ref, met_ref, gain_ref, bias_ref, grad_ref, slope_ref, narrow_slope_ref,
        in_ref, out_ref, down_ref, up_ref, output, third, dnarrow, sums, share,
    ):
        unit, scale = normed(two_ref[:, :depth] + whole_sum((part_ref, met_ref)))
        output[...] = unit * gain_ref[...] + bias_ref[...]
        value = norm_rows_back(unit, scale, gain_ref[...], grad_ref[...].astype(F32), sums)
        rounded = value.astype(BF16)
        third[...] = value
        narrow = 4.0 * times_transposed(rounded, up_ref[...])
        narrow = (narrow * narrow_slope_ref[...].astype(F32)).astype(BF16)
        dnarrow[...] = narrow
        total = times_transposed(narrow, down_ref[...])
        for step in range(steps):
            part = slice(step * size, (step + 1) * size)
            grads = times_transposed(rounded, out_ref[part, :]) * slope_ref[:, part].astype(F32)
            total += times_transposed(grads.astype(BF16), in_ref[:, part])
        share[...] = total.astype(BF16)

    args = (two, part, met, row(gain), row(bias), cotangent, slope, narrow_slope, ffn_in, ffn_out, down, up)
    outs = (
        jax.ShapeDtypeStruct((rows, depth), F32),
        jax.ShapeDtypeStruct((rows, depth), F32),
        jax.ShapeDtypeStruct((rows, narrow_width), BF16),
        jax.ShapeDtypeStruct((2, depth), F32),
        jax.ShapeDtypeStruct((rows, depth), BF16),
    )
    return call(kernel, outs, args, flops=4 * rows * depth * hidden)


def second_norm_back(third, part, met, two, gain, bias, weight, attended, logs, copies):
    rows, depth = third.shape
    pairs = weight.shape[0] // PAIR

    def kernel(
        third_ref, part_ref, met_ref, two_ref, gain_ref, bias_ref, weight_ref, attended_ref, logs_ref,
        second, sums, out,
    ):
        grad = third_ref[...] + whole_sum((part_ref, met_ref))
        unit = (two_ref[:, :depth] - bias_ref[...]) * (1.0 / gain_ref[...])
        value = norm_rows_back(unit, two_ref[:, depth : depth + 1], gain_ref[...], grad, sums)
        second[...] = value
        grads = times_transposed(weight_ref[...], value.astype(BF16)).astype(BF16)
        for pair in range(pairs):
            low = grads[pair * PAIR : (pair + 1) * PAIR]
            for copy in range(copies):
                out[copy * pairs + pair, :PAIR, :] = low
            low = low.astype(F32)
            first, later = [], []
            for side in range(2):
                head = 2 * pair + side
                product = low[side * HEAD_DIM : (side + 1) * HEAD_DIM] * attended_ref[head]
                first.extend(split_low(logs_ref[head : head + 1, :]))
                later.extend(split_low(jnp.sum(product, axis=0, keepdims=True)))
            statistics = stat_rows(first + later, rows)
            for copy in range(copies):
                out[copy * pairs + pair, PAIR : PAIR + STATS, :] = statistics

    return call(
        kernel,
        (
            jax.ShapeDtypeStruct((rows, depth), F32),
            jax.ShapeDtypeStruct((2, depth), F32),
            jax.ShapeDtypeStruct((copies * pairs, PAIR + STATS, rows), BF16),
        ),
        (third, part, met, two, row(gain), row(bias), weight, attended, logs),
        flops=2 * rows * depth * pairs * PAIR,
    )


def first_norm_back(second, parts, one, gain, bias, weight, packs):
    rows, depth = second.shape
    pairs, each = weight.shape[0] // PAIR, rows // packs
    count = len(parts)

    def kernel(second_ref, *refs):
        one_ref, gain_ref, bias_ref, weight_ref, first, sums, out = refs[count:]
        grad = second_ref[...] + whole_sum_back(refs[:count])
        unit = (one_ref[:, :depth] - bias_ref[...]) * (1.0 / gain_ref[...])
        value = norm_rows_back(unit, one_ref[:, depth : depth + 1], gain_ref[...], grad, sums)
        first[...] = value
        grads = times_transposed(weight_ref[...], value.astype(BF16)).astype(BF16)
        for pack in range(packs):
            for pair in range(pairs):
                out[pack, pair] = grads[pair * PAIR : (pair + 1) * PAIR, pack * each : (pack + 1) * each]

    return call(
        kernel,
        (
            jax.ShapeDtypeStruct((rows, depth), F32),
            jax.ShapeDtypeStruct((2, depth), F32),
            jax.ShapeDtypeStruct((packs, pairs, PAIR, each), BF16),
        ),
        (second, *parts, one, row(gain), row(bias), weight),
        flops=2 * rows * depth * pairs * PAIR,
    )


def early_weight_grads(second, mixed_cross, third, narrow, two, narrow_grads, second_sums, third_sums):
    depth, width = second.shape[1], mixed_cross.shape[0]
    half = narrow.shape[1]

    def kernel(
        second_ref, cross_ref, third_ref, narrow_ref, two_ref, dnarrow_ref, second_sums_ref, third_sums_ref, out
    ):
        out[:, :width] = times_transposed(second_ref[...].astype(BF16).T, cross_ref[...]).astype(BF16)
        up = 4.0 * matrix_product(third_ref[...].astype(BF16).T, narrow_ref[...])
        out[:, width : width + half] = up.astype(BF16)
        down = matrix_product(two_ref[:, :depth].astype(BF16).T, dnarrow_ref[...])
        out[:, width + half : 2 * width] = down.astype(BF16)
        sums = jnp.concatenate(
            [second_sums_ref[...], third_sums_ref[...], jnp.zeros((PAIR - 4, depth), F32)], axis=0
        )
        out[:, 2 * width :] = sums.T.astype(BF16)

    args = (second, mixed_cross, third, narrow, two, narrow_grads, second_sums, third_sums)
    return call(
        kernel,
        jax.ShapeDtypeStruct((depth, 2 * width + PAIR), BF16),
        args,
        flops=4 * depth * width * second.shape[0],
    )


def middle_weight_grads(first, mixed_self, one, query_grads, source, source_dkv):
    depth = first.shape[1]
    width = mixed_self.shape[0]
    pairs = width // PAIR

    def kernel(first_ref, self_ref, one_ref, query_ref, source_ref, dkv_ref, out):
        step = pl.program_id(0)

        def rows_by_features(left, right):
            out[...] = times_transposed(left[:, :depth].astype(BF16).T, right[...]).astype(BF16)

        pl.when(step == 0)(lambda: rows_by_features(first_ref, self_ref))
        pl.when(step == 1)(lambda: rows_by_features(one_ref, query_ref))

        def sources(number):
            right = jnp.concatenate([dkv_ref[pair, number] for pair in range(pairs)], axis=1)
            out[...] = matrix_product(source_ref[...].T, right).astype(BF16)

        pl.when(step == 2)(lambda: sources(0))
        pl.when(step == 3)(lambda: sources(1))

    args = (first, mixed_self, one, query_grads, source, source_dkv)
    return call(
        kernel,
        jax.ShapeDtypeStruct((depth, 4 * width), BF16),
        args,
        grid=(4,),
        in_specs=[blocks(value) for value in args],
        out_specs=pl.BlockSpec((depth, width), lambda i: (0, i)),
        flops=2 * depth * width * 2048,
    )


def on_device(
    seq_size,
    head_size,
    inputs,
    encoded,
    tgt_bounds,
    src_bounds,
    self_query,
    self_key,
    self_value,
    self_out,
    cross_query,
    cross_key,
    cross_value,
    cross_out,
    ffn_in,
    ffn_out,
    adapter_down,
    adapter_up,
    norm1_gain,
    norm1_bias,
    norm2_gain,
    norm2_bias,
    norm3_gain,
    norm3_bias,
    cotangent,
):
    pack_count, row_count, model_width = inputs.shape
    source_rows = encoded.shape[1]
    local_width = self_query.shape[1]
    pairs_here = local_width // PAIR
    chips = seq_size // 2
    copies = chips // pairs_here
    rows = pack_count * row_count
    starts = tgt_bounds.shape[1]
    position = lax.axis_index("seq")
    core = position % 2
    base = position // (2 * pairs_here) * (2 * pairs_here)
    place = jnp.stack([base, core]).astype(jnp.int32)
    by_pack = pairs_here * pack_count == chips and seq_size == 16 and row_count == PAIR
    row_place = jnp.stack([position // (2 * pairs_here), core]).astype(jnp.int32)
    row_shape = RowShape(chips, row_count, starts)
    self_bounds = (tgt_bounds.reshape(-1), tgt_bounds.reshape(-1))
    cross_bounds = (tgt_bounds.reshape(-1), src_bounds.reshape(-1))
    self_shape = Shape(chips, pairs_here, pack_count, row_count, row_count, starts, True)
    cross_shape = Shape(chips, pairs_here, pack_count, row_count, source_rows, starts, False)
    flat_inputs = inputs.reshape(rows, model_width)
    flat_encoded = encoded.reshape(pack_count * source_rows, model_width)

    all_chips = [[2 * chip + side for chip in range(chips)] for side in range(2)]
    near_chips = [
        [2 * (copy * pairs_here + pair) + side for pair in range(pairs_here)]
        for copy in range(copies)
        for side in range(2)
    ]

    def swap_core(value):
        return lax.ppermute(value, "seq", [(i, i ^ 1) for i in range(seq_size)])

    def to_all(value):
        return lax.all_to_all(value, "seq", 0, 0, axis_index_groups=all_chips, tiled=True)

    def to_near(value):
        if pairs_here == 1:
            return value
        return lax.all_to_all(value, "seq", 0, 0, axis_index_groups=near_chips, tiled=True)

    def exchange(value):
        low = value.astype(BF16)
        if head_size == 2:
            return low, lax.ppermute(low, "head", [(0, 1), (1, 0)])
        return lax.psum(low.astype(F32), "head"), jnp.zeros_like(low)

    def spread(message):
        own = to_all(message)
        return own, swap_core(own)

    def spread_queries(features):
        return spread(jnp.tile(features.reshape(pairs_here, -1, rows), (copies, 1, 1)))

    def pair_rows(keys, values):
        def cut(value):
            return value.reshape(-1, pairs_here, PAIR).transpose(1, 0, 2)

        return jnp.stack([cut(keys), cut(values)], axis=1)

    def join_rows(message):
        return message.transpose(1, 2, 0, 3).reshape(2, -1, local_width)

    def logs_of(message):
        stats = message[:, PAIR : PAIR + 4, :].astype(F32)
        return stats[:, 0::2] + stats[:, 1::2]

    def weighted(parts, logs):
        highest = jnp.max(logs, axis=0)
        weights = jnp.exp(logs - highest)
        denominator = jnp.sum(weights, axis=0)
        shares = weights / denominator
        split = parts.reshape(parts.shape[:-2] + (2, HEAD_DIM, rows)).astype(F32)
        merged = jnp.sum(split * shares[:, :, :, None, :], axis=0)
        return merged, highest + jnp.log(denominator)

    def collect(own_part, other_part):
        met = swap_core(other_part)
        parts = jnp.stack([own_part, met])
        logs = jnp.stack([logs_of(own_part), logs_of(met)])
        merged, total = weighted(parts[:, :, :PAIR], logs)
        high, low = split_parts(total)
        statistics = jnp.stack([high, low], axis=2).reshape(chips, 4, rows)
        statistics = jnp.pad(statistics, ((0, 0), (0, STATS - 4), (0, 0)))
        message = jnp.concatenate(
            [merged.reshape(chips, PAIR, rows).astype(BF16), statistics.astype(BF16)], axis=1
        )
        back = to_all(message)
        logs = logs_of(back).reshape(copies, pairs_here, 2, rows)
        features = back[:, :PAIR].reshape(copies, pairs_here, PAIR, rows)
        merged, total = weighted(features, logs)
        return merged, total

    def spread_grads(grad_features, merged, total):
        split = grad_features.reshape(pairs_here, 2, HEAD_DIM, rows).astype(F32)
        delta = jnp.sum(split * merged, axis=2)
        statistics = jnp.concatenate(
            [
                jnp.stack(split_parts(total), axis=2).reshape(pairs_here, 4, rows),
                jnp.stack(split_parts(delta), axis=2).reshape(pairs_here, 4, rows),
                jnp.zeros((pairs_here, STATS - 8, rows), F32),
            ],
            axis=1,
        ).astype(BF16)
        message = jnp.concatenate([grad_features.reshape(pairs_here, PAIR, rows), statistics], axis=1)
        return spread_queries(message)

    def collect_query_grads(own_part, other_part):
        total = (own_part.astype(F32) + swap_core(other_part).astype(F32)).astype(BF16)
        back = to_all(total).reshape(copies, local_width, rows)
        return jnp.sum(back.astype(F32), axis=0).astype(BF16)

    def scatter(joined):
        return lax.psum_scatter(joined, "seq", scatter_dimension=0, tiled=True)

    def scatter_by_halves(keep, send, done):
        width = keep.shape[2]

        def pass_on(value, bit):
            return lax.ppermute(value, "seq", [(i, i ^ bit) for i in range(seq_size)])

        values = [value.reshape(2, 2, 2, -1, width) for value in (keep, swap_core(send))]
        cuts = [(0, width // 2), (width // 2, width)]
        values = [values, values]
        for bits, axes in (((2, 4), (2, 1)), ((4, 2), (1, 1)), ((8, 8), (0, 0))):
            found = halve(values, [position // bit % 2 for bit in bits], axes, cuts)
            if bits == (8, 8):
                found, done = lax.optimization_barrier((found, done))
            values = [[kept, pass_on(sent, bit)] for (kept, sent), bit in zip(found, bits)]
            cuts = [(0, width // 2)] * 2
        return last_sums(*values, 3), done

    scaling = HEAD_DIM**-0.5
    cross_kv = project_sources(flat_encoded, cross_key, cross_value)
    if by_pack:
        message = project_self(flat_inputs, self_query, self_key, self_value, pack_count)
        met = to_all(message)
        self_q, self_kv = met[:, 0], met[:, 1:]
        self_kv_other = swap_core(self_kv)
        self_heads, self_logs = row_forward(
            row_shape, self_bounds[0], row_place, self_q, self_kv, self_kv_other
        )
        back = to_all(self_heads)
        back, cross_kv = lax.optimization_barrier((back, cross_kv))
        back = back.reshape(pack_count, pairs_here, PAIR, row_count)
        mixed_self = back.transpose(1, 2, 0, 3).reshape(local_width, rows)
    else:
        query_self = (contract(self_query, flat_inputs, 0, 1) * scaling).astype(BF16)
        key_self = matrix_product(flat_inputs, self_key).astype(BF16)
        value_self = matrix_product(flat_inputs, self_value).astype(BF16)
        self_q = spread_queries(query_self)
        self_kv = to_near(pair_rows(key_self, value_self))
        own_part, other_part = attention_forward(self_shape, self_bounds, place, *self_q, self_kv)
        attended_self, log_self = collect(own_part, other_part)
        mixed_self = attended_self.reshape(local_width, rows).astype(BF16)
    parts = exchange(transposed_times(mixed_self, self_out))
    normed_one, query_cross = first_norm(
        flat_inputs, parts, norm1_gain, norm1_bias, cross_query, copies
    )
    cross_kv = to_near(cross_kv)
    query_cross, cross_kv = lax.optimization_barrier((query_cross, cross_kv))
    cross_q = spread(query_cross)
    own_part, other_part = attention_forward(cross_shape, cross_bounds, place, *cross_q, cross_kv)
    back = to_all(merge_cores(own_part, swap_core(other_part)))
    attended_cross, log_cross, mixed_cross, part = finish_rows(back, cross_out, copies)
    parts = exchange(part)
    normed_two, slope, narrow_low, narrow_slope, branch = feed_forward(
        normed_one, parts, norm2_gain, norm2_bias, ffn_in, ffn_out, adapter_down, adapter_up
    )
    part, met = exchange(branch)
    output, grad_third, grad_narrow, third_sums, grad_two_part = feed_backward(
        normed_two, part, met, norm3_gain, norm3_bias, cotangent.reshape(rows, model_width),
        slope, narrow_slope, ffn_in, ffn_out, adapter_down, adapter_up,
    )
    part, met = exchange(grad_two_part)
    grad_second, second_sums, message = second_norm_back(
        grad_third, part, met, normed_two, norm2_gain, norm2_bias, cross_out,
        attended_cross, log_cross, copies,
    )
    early = early_weight_grads(
        grad_second, mixed_cross, grad_third, narrow_low, normed_two, grad_narrow,
        second_sums, third_sums,
    )
    cross_g = spread(message)
    early = scatter(early)
    own_part, other_part, cross_dkv = attention_backward(
        cross_shape, cross_bounds, place, *cross_q, *cross_g, cross_kv
    )
    grad_query_cross = collect_query_grads(own_part, other_part)
    grad_query_cross, early = lax.optimization_barrier((grad_query_cross, early))
    part, met = exchange(contract(grad_query_cross, cross_query, 0, 1))
    adapters_up, adapters_down, norms = spread_adapters(
        lax.all_gather(early[:, local_width:], "seq", axis=0, tiled=True), adapter_up.shape[0]
    )
    source_dkv = to_near(cross_dkv)
    grad_first, first_sums, grad_heads = first_norm_back(
        grad_second, (part, met), normed_one, norm1_gain, norm1_bias, self_out, pack_count
    )
    source_part = source_grads(source_dkv, cross_key, cross_value)
    middle = middle_weight_grads(
        grad_first, mixed_self, normed_one, grad_query_cross, flat_encoded, source_dkv
    )
    if by_pack:
        grad_heads = to_all(grad_heads.reshape(chips, PAIR, row_count))
        grad_heads, middle, source_part = lax.optimization_barrier((grad_heads, middle, source_part))
        source_part, source_met = exchange(source_part)
        dq, own_dkv, other_dkv = row_backward(
            row_shape, self_bounds[0], row_place, self_q, self_heads, self_logs, grad_heads,
            self_kv, self_kv_other,
        )
        dkv = (own_dkv.astype(F32) + swap_core(other_dkv).astype(F32)).astype(BF16)
        high, low = split_parts(first_sums + swap_core(first_sums))
        sums = jnp.concatenate([high, low]).astype(BF16).reshape(1, 1, -1, PAIR)
        sums = jnp.broadcast_to(sums, (chips,) + sums.shape[1:])[:, 0]
        message = jnp.concatenate([dq, dkv[:, 0], dkv[:, 1], sums], axis=1)
        back = to_all(message)
        first_sums = back[:, 3 * row_count :].astype(F32).reshape(chips, 2, 2, model_width)
        first_sums = jnp.sum(first_sums[:, 0] + first_sums[:, 1], axis=0)
        back, source_met = lax.optimization_barrier((back, source_met))
        keep, send = self_weight_grads(flat_inputs, back, pack_count, core)
        back, keep, send = lax.optimization_barrier((back, keep, send))
        self_grads, middle = scatter_by_halves(keep, send, scatter(middle))
        part, met = exchange(input_grads(back, self_query, self_key, self_value, pack_count))
        grad_inputs = grad_first + (part.astype(F32) + met.astype(F32))
    else:
        source_part, source_met = exchange(source_part)
        grad_mixed_self = grad_heads.transpose(1, 2, 0, 3).reshape(local_width, rows)
        self_g = spread_grads(grad_mixed_self, attended_self, log_self)
        own_part, other_part, self_dkv = attention_backward(
            self_shape, self_bounds, place, *self_q, *self_g, self_kv
        )
        grad_query_self = collect_query_grads(own_part, other_part)
        grad_key_self, grad_value_self = join_rows(to_near(self_dkv))
        grad_in_part = (
            transposed_times(grad_query_self, contract_t(self_query))
            + times_transposed(grad_key_self, self_key)
            + times_transposed(grad_value_self, self_value)
        )
        part, met = exchange(grad_in_part)
        grad_inputs = grad_first + (part.astype(F32) + met.astype(F32))
        grad_self_query = contract(flat_inputs, grad_query_self, 0, 1)
        grad_self_key = transposed_times(flat_inputs, grad_key_self)
        grad_self_value = transposed_times(flat_inputs, grad_value_self)
        self_parts = jnp.concatenate(
            [part.astype(BF16) for part in (grad_self_query, grad_self_key, grad_self_value)], axis=1
        )
        self_grads = jnp.split(scatter(self_parts).astype(F32), 3, axis=1)
        middle = scatter(middle)
        first_sums = jnp.sum(lax.all_gather(first_sums, "seq"), axis=0)

    grad_source = source_part.astype(F32) + source_met.astype(F32)
    cross_out_g, self_out_g, cross_query_g, cross_key_g, cross_value_g = spread_middle(
        early[:, :local_width], middle
    )
    self_query_g, self_key_g, self_value_g = self_grads
    return (
        output.reshape(pack_count, row_count, model_width),
        grad_inputs.reshape(pack_count, row_count, model_width),
        grad_source.reshape(pack_count, source_rows, model_width),
        self_query_g,
        self_key_g,
        self_value_g,
        self_out_g,
        cross_query_g,
        cross_key_g,
        cross_value_g,
        cross_out_g,
        adapters_down,
        adapters_up,
        first_sums[0],
        first_sums[1],
        norms[0],
        norms[1],
        norms[2],
        norms[3],
    )


def contract_t(weight):
    return weight.T


def solution(mesh):
    placed = (
        P(None, "seq", None),
        P(None, "seq", None),
        P(),
        P(),
        P(None, "head"),
        P(None, "head"),
        P(None, "head"),
        P("head", None),
        P(None, "head"),
        P(None, "head"),
        P(None, "head"),
        P("head", None),
        P(None, "head"),
        P("head", None),
        P(None, "head"),
        P("head", None),
        P(),
        P(),
        P(),
        P(),
        P(),
        P(),
        P(None, "seq", None),
    )
    return jax.shard_map(
        functools.partial(on_device, mesh.shape["seq"], mesh.shape["head"]),
        mesh=mesh,
        in_specs=placed,
        out_specs=(
            P(None, "seq", None),
            P(None, "seq", None),
            P(None, "seq", None),
            P("seq", "head"),
            P("seq", "head"),
            P("seq", "head"),
            P("head", "seq"),
            P("seq", "head"),
            P("seq", "head"),
            P("seq", "head"),
            P("head", "seq"),
            P(None, "head"),
            P("head", None),
            P(),
            P(),
            P(),
            P(),
            P(),
            P(),
        ),
        check_vma=False,
    )
```
